32 devices in a mesh: shot: 4 (over y, x), slab: 8 (over z, core).
Axes of the slice: x: 2, y: 2, z: 4, core: 2. Of those that a mesh axis runs over, the one named last changes fastest.
Arguments:
- source_field: bfloat16 [4, 2, 1024, 2, 1024], P('shot', None, 'slab'), may hold values from -6 to 6
- residual_data: bfloat16 [4, 2, 1024, 2, 1024], P('shot', None, 'slab'), may hold values from -6 to 6
- receiver_lines: int32 [4, 1024], P('shot'), may hold values 0 or 1
- shot_positions: int32 [4, 2], P('shot'), may hold values from 0 to 1023
- slowness: float32 [2, 1024, 1024], P(None, 'slab'), may hold values from 0.5 to 2
- frequency: float32 [2], replicated, may hold values from 0.5 to 4
- line_inverse: bfloat16 [2, 2, 2, 512, 512], replicated, may hold values from -0.4 to 1.2
- coupling: float32 [2, 2], replicated, may hold values from -0.6 to 0.6
Outputs:
- gradient: float32 [2, 1024, 1024], P(None, 'slab', 'shot')
The draws below stay inside these ranges and needn't reach their ends.
All inputs are finite; a program needn't handle non-finite values. No bound on the sum of `receiver_lines` on one device may be relied on, other than what follows from the above.
Results may differ from the reference program's by a relative error of at most 0.0082.
Values may be sent and summed in bfloat16 or wider, within the bound.
No kernel may reach another device: no remote copies, remote signals or barrier semaphores. Data moves between devices by JAX's collectives and lax.ppermute only.
A program may use at most 64 MiB of HBM per device.

```python
import math
import jax
import jax.numpy as jnp
from jax import lax

NX = 1024
BLOCK = 512
BLOCKS = 2
NF = 2
STEPS = 2
SHOTS = 4


def draw_line_inverse(key, part):
    jitter = jnp.clip(jax.random.normal(key, (NF, 2, BLOCKS, BLOCK, BLOCK), jnp.float32), -6.0, 6.0)
    identity = jnp.eye(BLOCK, dtype=jnp.float32)
    centre = jnp.stack([0.8 * identity, 0.0 * identity])[None, :, None]
    return (centre + 0.35 / math.sqrt(BLOCK) * jitter).astype(jnp.bfloat16)


def set_ends(values, stream_key, low, largest):
    index_at = [jax.random.randint(jax.random.fold_in(stream_key, axis), (), 0, length) for axis, length in enumerate(values.shape)]
    main_axis = values.shape.index(max(values.shape))
    neighbour = index_at[:main_axis] + [(index_at[main_axis] + 1) % values.shape[main_axis]] + index_at[main_axis + 1:]
    return values.at[tuple(index_at)].set(low).at[tuple(neighbour)].set(largest)


def block_scale(key, extent, shards, least, high):
    def one(axis_at, parts):
        steps = jax.random.uniform(jax.random.fold_in(jax.random.fold_in(key, 6), axis_at), (parts,), jnp.float32, least / len(shards), high / len(shards))
        return jnp.repeat(jnp.exp(steps), extent[axis_at] // parts).reshape((-1,) + (1,) * (len(extent) - axis_at - 1))

    factor_of = one(*shards[0])
    for cut in shards[1:]:
        factor_of = factor_of * one(*cut)
    return factor_of


def bell_draw(key, shape, deviation, reach, cuts=(), kind=jnp.bfloat16):
    entries = deviation * jax.random.normal(key, shape, jnp.float32)
    if cuts:
        entries = entries * block_scale(key, shape, cuts, -0.22, 0.18)
    return jnp.clip(entries, -reach, reach).astype(kind)


def setup_inputs(seed: int = 0) -> dict:
    key_of = jax.random.split(jax.random.key(seed), 9)
    source_field = bell_draw(key_of[0], (SHOTS, NF, NX, 2, NX), 1.0, 6.0, ((0, 4), (2, 8)))
    residual_data = bell_draw(key_of[1], (SHOTS, NF, NX, 2, NX), 1.0, 6.0, ((0, 4), (2, 8)))
    receiver_lines = set_ends((jax.random.randint(key_of[2], (SHOTS, NX), 0, 4) < 3).astype(jnp.int32), jax.random.fold_in(key_of[2], 1), 0, 1)
    shot_positions = set_ends(jax.random.randint(key_of[3], (SHOTS, 2), 0, NX), jax.random.fold_in(key_of[3], 1), 0, NX - 1).astype(jnp.int32)
    slowness = jnp.clip(jnp.exp(math.log(2.0) - 1.3862944 * jax.random.uniform(key_of[4], (STEPS, NX, NX), jnp.float32) ** block_scale(key_of[4], (STEPS, NX, NX), ((1, 8),), -0.2, 0.2)), 0.5, 2.0)
    frequency = jnp.clip(jnp.exp(jax.random.uniform(key_of[5], (NF,), jnp.float32, math.log(0.5), math.log(4.0))), 0.5, 4.0)
    line_inverse = draw_line_inverse(jax.random.fold_in(key_of[8], 71), 0)
    coupling = jnp.clip(jax.random.uniform(key_of[7], (NF, 2), jnp.float32, -0.6, 0.6), -0.6, 0.6)
    return {"source_field": source_field, "residual_data": residual_data, "receiver_lines": receiver_lines, "shot_positions": shot_positions, "slowness": slowness, "frequency": frequency, "line_inverse": line_inverse, "coupling": coupling}


def pick_index(values, position, axis_number, keep=False):
    return lax.index_in_dim(values, position, axis_number, keepdims=keep)


def line_solve(wavefield, line_inverse, coupling, line_dim):
    in_shape = wavefield.shape
    freq_count = line_inverse.shape[0]
    blocks = line_inverse.shape[2]
    block_len = line_inverse.shape[3]
    real_blocks = line_inverse[:, 0].astype(jnp.float32)
    imag_blocks = line_inverse[:, 1].astype(jnp.float32)
    if line_dim == 5:
        pieces = wavefield.reshape(in_shape[:5] + (blocks, block_len)).astype(jnp.float32)
        formula = "shfxcgj,fgij->shfxcgi"
    else:
        pieces = wavefield.reshape(in_shape[:3] + (blocks, block_len, in_shape[4] * in_shape[5])).astype(jnp.float32)
        formula = "shfgjz,fgij->shfgiz"
    with_real = jnp.einsum(formula, pieces, real_blocks, precision=lax.Precision.HIGHEST)
    with_imag = jnp.einsum(formula, pieces, imag_blocks, precision=lax.Precision.HIGHEST)
    if line_dim == 5:
        comp_axis, block_axis, cell_axis = 4, 4, 4
        col_shape = (1, 1, freq_count, 1, block_len)
    else:
        with_real = with_real.reshape(in_shape[:3] + (blocks, block_len, in_shape[4], in_shape[5]))
        with_imag = with_imag.reshape(in_shape[:3] + (blocks, block_len, in_shape[4], in_shape[5]))
        comp_axis, block_axis, cell_axis = 5, 3, 3
        col_shape = (1, 1, freq_count, block_len, 1)
    signs_six = jnp.array([1.0, -1.0], jnp.float32).reshape(1, 2, 1, 1, 1, 1)
    signs_five = jnp.array([1.0, -1.0], jnp.float32).reshape(1, 2, 1, 1, 1)
    u_real = pick_index(with_real, 0, comp_axis) - signs_six * pick_index(with_imag, 1, comp_axis)
    u_imag = pick_index(with_real, 1, comp_axis) + signs_six * pick_index(with_imag, 0, comp_axis)
    coup_real = coupling[:, 0].reshape(1, 1, freq_count, 1, 1)
    coup_imag = coupling[:, 1].reshape(1, 1, freq_count, 1, 1)

    def factor(block_index, column):
        col_real = line_inverse[:, 0, block_index, :, column].astype(jnp.float32).reshape(col_shape)
        col_imag = line_inverse[:, 1, block_index, :, column].astype(jnp.float32).reshape(col_shape)
        return coup_real * col_real - coup_imag * col_imag, signs_five * (coup_imag * col_real + coup_real * col_imag)

    fwd_real = [pick_index(u_real, 0, block_axis)]
    fwd_imag = [pick_index(u_imag, 0, block_axis)]
    for block_index in range(1, blocks):
        mult_real, mult_imag = factor(block_index, 0)
        prev_real = pick_index(fwd_real[-1], block_len - 1, cell_axis, True)
        prev_imag = pick_index(fwd_imag[-1], block_len - 1, cell_axis, True)
        fwd_real.append(pick_index(u_real, block_index, block_axis) + mult_real * prev_real - mult_imag * prev_imag)
        fwd_imag.append(pick_index(u_imag, block_index, block_axis) + mult_real * prev_imag + mult_imag * prev_real)
    out_real = list(fwd_real)
    out_imag = list(fwd_imag)
    for block_index in range(blocks - 2, -1, -1):
        mult_real, mult_imag = factor(block_index, block_len - 1)
        next_real = pick_index(out_real[block_index + 1], 0, cell_axis, True)
        next_imag = pick_index(out_imag[block_index + 1], 0, cell_axis, True)
        out_real[block_index] = fwd_real[block_index] + mult_real * next_real - mult_imag * next_imag
        out_imag[block_index] = fwd_imag[block_index] + mult_real * next_imag + mult_imag * next_real
    real_line = jnp.stack(out_real, axis=block_axis)
    imag_line = jnp.stack(out_imag, axis=block_axis)
    real_line = real_line.reshape(in_shape[:4] + (in_shape[5],))
    imag_line = imag_line.reshape(in_shape[:4] + (in_shape[5],))
    return jnp.stack([real_line, imag_line], axis=4).astype(jnp.bfloat16)


def phase_shift(wavefield, slow_field, frequency):
    angles = frequency[:, None, None] * slow_field[None]
    cosine = jnp.cos(angles)[None, None]
    sine_part = jnp.sin(angles)[None, None]
    signs_five = jnp.array([1.0, -1.0], jnp.float32).reshape(1, 2, 1, 1, 1)
    real_part = wavefield[:, :, :, :, 0].astype(jnp.float32)
    imag_part = wavefield[:, :, :, :, 1].astype(jnp.float32)
    new_real = real_part * cosine - signs_five * imag_part * sine_part
    new_imag = imag_part * cosine + signs_five * real_part * sine_part
    return jnp.stack([new_real, new_imag], axis=4).astype(jnp.bfloat16)


def image_term(wavefield, row_cells, col_cells, shot_positions, frequency):
    source = wavefield[:, 0].astype(jnp.float32)
    receiver = wavefield[:, 1].astype(jnp.float32)
    cross = source[:, :, :, 0] * receiver[:, :, :, 1] - source[:, :, :, 1] * receiver[:, :, :, 0]
    weighted = jnp.sum(cross * frequency[None, :, None, None], axis=1)
    row_gap = row_cells[None, :, None] - shot_positions[:, 0][:, None, None]
    col_gap = col_cells[None, None, :] - shot_positions[:, 1][:, None, None]
    spread = (row_gap * row_gap + col_gap * col_gap).astype(jnp.float32)
    taper = 1.0 / (1.0 + spread * (16.0 / (NX * NX)))
    return jnp.sum(weighted * taper, axis=0)


def reference(source_field, residual_data, receiver_lines, shot_positions, slowness, frequency, line_inverse, coupling):
    line_len = source_field.shape[4]
    cells = jnp.arange(line_len, dtype=jnp.int32)

    def one_shot(running, inputs):
        source, residual, line_mask, position = inputs
        receiver = residual * line_mask.astype(jnp.bfloat16)[None, None, None, :]
        wavefield = jnp.stack([source, receiver], axis=0)[None]
        layers = []
        for depth_index in range(STEPS):
            shifted = phase_shift(wavefield, slowness[depth_index], frequency)
            if depth_index % 2 == 0:
                wavefield = line_solve(line_solve(shifted, line_inverse, coupling, 5), line_inverse, coupling, 3)
            else:
                wavefield = line_solve(line_solve(shifted, line_inverse, coupling, 3), line_inverse, coupling, 5)
            layers.append(image_term(wavefield, cells, cells, position[None], frequency))
        return running + jnp.stack(layers), None

    start = jnp.zeros((STEPS, line_len, line_len), jnp.float32)
    running, _unused = lax.scan(one_shot, start, (source_field, residual_data, receiver_lines, shot_positions))
    return running
```

```python
from functools import partial

import jax
import jax.numpy as jnp
from jax import lax
from jax.experimental import pallas as pl
from jax.experimental.pallas import tpu as pltpu
from jax.sharding import PartitionSpec as P

NX = 1024
STEPS = 2


def pick_index(values, position, axis_number, keep=False):
    return lax.index_in_dim(values, position, axis_number, keepdims=keep)


def line_solve(wavefield, line_inverse, coupling, line_dim):
    in_shape = wavefield.shape
    freq_count = line_inverse.shape[0]
    blocks = line_inverse.shape[2]
    block_len = line_inverse.shape[3]
    real_blocks = line_inverse[:, 0]
    imag_blocks = line_inverse[:, 1]
    if line_dim == 5:
        pieces = wavefield.reshape(in_shape[:5] + (blocks, block_len))
        formula = "shfxcgj,fgij->shfxcgi"
    else:
        pieces = wavefield.reshape(in_shape[:3] + (blocks, block_len, in_shape[4] * in_shape[5]))
        formula = "shfgjz,fgij->shfgiz"
    with_real = jnp.einsum(formula, pieces, real_blocks, preferred_element_type=jnp.float32)
    with_imag = jnp.einsum(formula, pieces, imag_blocks, preferred_element_type=jnp.float32)
    if line_dim == 5:
        comp_axis, block_axis, cell_axis = (4, 4, 4)
        col_shape = (1, 1, freq_count, 1, block_len)
    else:
        with_real = with_real.reshape(in_shape[:3] + (blocks, block_len, in_shape[4], in_shape[5]))
        with_imag = with_imag.reshape(in_shape[:3] + (blocks, block_len, in_shape[4], in_shape[5]))
        comp_axis, block_axis, cell_axis = (5, 3, 3)
        col_shape = (1, 1, freq_count, block_len, 1)
    signs_six = jnp.array([1.0, -1.0], jnp.float32).reshape(1, 2, 1, 1, 1, 1)
    signs_five = jnp.array([1.0, -1.0], jnp.float32).reshape(1, 2, 1, 1, 1)
    u_real = pick_index(with_real, 0, comp_axis) - signs_six * pick_index(with_imag, 1, comp_axis)
    u_imag = pick_index(with_real, 1, comp_axis) + signs_six * pick_index(with_imag, 0, comp_axis)
    coup_real = coupling[:, 0].reshape(1, 1, freq_count, 1, 1)
    coup_imag = coupling[:, 1].reshape(1, 1, freq_count, 1, 1)

    def factor(block_index, column):
        col_real = line_inverse[:, 0, block_index, :, column].astype(jnp.float32).reshape(col_shape)
        col_imag = line_inverse[:, 1, block_index, :, column].astype(jnp.float32).reshape(col_shape)
        return (
            coup_real * col_real - coup_imag * col_imag,
            signs_five * (coup_imag * col_real + coup_real * col_imag),
        )

    fwd_real = [pick_index(u_real, 0, block_axis)]
    fwd_imag = [pick_index(u_imag, 0, block_axis)]
    block_index = 1
    mult_real, mult_imag = factor(block_index, 0)
    prev_real = pick_index(fwd_real[-1], block_len - 1, cell_axis, True)
    prev_imag = pick_index(fwd_imag[-1], block_len - 1, cell_axis, True)
    fwd_real.append(
        pick_index(u_real, block_index, block_axis) + mult_real * prev_real - mult_imag * prev_imag
    )
    fwd_imag.append(
        pick_index(u_imag, block_index, block_axis) + mult_real * prev_imag + mult_imag * prev_real
    )
    out_real = list(fwd_real)
    out_imag = list(fwd_imag)
    block_index = 0
    mult_real, mult_imag = factor(block_index, block_len - 1)
    next_real = pick_index(out_real[block_index + 1], 0, cell_axis, True)
    next_imag = pick_index(out_imag[block_index + 1], 0, cell_axis, True)
    out_real[block_index] = fwd_real[block_index] + mult_real * next_real - mult_imag * next_imag
    out_imag[block_index] = fwd_imag[block_index] + mult_real * next_imag + mult_imag * next_real
    real_line = jnp.stack(out_real, axis=block_axis).reshape(in_shape[:4] + (in_shape[5],))
    imag_line = jnp.stack(out_imag, axis=block_axis).reshape(in_shape[:4] + (in_shape[5],))
    return jnp.stack([real_line, imag_line], axis=4).astype(jnp.bfloat16)


def phase_shift(wavefield, slow_field, frequency):
    angles = frequency[:, None, None] * slow_field[None]
    cosine = jnp.cos(angles)[None, None]
    sine_part = jnp.sin(angles)[None, None]
    signs_five = jnp.array([1.0, -1.0], jnp.float32).reshape(1, 2, 1, 1, 1)
    real_part = wavefield[:, :, :, :, 0].astype(jnp.float32)
    imag_part = wavefield[:, :, :, :, 1].astype(jnp.float32)
    new_real = real_part * cosine - signs_five * imag_part * sine_part
    new_imag = imag_part * cosine + signs_five * real_part * sine_part
    return jnp.stack([new_real, new_imag], axis=4).astype(jnp.bfloat16)


def image_term(wavefield, row_cells, col_cells, shot_positions, frequency):
    source = wavefield[:, 0].astype(jnp.float32)
    receiver = wavefield[:, 1].astype(jnp.float32)
    cross = source[:, :, :, 0] * receiver[:, :, :, 1] - source[:, :, :, 1] * receiver[:, :, :, 0]
    weighted = jnp.sum(cross * frequency[None, :, None, None], axis=1)
    row_gap = row_cells[None, :, None] - shot_positions[:, 0][:, None, None]
    col_gap = col_cells[None, None, :] - shot_positions[:, 1][:, None, None]
    spread = (row_gap * row_gap + col_gap * col_gap).astype(jnp.float32)
    taper = 1.0 / (1.0 + spread * (16.0 / (NX * NX)))
    return jnp.sum(weighted * taper, axis=0)


def general_shards(
    source_field,
    residual_data,
    receiver_lines,
    shot_positions,
    slowness,
    frequency,
    line_inverse,
    coupling,
):
    row_count = source_field.shape[2]
    line_len = source_field.shape[4]
    receiver = residual_data * receiver_lines.astype(jnp.bfloat16)[:, None, None, None, :]
    wavefield = jnp.stack([source_field, receiver], axis=1)
    slab_start = lax.axis_index("slab") * row_count
    own_cells = slab_start + jnp.arange(row_count, dtype=jnp.int32)
    all_cells = jnp.arange(line_len, dtype=jnp.int32)
    solve_first = partial(line_solve, line_inverse=line_inverse, coupling=coupling, line_dim=3)
    solve_second = partial(line_solve, line_inverse=line_inverse, coupling=coupling, line_dim=5)

    def forward(fields):
        return solve_first(lax.all_to_all(fields, "slab", split_axis=5, concat_axis=3, tiled=True))

    def backward(fields):
        return lax.all_to_all(fields, "slab", split_axis=3, concat_axis=5, tiled=True)

    images = []
    for depth_index in range(STEPS):
        shifted = phase_shift(wavefield, slowness[depth_index], frequency)
        if depth_index % 2 == 0:
            wavefield = backward(forward(solve_second(shifted)))
        else:
            wavefield = solve_second(backward(forward(shifted)))
        local_image = image_term(wavefield, own_cells, all_cells, shot_positions, frequency)
        images.append(lax.psum_scatter(local_image, "shot", scatter_dimension=1, tiled=True))
    return jnp.stack(images)


F32 = jnp.float32
BF16 = jnp.bfloat16
SMEM = pltpu.SMEM
VMEM = pltpu.VMEM
MIDDLE = 1.25


def params(mib):
    return pltpu.CompilerParams(vmem_limit_bytes=mib << 20)


def sincos(angle):
    turns = jnp.floor(angle * 0.6366197723675814 + 0.5)
    quarter = turns.astype(jnp.int32)
    rest = (angle - turns * 1.5703125) - turns * 4.838267948966e-4
    square = rest * rest
    sine = rest + rest * square * (
        -1.6666667e-1 + square * (8.3333333e-3 + square * (-1.9841270e-4 + square * 2.7557319e-6))
    )
    cosine = 1.0 + square * (
        -0.5 + square * (4.1666667e-2 + square * (-1.3888889e-3 + square * 2.4801587e-5))
    )
    odd = (quarter & 1) == 1
    sine_out = jnp.where(odd, cosine, sine)
    cosine_out = jnp.where(odd, sine, cosine)
    sine_out = jnp.where((quarter & 2) == 2, -sine_out, sine_out)
    cosine_out = jnp.where(((quarter + 1) & 2) == 2, -cosine_out, cosine_out)
    return sine_out, cosine_out


def dot_t(left, right):
    return lax.dot_general(left, right, (((1,), (1,)), ((), ())), preferred_element_type=F32)


def dot(left, right):
    return lax.dot_general(left, right, (((1,), (0,)), ((), ())), preferred_element_type=F32)


def dot_rows(left, right):
    return lax.dot_general(left, right, (((0,), (0,)), ((), ())), preferred_element_type=F32)


def slab_kernel(
    conjugate, other, meta, freq, field, slow, inverse, ends, mask, edge_row, same, cross, partial_edge
):
    rows = slow.shape[1]
    half = inverse.shape[3]
    zz = meta[1]
    f = meta[0] ^ other
    sine, cosine = sincos(freq[f] * slow[0])
    real = field[0, 0, :, 0, :].astype(F32)
    imag = field[0, 0, :, 1, :].astype(F32)
    if conjugate:
        real = real * mask[...]
        imag = -(imag * mask[...])
    new_real = (real * cosine - imag * sine).astype(BF16)
    new_imag = (imag * cosine + real * sine).astype(BF16)
    solved = []
    for k in range(2):
        left = jnp.concatenate(
            [new_real[:, k * half : (k + 1) * half], new_imag[:, k * half : (k + 1) * half]], axis=0
        )
        by_real = dot_t(left, inverse[0, 0, k])
        by_imag = dot_t(left, inverse[0, 1, k])
        solved.append((by_real[:rows] - by_imag[rows:], by_real[rows:] + by_imag[:rows]))

    def couple(k, edge):
        value, column = solved[k], ends[0, k]
        qr, qi = column[0:1], column[1:2]
        er, ei = edge
        return value[0] + er * qr - ei * qi, value[1] + er * qi + ei * qr

    last = (solved[0][0][:, half - 1 :], solved[0][1][:, half - 1 :])
    upper = couple(1, last)
    lower = couple(0, (upper[0][:, 0:1], upper[1][:, 0:1]))
    lower = [v.astype(BF16) for v in lower]
    upper = [v.astype(BF16) for v in upper]
    first = zz == 0
    pieces = []
    for part in range(2):
        mine = jnp.where(first, lower[part], upper[part])
        away = jnp.where(first, upper[part], lower[part])
        same[part * rows : (part + 1) * rows] = mine
        cross[part * rows : (part + 1) * rows] = away
        pieces.append(jnp.concatenate([mine, away], axis=1))
    row = edge_row[0]
    with_real = dot(row, pieces[0])
    with_imag = dot(row, pieces[1])
    edge_real = with_real[0:1] - with_imag[1:2]
    edge_imag = with_imag[0:1] + with_real[1:2]
    partial_edge[0:1] = edge_real[:, :half]
    partial_edge[1:2] = edge_imag[:, :half]
    partial_edge[2:3] = edge_real[:, half:]
    partial_edge[3:4] = edge_imag[:, half:]


def slab_step(conjugate, other, meta, freq, field, slowness, inverse, ends, mask, edge_row):
    rows, length = slowness.shape[1:]
    half = length // 2

    def at_f(*rest):
        return lambda i, m: (m[0] ^ other,) + rest

    return pl.pallas_call(
        partial(slab_kernel, conjugate, other),
        grid_spec=pltpu.PrefetchScalarGridSpec(
            num_scalar_prefetch=1,
            grid=(1,),
            in_specs=[
                pl.BlockSpec(memory_space=SMEM),
                pl.BlockSpec((1, 1, rows, 2, length), lambda i, m: (0, m[0] ^ other, 0, 0, 0)),
                pl.BlockSpec((1, rows, length), lambda i, m: (0, 0, 0)),
                pl.BlockSpec((1, 2, 2, half, half), at_f(0, 0, 0, 0)),
                pl.BlockSpec((1, 2, 2, half), at_f(0, 0, 0)),
                pl.BlockSpec((1, length), lambda i, m: (0, 0)),
                pl.BlockSpec((1, 16, rows), at_f(0, 0)),
            ],
            out_specs=[
                pl.BlockSpec((2 * rows, half), lambda i, m: (0, 0)),
                pl.BlockSpec((2 * rows, half), lambda i, m: (0, 0)),
                pl.BlockSpec((4, half), lambda i, m: (0, 0)),
            ],
        ),
        out_shape=[
            jax.ShapeDtypeStruct((2 * rows, half), BF16),
            jax.ShapeDtypeStruct((2 * rows, half), BF16),
            jax.ShapeDtypeStruct((4, half), F32),
        ],
        compiler_params=params(32),
        name="slab_step",
    )(meta, freq, field, slowness, inverse, ends, mask, edge_row)


def phase_kernel(meta, values, place, own, core, far, far_core, sine, cosine, weight):
    rows, half = own.shape
    for k, piece in enumerate((own, core, far, far_core)):
        start = pl.multiple_of((meta[3] ^ k) * rows, rows)
        s, c = sincos(values[0] * (piece[...].astype(F32) + MIDDLE))
        sine[pl.ds(start, rows)] = s
        cosine[pl.ds(start, rows)] = c
    row = lax.broadcasted_iota(jnp.int32, (weight.shape[0], half), 0) + meta[2] * half - place[0, 0]
    col = lax.broadcasted_iota(jnp.int32, (weight.shape[0], half), 1) + meta[1] * half - place[0, 1]
    spread = (row * row + col * col).astype(F32)
    weight[...] = -values[0] / (1.0 + spread * (16.0 / (NX * NX)))


def column_kernel(
    meta, values, own, core, far, far_core, inverse, edge_row, edges, sine, cosine, solved, shifted, own_edge, real, imag
):
    rows = own.shape[0] // 2
    half = own.shape[1]
    for k, piece in enumerate((own, core, far, far_core)):
        start = pl.multiple_of((meta[3] ^ k) * rows, rows)
        real[pl.ds(start, rows)] = piece[:rows]
        imag[pl.ds(start, rows)] = piece[rows:]
    cr, ci, ar, ai = values[1], values[2], values[3], values[4]
    row = edge_row[...]
    with_real = dot(row, real[...])
    with_imag = dot(row, imag[...])
    own_real = with_real[0:1] - with_imag[1:2]
    own_imag = with_imag[0:1] + with_real[1:2]
    hr = edges[0:1] + ar * own_real - ai * own_imag
    hi = edges[1:2] + ar * own_imag + ai * own_real
    add_real = cr * hr - ci * hi
    add_imag = cr * hi + ci * hr
    upper = meta[2] == 1
    low = lax.broadcasted_iota(jnp.int32, (16, half), 0) == 0
    high = lax.broadcasted_iota(jnp.int32, (16, half), 0) == 15
    for ref, add in ((real, add_real), (imag, add_imag)):
        ref[0:16] = (ref[0:16].astype(F32) + jnp.where(low & upper, add, 0.0)).astype(BF16)
        ref[half - 16 :] = (
            ref[half - 16 :].astype(F32) + jnp.where(high & jnp.logical_not(upper), add, 0.0)
        ).astype(BF16)
    left = inverse[0, :, 0].reshape(2 * half, half)
    for n in range(0, half, 256):
        cols = slice(n, n + 256)
        by_real = dot(left, real[:, cols])
        by_imag = dot(left, imag[:, cols])
        xr = (by_real[:half] - by_imag[half:]).astype(BF16)
        xi = (by_imag[:half] + by_real[half:]).astype(BF16)
        solved[:half, cols] = xr
        solved[half:, cols] = xi
        xr, xi = xr.astype(F32), xi.astype(F32)
        s, c = sine[:, cols], cosine[:, cols]
        shifted[:half, cols] = (xr * c - xi * s).astype(BF16)
        shifted[half:, cols] = (xi * c + xr * s).astype(BF16)
    with_real = dot(row, shifted[:half])
    with_imag = dot(row, shifted[half:])
    own_edge[0:1] = with_real[0:1] - with_imag[1:2]
    own_edge[1:2] = with_imag[0:1] + with_real[1:2]


def both_kernel(meta, shifted, inverse_x, inverse_y, edge_row_y, solved, edge):
    half = shifted.shape[1]
    left = inverse_x[0, :, 0].reshape(2 * half, half)
    by_real = dot(left, shifted[:half])
    by_imag = dot(left, shifted[half:])
    u = jnp.concatenate(
        [(by_real[:half] - by_imag[half:]).astype(BF16), (by_imag[:half] + by_real[half:]).astype(BF16)], axis=0
    )
    row = dot_t(edge_row_y[...], u)
    edge[0:1] = row[0:1, :half] - row[1:2, half:]
    edge[1:2] = row[0:1, half:] + row[1:2, :half]
    by_real = dot_t(u, inverse_y[0, 0, 0])
    by_imag = dot_t(u, inverse_y[0, 1, 0])
    solved[:half] = (by_real[:half] - by_imag[half:]).astype(BF16)
    solved[half:] = (by_real[half:] + by_imag[:half]).astype(BF16)


def image_pieces(meta, image, keep, send):
    rows, cols = keep.shape[1:]
    for kz in range(2):
        for kx in range(2):
            col = pl.multiple_of((meta[5] ^ kx) * cols, cols)
            for other, ref in ((0, keep), (1, send)):
                row = pl.multiple_of(((meta[4] ^ kz) * 2 + (meta[0] ^ other)) * rows, rows)
                ref[kz * 2 + kx] = image[pl.ds(row, rows), pl.ds(col, cols)].astype(BF16)


def first_image_kernel(meta, source, receiver, weight, keep, send, image):
    half = source.shape[1]
    sr, si = source[:half].astype(F32), source[half:].astype(F32)
    rr, ri = receiver[:half].astype(F32), receiver[half:].astype(F32)
    image[...] = (sr * ri + si * rr) * weight[...]
    image_pieces(meta, image, keep, send)


def turn_kernel(values, edge_x, near_x, row_y, edge_y, column_x, whole, edge):
    ar, ai = values[3], values[4]
    for n in range(2):
        r, i = slice(2 * n, 2 * n + 1), slice(2 * n + 1, 2 * n + 2)
        hr = near_x[r] + ar * edge_x[r] - ai * edge_x[i]
        hi = near_x[i] + ar * edge_x[i] + ai * edge_x[r]
        whole[r] = hr
        whole[i] = hi
        yr, yi = row_y[0:1], row_y[1:2]
        sr = jnp.sum(hr * yr - hi * yi, axis=1, keepdims=True)
        si = jnp.sum(hr * yi + hi * yr, axis=1, keepdims=True)
        pr, pi = column_x[0:1], column_x[1:2]
        edge[r] = edge_y[r] + sr * pr - si * pi
        edge[i] = edge_y[i] + sr * pi + si * pr


def split(value):
    high = value.astype(BF16)
    return high.astype(F32), (value - high.astype(F32))


def row_kernel(whole, inverse_y, out):
    high, low = split(whole[...])
    left = jnp.concatenate([high, low, high, low], axis=0).astype(BF16)
    by_real = dot_t(left, inverse_y[0, 0, 0])
    by_imag = dot_t(left, inverse_y[0, 1, 0])
    by_real = by_real[0:4] + by_real[4:8]
    by_imag = by_imag[0:4] + by_imag[4:8]
    for n in range(2):
        r, i = slice(2 * n, 2 * n + 1), slice(2 * n + 1, 2 * n + 2)
        out[r] = by_real[r] - by_imag[i]
        out[i] = by_real[i] + by_imag[r]


def second_image_kernel(
    meta, values, source, receiver, weight, rows_y, edge, near, column_x, column_y, keep, send, image
):
    half = source.shape[1]
    ar, ai = values[5], values[6]

    def triple(value, order):
        high, low = split(value)
        return [high, high, low] if order == 0 else [high, low, high]

    fields = []
    for n, ref in enumerate((source, receiver)):
        r, i = slice(2 * n, 2 * n + 1), slice(2 * n + 1, 2 * n + 2)
        gr = near[r] + ar * edge[r] - ai * edge[i]
        gi = near[i] + ar * edge[i] + ai * edge[r]
        pr, pi = column_x[0:1], column_x[1:2]
        tr, ti = rows_y[r], rows_y[i]
        qr, qi = column_y[0:1], column_y[1:2]
        left, right_real, right_imag = [], [], []
        for a, b, c in ((pr, tr, ti), (pi, -ti, tr), (gr, qr, qi), (gi, -qi, qr)):
            left += triple(a, 0)
            right_real += triple(b, 1)
            right_imag += triple(c, 1)
        pad = [jnp.zeros((4, half), F32)]
        left = jnp.concatenate(left + pad, axis=0).astype(BF16)
        right_real = jnp.concatenate(right_real + pad, axis=0).astype(BF16)
        right_imag = jnp.concatenate(right_imag + pad, axis=0).astype(BF16)
        fields.append(
            (
                ref[:half].astype(F32) + dot_rows(left, right_real),
                ref[half:].astype(F32) + dot_rows(left, right_imag),
            )
        )
    (sr, si), (rr, ri) = fields
    image[...] = (sr * ri + si * rr) * weight[...]
    image_pieces(meta, image, keep, send)


def block_shards(
    source_field, residual_data, receiver_lines, shot_positions, slowness, frequency, line_inverse, coupling
):
    rows, length = slowness.shape[1:]
    half = line_inverse.shape[-1]
    slab = lax.axis_index("slab")
    shot = lax.axis_index("shot")
    c, zz, xb, local = slab % 2, (slab // 2) % 2, slab // 4, slab % 4
    y, x = shot // 2, shot % 2
    meta = jnp.stack([c, zz, xb, local, y, x]).astype(jnp.int32)

    end_columns = jnp.stack([line_inverse[:, :, 0, :, half - 1], line_inverse[:, :, 1, :, 0]], axis=1).astype(F32)
    cr = coupling[:, 0][:, None, None]
    ci = coupling[:, 1][:, None, None]
    ends = jnp.stack(
        [
            cr * end_columns[:, :, 0] - ci * end_columns[:, :, 1],
            cr * end_columns[:, :, 1] + ci * end_columns[:, :, 0],
        ],
        axis=2,
    )
    edge_rows = jnp.stack([line_inverse[:, :, 0, half - 1], line_inverse[:, :, 1, 0]], axis=1)
    rows_x = jnp.where(xb == 0, edge_rows[:, 0], edge_rows[:, 1])
    slab_rows = jnp.pad(lax.dynamic_slice_in_dim(rows_x, local * rows, rows, 2), ((0, 0), (0, 14), (0, 0)))

    def mine(values):
        return jnp.where(c == 0, values[0], values[1])

    row_x = jnp.pad(mine(rows_x), ((0, 14), (0, 0)))
    row_y = mine(jnp.where(zz == 0, edge_rows[:, 0], edge_rows[:, 1]))
    row_y_wide = jnp.pad(row_y, ((0, 14), (0, 0)))
    row_y = row_y.astype(F32)
    ends_own = mine(ends)
    column_x = jnp.where(xb == 0, ends_own[0], ends_own[1])
    column_y = jnp.where(zz == 0, ends_own[0], ends_own[1])
    turn = ends_own[1, :, 0]
    coup = mine(coupling)
    values = jnp.concatenate(
        [mine(frequency)[None], coup, jnp.where(xb == 0, turn, 0.0), jnp.where(zz == 0, turn, 0.0)]
    )
    mask = receiver_lines.astype(F32)

    def move(array, k):
        return lax.ppermute(array, "slab", [(i, i ^ k) for i in range(8)])

    pieces, edges = [], []
    for n, field in enumerate((source_field, residual_data)):
        at = [None] * 4
        parts = [None] * 4
        for other in (0, 1):
            same, cross, edge = slab_step(
                n == 1, other, meta, frequency, field, slowness, line_inverse, ends, mask, slab_rows
            )
            at[2 + other] = move(cross, 2 + other)
            at[other] = move(same, 1) if other else same
            parts[other] = edge[:2]
            parts[2 + other] = edge[2:]
        pieces.append(at)
        edges.append(parts)
    layer = (slowness[1] - MIDDLE).astype(jnp.float16)
    low, high = layer[:, :half], layer[:, half:]
    own_slow = jnp.where(zz == 0, low, high)
    far_slow = move(jnp.where(zz == 0, high, low), 2)
    core_slow = move(jnp.stack([own_slow, far_slow]), 1)

    near0 = 0.0
    for k in range(4):
        near0 = near0 + move(jnp.stack([edges[0][k], edges[1][k]]), 4 + k)

    block = jax.ShapeDtypeStruct((half, half), F32)
    pair = jax.ShapeDtypeStruct((2 * half, half), BF16)
    smem = pl.BlockSpec(memory_space=SMEM)
    vmem = pl.BlockSpec(memory_space=VMEM)
    sine, cosine, weight = pl.pallas_call(
        phase_kernel,
        in_specs=[smem] * 3 + [vmem] * 4,
        out_specs=[vmem] * 3,
        out_shape=[block] * 3,
        compiler_params=params(24),
        name="phase",
    )(
        meta,
        values,
        shot_positions,
        own_slow.astype(F32),
        core_slow[0].astype(F32),
        far_slow.astype(F32),
        core_slow[1].astype(F32),
    )

    def own_block(axis):
        return pl.BlockSpec((1, 2, 1, half, half), lambda i, m: (m[0], 0, m[axis], 0, 0))

    def whole(*shape):
        return pl.BlockSpec(shape, lambda i, m: (0,) * len(shape))

    def column_step(at, near):
        return pl.pallas_call(
            column_kernel,
            grid_spec=pltpu.PrefetchScalarGridSpec(
                num_scalar_prefetch=1,
                grid=(1,),
                in_specs=[smem]
                + [whole(2 * rows, half)] * 4
                + [own_block(2), whole(16, half), whole(2, half), whole(half, half), whole(half, half)],
                out_specs=[whole(2 * half, half), whole(2 * half, half), whole(2, half)],
                scratch_shapes=[VMEM((half, half), BF16)] * 2,
            ),
            out_shape=[pair, pair, jax.ShapeDtypeStruct((2, half), F32)],
            compiler_params=params(40),
            name="column",
        )(meta, values, *at, line_inverse, row_x, near, sine, cosine)

    def both_step(shifted):
        return pl.pallas_call(
            both_kernel,
            grid_spec=pltpu.PrefetchScalarGridSpec(
                num_scalar_prefetch=1,
                grid=(1,),
                in_specs=[whole(2 * half, half), own_block(2), own_block(1), whole(16, half)],
                out_specs=[whole(2 * half, half), whole(2, half)],
            ),
            out_shape=[pair, jax.ShapeDtypeStruct((2, half), F32)],
            compiler_params=params(40),
            name="both",
        )(meta, shifted, line_inverse, line_inverse, row_y_wide)

    solved, finals, edge_x, edge_y = [], [], [], []
    for n in range(2):
        x0, shifted, edge = column_step(pieces[n], near0[n])
        v, across = both_step(shifted)
        solved.append(x0)
        finals.append(v)
        edge_x.append(edge)
        edge_y.append(across)
    edge_x = jnp.concatenate(edge_x)
    edge_y = jnp.concatenate(edge_y)
    near_x = move(edge_x, 4)
    four = jax.ShapeDtypeStruct((4, half), F32)
    coupled, edge = pl.pallas_call(
        turn_kernel,
        in_specs=[smem] + [vmem] * 5,
        out_specs=[vmem] * 2,
        out_shape=[four] * 2,
        compiler_params=params(8),
        name="turn",
    )(values, edge_x, near_x, row_y, edge_y, column_x)
    near_y = move(edge, 2)
    rows_y = row_call(meta, coupled, line_inverse, half)
    cut = jax.ShapeDtypeStruct((4, rows, half // 2), BF16)
    keep0, send0 = pl.pallas_call(
        first_image_kernel,
        in_specs=[smem] + [vmem] * 3,
        out_specs=[vmem] * 2,
        out_shape=[cut] * 2,
        scratch_shapes=[VMEM((half, half), F32)],
        compiler_params=params(24),
        name="first_image",
    )(meta, solved[0], solved[1], weight)
    keep1, send1 = pl.pallas_call(
        second_image_kernel,
        in_specs=[smem] * 2 + [vmem] * 8,
        out_specs=[vmem] * 2,
        out_shape=[cut] * 2,
        scratch_shapes=[VMEM((half, half), F32)],
        compiler_params=params(24),
        name="second_image",
    )(meta, values, finals[0], finals[1], weight, rows_y, edge, near_y, column_x, column_y)
    part0 = keep0.astype(F32) + move(send0, 1).astype(F32)
    part1 = keep1.astype(F32) + move(send1, 1).astype(F32)
    both = jnp.stack([part0, part1], axis=1).astype(BF16)
    total = 0.0
    for kz in range(2):
        for kx in range(2):
            route = []
            for s in range(4):
                for b in range(8):
                    sy, sx, bx, by, bc = s // 2, s % 2, b // 4, (b // 2) % 2, b % 2
                    target = (by * 2 + (sx ^ kx)) * 8 + bx * 4 + (sy ^ kz) * 2 + bc
                    route.append((s * 8 + b, target))
            total = total + lax.ppermute(both[kz * 2 + kx], ("shot", "slab"), route).astype(F32)
    return total


def row_call(meta, coupled, line_inverse, half):
    def body(m, values, inverse, out):
        row_kernel(values, inverse, out)

    return pl.pallas_call(
        body,
        grid_spec=pltpu.PrefetchScalarGridSpec(
            num_scalar_prefetch=1,
            grid=(1,),
            in_specs=[
                pl.BlockSpec((4, half), lambda i, m: (0, 0)),
                pl.BlockSpec((1, 2, 1, half, half), lambda i, m: (m[0], 0, m[1], 0, 0)),
            ],
            out_specs=pl.BlockSpec((4, half), lambda i, m: (0, 0)),
        ),
        out_shape=jax.ShapeDtypeStruct((4, half), F32),
        compiler_params=params(8),
        name="coupling_row",
    )(meta, coupled, line_inverse)


def solution(mesh):
    placed = (
        P("shot", None, "slab", None, None),
        P("shot", None, "slab", None, None),
        P("shot", None),
        P("shot", None),
        P(None, "slab", None),
        P(),
        P(),
        P(),
    )
    fits = mesh.shape["slab"] == 8 and mesh.shape["shot"] == 4

    def run(*args):
        line_inverse = args[6]
        blocks = fits and line_inverse.shape[0] == 2 and line_inverse.shape[2] == 2
        body = block_shards if blocks else general_shards
        return jax.shard_map(
            body, mesh=mesh, in_specs=placed, out_specs=P(None, "slab", "shot"), check_vma=False
        )(*args)

    return run
```

```python
from functools import partial

import jax
import jax.numpy as jnp
from jax import lax
from jax.experimental import pallas as pl
from jax.experimental.pallas import tpu as pltpu
from jax.sharding import PartitionSpec as P

NX = 1024
STEPS = 2


def pick_index(values, position, axis_number, keep=False):
    return lax.index_in_dim(values, position, axis_number, keepdims=keep)


def line_solve(wavefield, line_inverse, coupling, line_dim):
    in_shape = wavefield.shape
    freq_count = line_inverse.shape[0]
    blocks = line_inverse.shape[2]
    block_len = line_inverse.shape[3]
    real_blocks = line_inverse[:, 0]
    imag_blocks = line_inverse[:, 1]
    if line_dim == 5:
        pieces = wavefield.reshape(in_shape[:5] + (blocks, block_len))
        formula = "shfxcgj,fgij->shfxcgi"
    else:
        pieces = wavefield.reshape(in_shape[:3] + (blocks, block_len, in_shape[4] * in_shape[5]))
        formula = "shfgjz,fgij->shfgiz"
    with_real = jnp.einsum(formula, pieces, real_blocks, preferred_element_type=jnp.float32)
    with_imag = jnp.einsum(formula, pieces, imag_blocks, preferred_element_type=jnp.float32)
    if line_dim == 5:
        comp_axis, block_axis, cell_axis = (4, 4, 4)
        col_shape = (1, 1, freq_count, 1, block_len)
    else:
        with_real = with_real.reshape(in_shape[:3] + (blocks, block_len, in_shape[4], in_shape[5]))
        with_imag = with_imag.reshape(in_shape[:3] + (blocks, block_len, in_shape[4], in_shape[5]))
        comp_axis, block_axis, cell_axis = (5, 3, 3)
        col_shape = (1, 1, freq_count, block_len, 1)
    signs_six = jnp.array([1.0, -1.0], jnp.float32).reshape(1, 2, 1, 1, 1, 1)
    signs_five = jnp.array([1.0, -1.0], jnp.float32).reshape(1, 2, 1, 1, 1)
    u_real = pick_index(with_real, 0, comp_axis) - signs_six * pick_index(with_imag, 1, comp_axis)
    u_imag = pick_index(with_real, 1, comp_axis) + signs_six * pick_index(with_imag, 0, comp_axis)
    coup_real = coupling[:, 0].reshape(1, 1, freq_count, 1, 1)
    coup_imag = coupling[:, 1].reshape(1, 1, freq_count, 1, 1)

    def factor(block_index, column):
        col_real = line_inverse[:, 0, block_index, :, column].astype(jnp.float32).reshape(col_shape)
        col_imag = line_inverse[:, 1, block_index, :, column].astype(jnp.float32).reshape(col_shape)
        return (
            coup_real * col_real - coup_imag * col_imag,
            signs_five * (coup_imag * col_real + coup_real * col_imag),
        )

    fwd_real = [pick_index(u_real, 0, block_axis)]
    fwd_imag = [pick_index(u_imag, 0, block_axis)]
    block_index = 1
    mult_real, mult_imag = factor(block_index, 0)
    prev_real = pick_index(fwd_real[-1], block_len - 1, cell_axis, True)
    prev_imag = pick_index(fwd_imag[-1], block_len - 1, cell_axis, True)
    fwd_real.append(
        pick_index(u_real, block_index, block_axis) + mult_real * prev_real - mult_imag * prev_imag
    )
    fwd_imag.append(
        pick_index(u_imag, block_index, block_axis) + mult_real * prev_imag + mult_imag * prev_real
    )
    out_real = list(fwd_real)
    out_imag = list(fwd_imag)
    block_index = 0
    mult_real, mult_imag = factor(block_index, block_len - 1)
    next_real = pick_index(out_real[block_index + 1], 0, cell_axis, True)
    next_imag = pick_index(out_imag[block_index + 1], 0, cell_axis, True)
    out_real[block_index] = fwd_real[block_index] + mult_real * next_real - mult_imag * next_imag
    out_imag[block_index] = fwd_imag[block_index] + mult_real * next_imag + mult_imag * next_real
    real_line = jnp.stack(out_real, axis=block_axis).reshape(in_shape[:4] + (in_shape[5],))
    imag_line = jnp.stack(out_imag, axis=block_axis).reshape(in_shape[:4] + (in_shape[5],))
    return jnp.stack([real_line, imag_line], axis=4).astype(jnp.bfloat16)


def phase_shift(wavefield, slow_field, frequency):
    angles = frequency[:, None, None] * slow_field[None]
    cosine = jnp.cos(angles)[None, None]
    sine_part = jnp.sin(angles)[None, None]
    signs_five = jnp.array([1.0, -1.0], jnp.float32).reshape(1, 2, 1, 1, 1)
    real_part = wavefield[:, :, :, :, 0].astype(jnp.float32)
    imag_part = wavefield[:, :, :, :, 1].astype(jnp.float32)
    new_real = real_part * cosine - signs_five * imag_part * sine_part
    new_imag = imag_part * cosine + signs_five * real_part * sine_part
    return jnp.stack([new_real, new_imag], axis=4).astype(jnp.bfloat16)


def image_term(wavefield, row_cells, col_cells, shot_positions, frequency):
    source = wavefield[:, 0].astype(jnp.float32)
    receiver = wavefield[:, 1].astype(jnp.float32)
    cross = source[:, :, :, 0] * receiver[:, :, :, 1] - source[:, :, :, 1] * receiver[:, :, :, 0]
    weighted = jnp.sum(cross * frequency[None, :, None, None], axis=1)
    row_gap = row_cells[None, :, None] - shot_positions[:, 0][:, None, None]
    col_gap = col_cells[None, None, :] - shot_positions[:, 1][:, None, None]
    spread = (row_gap * row_gap + col_gap * col_gap).astype(jnp.float32)
    taper = 1.0 / (1.0 + spread * (16.0 / (NX * NX)))
    return jnp.sum(weighted * taper, axis=0)


def general_shards(
    source_field,
    residual_data,
    receiver_lines,
    shot_positions,
    slowness,
    frequency,
    line_inverse,
    coupling,
):
    row_count = source_field.shape[2]
    line_len = source_field.shape[4]
    receiver = residual_data * receiver_lines.astype(jnp.bfloat16)[:, None, None, None, :]
    wavefield = jnp.stack([source_field, receiver], axis=1)
    slab_start = lax.axis_index("slab") * row_count
    own_cells = slab_start + jnp.arange(row_count, dtype=jnp.int32)
    all_cells = jnp.arange(line_len, dtype=jnp.int32)
    solve_first = partial(line_solve, line_inverse=line_inverse, coupling=coupling, line_dim=3)
    solve_second = partial(line_solve, line_inverse=line_inverse, coupling=coupling, line_dim=5)

    def forward(fields):
        return solve_first(lax.all_to_all(fields, "slab", split_axis=5, concat_axis=3, tiled=True))

    def backward(fields):
        return lax.all_to_all(fields, "slab", split_axis=3, concat_axis=5, tiled=True)

    images = []
    for depth_index in range(STEPS):
        shifted = phase_shift(wavefield, slowness[depth_index], frequency)
        if depth_index % 2 == 0:
            wavefield = backward(forward(solve_second(shifted)))
        else:
            wavefield = solve_second(backward(forward(shifted)))
        local_image = image_term(wavefield, own_cells, all_cells, shot_positions, frequency)
        images.append(lax.psum_scatter(local_image, "shot", scatter_dimension=1, tiled=True))
    return jnp.stack(images)


F32 = jnp.float32
BF16 = jnp.bfloat16
SMEM = pltpu.SMEM
VMEM = pltpu.VMEM
MIDDLE = 1.25


def params(mib):
    return pltpu.CompilerParams(vmem_limit_bytes=mib << 20)


def sincos(angle):
    turns = jnp.floor(angle * 0.15915494309189535 + 0.5)
    rest = (angle - turns * 6.28125) - turns * 1.9353071795864769e-3
    rest = rest * 0.25
    square = rest * rest
    sine = rest + rest * square * (
        -1.6666667e-1 + square * (8.3333333e-3 + square * (-1.9841270e-4 + square * 2.7557319e-6))
    )
    cosine = 1.0 + square * (
        -0.5 + square * (4.1666667e-2 + square * (-1.3888889e-3 + square * 2.4801587e-5))
    )
    sine, cosine = 2.0 * sine * cosine, 1.0 - 2.0 * sine * sine
    return 2.0 * sine * cosine, 1.0 - 2.0 * sine * sine


def dot_t(left, right):
    return lax.dot_general(left, right, (((1,), (1,)), ((), ())), preferred_element_type=F32)


def dot(left, right):
    return lax.dot_general(left, right, (((1,), (0,)), ((), ())), preferred_element_type=F32)


def dot_rows(left, right):
    return lax.dot_general(left, right, (((0,), (0,)), ((), ())), preferred_element_type=F32)


def shift_kernel(conjugate, other, meta, freq, mask, field, slowness, out):
    rows = slowness.shape[1]
    f = meta[0] ^ other
    sine, cosine = sincos(freq[f] * slowness[0])
    real = field[0, f, :, 0, :].astype(F32)
    imag = field[0, f, :, 1, :].astype(F32)
    if conjugate:
        keep = mask[...].astype(F32)
        real = real * keep
        imag = -(imag * keep)
    out[:rows] = (real * cosine - imag * sine).astype(BF16)
    out[rows:] = (imag * cosine + real * sine).astype(BF16)


def edge_rows(meta, blocks, block, lanes):
    start = pl.multiple_of((1 - block) * (blocks.shape[2] - 16), 16)
    return jnp.concatenate([blocks[part, block, pl.ds(start, 16), lanes] for part in range(2)], axis=0)


def pick_edge(block, values):
    first = block == 0
    return jnp.where(first, values[15:16], values[0:1]), jnp.where(first, values[31:32], values[16:17])


def edge_product(block, real, imag):
    rr, ir = pick_edge(block, real)
    ri, ii = pick_edge(block, imag)
    return rr - ii, ri + ir


def slab_kernel(meta, coupling, own, core, blocks, same, cross, partial_edge, ends):
    blocks = blocks.at[meta[0]]
    rows = own.shape[0] // 2
    half = blocks.shape[2]
    f, zz, xb, local = meta[0], meta[1], meta[2], meta[3]
    cr, ci = coupling[f, 0], coupling[f, 1]
    spot = lax.broadcasted_iota(jnp.int32, (16, half), 1)
    line = lax.broadcasted_iota(jnp.int32, (16, half), 0)
    solved, columns = [], []
    for k in range(2):
        cells = slice(k * half, (k + 1) * half)
        hot = jnp.where((spot == (half - 1 if k == 0 else 0)) & (line == 0), 1.0, 0.0).astype(BF16)
        left = jnp.concatenate(
            [own[:rows, cells], core[:rows, cells], own[rows:, cells], core[rows:, cells], hot], axis=0
        )
        by_real = dot_t(left, blocks[0, k])
        by_imag = dot_t(left, blocks[1, k])
        n = 2 * rows
        solved.append((by_real[:n] - by_imag[n : 2 * n], by_real[n : 2 * n] + by_imag[:n]))
        ar, ai = by_real[2 * n : 2 * n + 1], by_imag[2 * n : 2 * n + 1]
        columns.append((cr * ar - ci * ai, cr * ai + ci * ar))
        ends[2 * k : 2 * k + 1] = columns[k][0]
        ends[2 * k + 1 : 2 * k + 2] = columns[k][1]

    def couple(k, er, ei):
        qr, qi = columns[k]
        return solved[k][0] + er * qr - ei * qi, solved[k][1] + er * qi + ei * qr

    upper = couple(1, solved[0][0][:, half - 1 :], solved[0][1][:, half - 1 :])
    lower = couple(0, upper[0][:, 0:1], upper[1][:, 0:1])
    first = zz == 0
    pieces = []
    for part in range(2):
        low, high = lower[part].astype(BF16), upper[part].astype(BF16)
        mine, away = jnp.where(first, low, high), jnp.where(first, high, low)
        for n in range(2):
            at = slice((2 * n + part) * rows, (2 * n + part + 1) * rows)
            same[at] = mine[n * rows : (n + 1) * rows]
            cross[at] = away[n * rows : (n + 1) * rows]
        pieces.append(jnp.concatenate([mine, away], axis=1))
    edges = [0.0, 0.0]
    for n in range(2):
        lanes = pl.ds(pl.multiple_of((local ^ n) * rows, rows), rows)
        row = edge_rows(meta, blocks, xb, lanes)
        real = dot(row, pieces[0][n * rows : (n + 1) * rows])
        imag = dot(row, pieces[1][n * rows : (n + 1) * rows])
        er, ei = edge_product(xb, real, imag)
        edges = [edges[0] + er, edges[1] + ei]
    partial_edge[0:1] = edges[0][:, :half]
    partial_edge[1:2] = edges[1][:, :half]
    partial_edge[2:3] = edges[0][:, half:]
    partial_edge[3:4] = edges[1][:, half:]


def phase_kernel(meta, freq, place, own, core, far, far_core, sine, cosine, weight):
    rows, half = own.shape
    omega = freq[meta[0]]
    for k, piece in enumerate((own, core, far, far_core)):
        start = pl.multiple_of((meta[3] ^ k) * rows, rows)
        s, c = sincos(omega * (piece[...].astype(F32) + MIDDLE))
        sine[pl.ds(start, rows)] = s
        cosine[pl.ds(start, rows)] = c
    row = lax.broadcasted_iota(jnp.int32, (weight.shape[0], half), 0) + meta[2] * half - place[0, 0]
    col = lax.broadcasted_iota(jnp.int32, (weight.shape[0], half), 1) + meta[1] * half - place[0, 1]
    spread = (row * row + col * col).astype(F32)
    weight[...] = -omega / (1.0 + spread * (16.0 / (NX * NX)))


def turn_value(meta, coupling, blocks, block):
    cr, ci = coupling[meta[0], 0], coupling[meta[0], 1]
    ar = blocks[0, 1, 0:16, 0:128].astype(F32)[0:1, 0:1]
    ai = blocks[1, 1, 0:16, 0:128].astype(F32)[0:1, 0:1]
    first = block == 0
    return jnp.where(first, cr * ar - ci * ai, 0.0), jnp.where(first, cr * ai + ci * ar, 0.0)


def column_kernel(
    meta, coupling, near, far, blocks, edge_same, edge_cross, sine, cosine, solved, shifted, own_edge, real, imag
):
    blocks = blocks.at[meta[0]]
    rows = near.shape[0] // 4
    half = near.shape[1]
    xb = meta[2]
    for k, (piece, n) in enumerate(((near, 0), (near, 1), (far, 0), (far, 1))):
        start = pl.multiple_of((meta[3] ^ k) * rows, rows)
        real[pl.ds(start, rows)] = piece[2 * n * rows : (2 * n + 1) * rows]
        imag[pl.ds(start, rows)] = piece[(2 * n + 1) * rows : (2 * n + 2) * rows]
    cr, ci = coupling[meta[0], 0], coupling[meta[0], 1]
    ar, ai = turn_value(meta, coupling, blocks, xb)
    row = edge_rows(meta, blocks, xb, slice(0, half))
    own_real, own_imag = edge_product(xb, dot(row, real[...]), dot(row, imag[...]))
    hr = edge_same[0:1] + edge_cross[0:1] + ar * own_real - ai * own_imag
    hi = edge_same[1:2] + edge_cross[1:2] + ar * own_imag + ai * own_real
    add_real = cr * hr - ci * hi
    add_imag = cr * hi + ci * hr
    upper = xb == 1
    low = lax.broadcasted_iota(jnp.int32, (16, half), 0) == 0
    high = lax.broadcasted_iota(jnp.int32, (16, half), 0) == 15
    for ref, add in ((real, add_real), (imag, add_imag)):
        ref[0:16] = (ref[0:16].astype(F32) + jnp.where(low & upper, add, 0.0)).astype(BF16)
        ref[half - 16 :] = (
            ref[half - 16 :].astype(F32) + jnp.where(high & jnp.logical_not(upper), add, 0.0)
        ).astype(BF16)
    left = jnp.concatenate([blocks[0, xb], blocks[1, xb]], axis=0)
    for n in range(0, half, 256):
        cols = slice(n, n + 256)
        by_real = dot(left, real[:, cols])
        by_imag = dot(left, imag[:, cols])
        xr = (by_real[:half] - by_imag[half:]).astype(BF16)
        xi = (by_imag[:half] + by_real[half:]).astype(BF16)
        solved[:half, cols] = xr
        solved[half:, cols] = xi
        xr, xi = xr.astype(F32), xi.astype(F32)
        s, c = sine[:, cols], cosine[:, cols]
        shifted[:half, cols] = (xr * c - xi * s).astype(BF16)
        shifted[half:, cols] = (xi * c + xr * s).astype(BF16)
    own_real, own_imag = edge_product(xb, dot(row, shifted[:half]), dot(row, shifted[half:]))
    own_edge[0:1] = own_real
    own_edge[1:2] = own_imag


def both_kernel(meta, shifted, blocks, solved, edge):
    blocks = blocks.at[meta[0]]
    half = shifted.shape[1]
    xb, zz = meta[2], meta[1]
    left = jnp.concatenate([blocks[0, xb], blocks[1, xb]], axis=0)
    by_real = dot(left, shifted[:half])
    by_imag = dot(left, shifted[half:])
    u = jnp.concatenate(
        [(by_real[:half] - by_imag[half:]).astype(BF16), (by_imag[:half] + by_real[half:]).astype(BF16)], axis=0
    )
    row = dot_t(edge_rows(meta, blocks, zz, slice(0, half)), u)
    edge_real, edge_imag = edge_product(zz, row[:, :half], row[:, half:])
    edge[0:1] = edge_real
    edge[1:2] = edge_imag
    by_real = dot_t(u, blocks[0, zz])
    by_imag = dot_t(u, blocks[1, zz])
    solved[:half] = (by_real[:half] - by_imag[half:]).astype(BF16)
    solved[half:] = (by_real[half:] + by_imag[:half]).astype(BF16)


def image_pieces(meta, image, keep, send):
    rows, cols = keep.shape[1:]
    for kz in range(2):
        for kx in range(2):
            col = pl.multiple_of((meta[5] ^ kx) * cols, cols)
            for other, ref in ((0, keep), (1, send)):
                row = pl.multiple_of(((meta[4] ^ kz) * 2 + (meta[0] ^ other)) * rows, rows)
                ref[kz * 2 + kx] = image[pl.ds(row, rows), pl.ds(col, cols)].astype(BF16)


def pick_end(ends, block):
    first = block == 0
    return jnp.where(first, ends[0:1], ends[2:3]), jnp.where(first, ends[1:2], ends[3:4])


def turn_kernel(meta, coupling, edge_x, near_x, edge_y0, edge_y1, ends, blocks, whole, edge):
    blocks = blocks.at[meta[0]]
    ar, ai = turn_value(meta, coupling, blocks, meta[2])
    zz = meta[1]
    yr, yi = pick_edge(zz, edge_rows(meta, blocks, zz, slice(0, ends.shape[1])).astype(F32))
    pr, pi = pick_end(ends, meta[2])
    for n in range(2):
        r, i = slice(2 * n, 2 * n + 1), slice(2 * n + 1, 2 * n + 2)
        hr = near_x[r] + ar * edge_x[r] - ai * edge_x[i]
        hi = near_x[i] + ar * edge_x[i] + ai * edge_x[r]
        whole[r] = hr
        whole[i] = hi
        sr = jnp.sum(hr * yr - hi * yi, axis=1, keepdims=True)
        si = jnp.sum(hr * yi + hi * yr, axis=1, keepdims=True)
        edge_y = (edge_y0, edge_y1)[n]
        edge[r] = edge_y[0:1] + sr * pr - si * pi
        edge[i] = edge_y[1:2] + sr * pi + si * pr


def split(value):
    high = value.astype(BF16)
    return high.astype(F32), (value - high.astype(F32))


def between_kernel(meta, whole, inverse, source, receiver, weight, out, keep, send, image):
    blocks = inverse.at[meta[0]]
    high, low = split(whole[...])
    left = jnp.concatenate([high, low, high, low], axis=0).astype(BF16)
    by_real = dot_t(left, blocks[0, meta[1]])
    by_imag = dot_t(left, blocks[1, meta[1]])
    by_real = by_real[0:4] + by_real[4:8]
    by_imag = by_imag[0:4] + by_imag[4:8]
    for n in range(2):
        r, i = slice(2 * n, 2 * n + 1), slice(2 * n + 1, 2 * n + 2)
        out[r] = by_real[r] - by_imag[i]
        out[i] = by_real[i] + by_imag[r]
    half = source.shape[1]
    sr, si = source[:half].astype(F32), source[half:].astype(F32)
    rr, ri = receiver[:half].astype(F32), receiver[half:].astype(F32)
    image[...] = (sr * ri + si * rr) * weight[...]
    image_pieces(meta, image, keep, send)


def second_image_kernel(
    meta, coupling, source, receiver, weight, rows_y, edge, near, ends, blocks, keep, send, image
):
    half = source.shape[1]
    blocks = blocks.at[meta[0]]
    ar, ai = turn_value(meta, coupling, blocks, meta[1])
    pr, pi = pick_end(ends, meta[2])
    qr, qi = pick_end(ends, meta[1])

    def triple(value, order):
        high, low = split(value)
        return [high, high, low] if order == 0 else [high, low, high]

    fields = []
    for n, ref in enumerate((source, receiver)):
        r, i = slice(2 * n, 2 * n + 1), slice(2 * n + 1, 2 * n + 2)
        gr = near[r] + ar * edge[r] - ai * edge[i]
        gi = near[i] + ar * edge[i] + ai * edge[r]
        tr, ti = rows_y[r], rows_y[i]
        left, right_real, right_imag = [], [], []
        for a, b, c in ((pr, tr, ti), (pi, -ti, tr), (gr, qr, qi), (gi, -qi, qr)):
            left += triple(a, 0)
            right_real += triple(b, 1)
            right_imag += triple(c, 1)
        pad = [jnp.zeros((4, half), F32)]
        left = jnp.concatenate(left + pad, axis=0).astype(BF16)
        right_real = jnp.concatenate(right_real + pad, axis=0).astype(BF16)
        right_imag = jnp.concatenate(right_imag + pad, axis=0).astype(BF16)
        fields.append(
            (
                ref[:half].astype(F32) + dot_rows(left, right_real),
                ref[half:].astype(F32) + dot_rows(left, right_imag),
            )
        )
    (sr, si), (rr, ri) = fields
    image[...] = (sr * ri + si * rr) * weight[...]
    image_pieces(meta, image, keep, send)


def block_shards(
    source_field, residual_data, receiver_lines, shot_positions, slowness, frequency, line_inverse, coupling
):
    rows, length = slowness.shape[1:]
    half = line_inverse.shape[-1]
    slab = lax.axis_index("slab")
    shot = lax.axis_index("shot")
    meta = jnp.stack(
        [slab & 1, (slab >> 1) & 1, slab >> 2, slab & 3, shot >> 1, shot & 1]
    ).astype(jnp.int32)
    smem = pl.BlockSpec(memory_space=SMEM)
    vmem = pl.BlockSpec(memory_space=VMEM)

    def shape(dtype, *sizes):
        return jax.ShapeDtypeStruct(sizes, dtype)

    def call(body, name, specs, outs, scratch, mib, *args):
        return pl.pallas_call(
            body,
            in_specs=specs,
            out_specs=[vmem] * len(outs),
            out_shape=outs,
            scratch_shapes=scratch,
            compiler_params=params(mib),
            name=name,
        )(*args)

    def move(array, k):
        return lax.ppermute(array, "slab", [(i, i ^ k) for i in range(8)])

    same, far, edges = [], [], []
    for n, field in enumerate((source_field, residual_data)):
        mask = receiver_lines
        if n == 1:
            mask, edges[0] = lax.optimization_barrier((mask, edges[0]))
        halves = []
        for other in (1, 0):
            halves.append(
                call(
                    partial(shift_kernel, n == 1, other),
                    "shift",
                    [smem, smem, vmem, vmem, vmem],
                    [shape(BF16, 2 * rows, length)],
                    [],
                    12,
                    meta,
                    frequency,
                    mask,
                    field,
                    slowness,
                )
            )
        own, core = halves[1][0], move(halves[0][0], 1)
        if n == 0:
            layer = (slowness[1] - MIDDLE).astype(jnp.float16)
            low, high = layer[:, :half], layer[:, half:]
            first = meta[1] == 0
            own_slow = jnp.where(first, low, high)
            far_slow = move(jnp.where(first, high, low), 2)
            core, far_slow = lax.optimization_barrier((core, far_slow))
        mine, cross, edge, ends = call(
            slab_kernel,
            "slab",
            [smem, smem, vmem, vmem, vmem],
            [shape(BF16, 4 * rows, half)] * 2 + [shape(F32, 4, half)] * 2,
            [],
            16,
            meta,
            coupling,
            own,
            core,
            line_inverse,
        )
        same.append(mine)
        edges.append(edge)
        if n == 0:
            far.append(move(cross, 2))
    own_slow, far_slow, edges[1] = lax.optimization_barrier((own_slow, far_slow, edges[1]))
    edges = jnp.stack(edges)
    edge_same = move(edges[:, :2], 4)
    edge_cross = move(edges[:, 2:], 6)
    cross, edge_same, edge_cross, far[0] = lax.optimization_barrier((cross, edge_same, edge_cross, far[0]))
    far.append(move(cross, 2))
    pair = shape(BF16, 2 * half, half)
    line = shape(F32, 2, half)
    four = shape(F32, 4, half)
    core_slow = move(jnp.stack([own_slow, far_slow]), 1)
    block = shape(F32, half, half)
    sine, cosine, weight = call(
        phase_kernel,
        "phase",
        [smem] * 3 + [vmem] * 4,
        [block] * 3,
        [],
        8,
        meta,
        frequency,
        shot_positions,
        own_slow.astype(F32),
        core_slow[0].astype(F32),
        far_slow.astype(F32),
        core_slow[1].astype(F32),
    )
    solved, finals, edge_x, edge_y = [], [], [], []
    for n in range(2):
        if n == 1:
            same[1], finals[0] = lax.optimization_barrier((same[1], finals[0]))
        x0, turned, edge = call(
            column_kernel,
            "column",
            [smem, smem] + [vmem] * 7,
            [pair, pair, line],
            [VMEM((half, half), BF16)] * 2,
            16,
            meta,
            coupling,
            same[n],
            far[n],
            line_inverse,
            edge_same[n],
            edge_cross[n],
            sine,
            cosine,
        )
        v, across = call(both_kernel, "both", [smem] + [vmem] * 2, [pair, line], [], 20, meta, turned, line_inverse)
        solved.append(x0)
        finals.append(v)
        edge_x.append(edge)
        edge_y.append(across)
    edge_x = jnp.concatenate(edge_x)
    near_x = move(edge_x, 4)
    coupled, edge = call(
        turn_kernel,
        "turn",
        [smem, smem] + [vmem] * 6,
        [four, four],
        [],
        4,
        meta,
        coupling,
        edge_x,
        near_x,
        *edge_y,
        ends,
        line_inverse,
    )
    near_y = move(edge, 2)
    cut = shape(BF16, 4, rows, half // 2)
    scratch = [VMEM((half, half), F32)]
    rows_y, keep0, send0 = call(
        between_kernel,
        "between",
        [smem] + [vmem] * 5,
        [four, cut, cut],
        scratch,
        12,
        meta,
        coupled,
        line_inverse,
        solved[0],
        solved[1],
        weight,
    )
    keep1, send1 = call(
        second_image_kernel,
        "second_image",
        [smem] * 2 + [vmem] * 8,
        [cut] * 2,
        scratch,
        12,
        meta,
        coupling,
        finals[0],
        finals[1],
        weight,
        rows_y,
        edge,
        near_y,
        ends,
        line_inverse,
    )
    part0 = keep0.astype(F32) + move(send0, 1).astype(F32)
    part1 = keep1.astype(F32) + move(send1, 1).astype(F32)
    both = jnp.stack([part0, part1], axis=1).astype(BF16)
    total = 0.0
    for kz in range(2):
        for kx in range(2):
            route = []
            for s in range(4):
                for b in range(8):
                    sy, sx, bx, by, bc = s // 2, s % 2, b // 4, (b // 2) % 2, b % 2
                    target = (by * 2 + (sx ^ kx)) * 8 + bx * 4 + (sy ^ kz) * 2 + bc
                    route.append((s * 8 + b, target))
            total = total + lax.ppermute(both[kz * 2 + kx], ("shot", "slab"), route).astype(F32)
    return total


def solution(mesh):
    placed = (
        P("shot", None, "slab", None, None),
        P("shot", None, "slab", None, None),
        P("shot", None),
        P("shot", None),
        P(None, "slab", None),
        P(),
        P(),
        P(),
    )
    fits = mesh.shape["slab"] == 8 and mesh.shape["shot"] == 4

    def run(*args):
        line_inverse = args[6]
        blocks = fits and line_inverse.shape[0] == 2 and line_inverse.shape[2] == 2
        body = block_shards if blocks else general_shards
        return jax.shard_map(
            body, mesh=mesh, in_specs=placed, out_specs=P(None, "slab", "shot"), check_vma=False
        )(*args)

    return run
```

```python
from functools import partial

import jax
import jax.numpy as jnp
from jax import lax
from jax.experimental import pallas as pl
from jax.experimental.pallas import tpu as pltpu
from jax.sharding import PartitionSpec as P

NX = 1024
STEPS = 2


def pick_index(values, position, axis_number, keep=False):
    return lax.index_in_dim(values, position, axis_number, keepdims=keep)


def line_solve(wavefield, line_inverse, coupling, line_dim):
    in_shape = wavefield.shape
    freq_count = line_inverse.shape[0]
    blocks = line_inverse.shape[2]
    block_len = line_inverse.shape[3]
    real_blocks = line_inverse[:, 0]
    imag_blocks = line_inverse[:, 1]
    if line_dim == 5:
        pieces = wavefield.reshape(in_shape[:5] + (blocks, block_len))
        formula = "shfxcgj,fgij->shfxcgi"
    else:
        pieces = wavefield.reshape(in_shape[:3] + (blocks, block_len, in_shape[4] * in_shape[5]))
        formula = "shfgjz,fgij->shfgiz"
    with_real = jnp.einsum(formula, pieces, real_blocks, preferred_element_type=jnp.float32)
    with_imag = jnp.einsum(formula, pieces, imag_blocks, preferred_element_type=jnp.float32)
    if line_dim == 5:
        comp_axis, block_axis, cell_axis = (4, 4, 4)
        col_shape = (1, 1, freq_count, 1, block_len)
    else:
        with_real = with_real.reshape(in_shape[:3] + (blocks, block_len, in_shape[4], in_shape[5]))
        with_imag = with_imag.reshape(in_shape[:3] + (blocks, block_len, in_shape[4], in_shape[5]))
        comp_axis, block_axis, cell_axis = (5, 3, 3)
        col_shape = (1, 1, freq_count, block_len, 1)
    signs_six = jnp.array([1.0, -1.0], jnp.float32).reshape(1, 2, 1, 1, 1, 1)
    signs_five = jnp.array([1.0, -1.0], jnp.float32).reshape(1, 2, 1, 1, 1)
    u_real = pick_index(with_real, 0, comp_axis) - signs_six * pick_index(with_imag, 1, comp_axis)
    u_imag = pick_index(with_real, 1, comp_axis) + signs_six * pick_index(with_imag, 0, comp_axis)
    coup_real = coupling[:, 0].reshape(1, 1, freq_count, 1, 1)
    coup_imag = coupling[:, 1].reshape(1, 1, freq_count, 1, 1)

    def factor(block_index, column):
        col_real = line_inverse[:, 0, block_index, :, column].astype(jnp.float32).reshape(col_shape)
        col_imag = line_inverse[:, 1, block_index, :, column].astype(jnp.float32).reshape(col_shape)
        return (
            coup_real * col_real - coup_imag * col_imag,
            signs_five * (coup_imag * col_real + coup_real * col_imag),
        )

    fwd_real = [pick_index(u_real, 0, block_axis)]
    fwd_imag = [pick_index(u_imag, 0, block_axis)]
    block_index = 1
    mult_real, mult_imag = factor(block_index, 0)
    prev_real = pick_index(fwd_real[-1], block_len - 1, cell_axis, True)
    prev_imag = pick_index(fwd_imag[-1], block_len - 1, cell_axis, True)
    fwd_real.append(
        pick_index(u_real, block_index, block_axis) + mult_real * prev_real - mult_imag * prev_imag
    )
    fwd_imag.append(
        pick_index(u_imag, block_index, block_axis) + mult_real * prev_imag + mult_imag * prev_real
    )
    out_real = list(fwd_real)
    out_imag = list(fwd_imag)
    block_index = 0
    mult_real, mult_imag = factor(block_index, block_len - 1)
    next_real = pick_index(out_real[block_index + 1], 0, cell_axis, True)
    next_imag = pick_index(out_imag[block_index + 1], 0, cell_axis, True)
    out_real[block_index] = fwd_real[block_index] + mult_real * next_real - mult_imag * next_imag
    out_imag[block_index] = fwd_imag[block_index] + mult_real * next_imag + mult_imag * next_real
    real_line = jnp.stack(out_real, axis=block_axis).reshape(in_shape[:4] + (in_shape[5],))
    imag_line = jnp.stack(out_imag, axis=block_axis).reshape(in_shape[:4] + (in_shape[5],))
    return jnp.stack([real_line, imag_line], axis=4).astype(jnp.bfloat16)


def phase_shift(wavefield, slow_field, frequency):
    angles = frequency[:, None, None] * slow_field[None]
    cosine = jnp.cos(angles)[None, None]
    sine_part = jnp.sin(angles)[None, None]
    signs_five = jnp.array([1.0, -1.0], jnp.float32).reshape(1, 2, 1, 1, 1)
    real_part = wavefield[:, :, :, :, 0].astype(jnp.float32)
    imag_part = wavefield[:, :, :, :, 1].astype(jnp.float32)
    new_real = real_part * cosine - signs_five * imag_part * sine_part
    new_imag = imag_part * cosine + signs_five * real_part * sine_part
    return jnp.stack([new_real, new_imag], axis=4).astype(jnp.bfloat16)


def image_term(wavefield, row_cells, col_cells, shot_positions, frequency):
    source = wavefield[:, 0].astype(jnp.float32)
    receiver = wavefield[:, 1].astype(jnp.float32)
    cross = source[:, :, :, 0] * receiver[:, :, :, 1] - source[:, :, :, 1] * receiver[:, :, :, 0]
    weighted = jnp.sum(cross * frequency[None, :, None, None], axis=1)
    row_gap = row_cells[None, :, None] - shot_positions[:, 0][:, None, None]
    col_gap = col_cells[None, None, :] - shot_positions[:, 1][:, None, None]
    spread = (row_gap * row_gap + col_gap * col_gap).astype(jnp.float32)
    taper = 1.0 / (1.0 + spread * (16.0 / (NX * NX)))
    return jnp.sum(weighted * taper, axis=0)


def general_shards(
    source_field,
    residual_data,
    receiver_lines,
    shot_positions,
    slowness,
    frequency,
    line_inverse,
    coupling,
):
    row_count = source_field.shape[2]
    line_len = source_field.shape[4]
    receiver = residual_data * receiver_lines.astype(jnp.bfloat16)[:, None, None, None, :]
    wavefield = jnp.stack([source_field, receiver], axis=1)
    slab_start = lax.axis_index("slab") * row_count
    own_cells = slab_start + jnp.arange(row_count, dtype=jnp.int32)
    all_cells = jnp.arange(line_len, dtype=jnp.int32)
    solve_first = partial(line_solve, line_inverse=line_inverse, coupling=coupling, line_dim=3)
    solve_second = partial(line_solve, line_inverse=line_inverse, coupling=coupling, line_dim=5)

    def forward(fields):
        return solve_first(lax.all_to_all(fields, "slab", split_axis=5, concat_axis=3, tiled=True))

    def backward(fields):
        return lax.all_to_all(fields, "slab", split_axis=3, concat_axis=5, tiled=True)

    images = []
    for depth_index in range(STEPS):
        shifted = phase_shift(wavefield, slowness[depth_index], frequency)
        if depth_index % 2 == 0:
            wavefield = backward(forward(solve_second(shifted)))
        else:
            wavefield = solve_second(backward(forward(shifted)))
        local_image = image_term(wavefield, own_cells, all_cells, shot_positions, frequency)
        images.append(lax.psum_scatter(local_image, "shot", scatter_dimension=1, tiled=True))
    return jnp.stack(images)


F32 = jnp.float32
BF16 = jnp.bfloat16
SMEM = pltpu.SMEM
VMEM = pltpu.VMEM
MIDDLE = 1.25


def params(mib):
    return pltpu.CompilerParams(vmem_limit_bytes=mib << 20)


def sincos(angle):
    turns = jnp.floor(angle * 0.15915494309189535 + 0.5)
    rest = (angle - turns * 6.28125) - turns * 1.9353071795864769e-3
    rest = rest * 0.25
    square = rest * rest
    sine = rest + rest * square * (
        -1.6666667e-1 + square * (8.3333333e-3 + square * (-1.9841270e-4 + square * 2.7557319e-6))
    )
    cosine = 1.0 + square * (
        -0.5 + square * (4.1666667e-2 + square * (-1.3888889e-3 + square * 2.4801587e-5))
    )
    sine, cosine = 2.0 * sine * cosine, 1.0 - 2.0 * sine * sine
    return 2.0 * sine * cosine, 1.0 - 2.0 * sine * sine


def dot_t(left, right):
    return lax.dot_general(left, right, (((1,), (1,)), ((), ())), preferred_element_type=F32)


def dot(left, right):
    return lax.dot_general(left, right, (((1,), (0,)), ((), ())), preferred_element_type=F32)


def dot_rows(left, right):
    return lax.dot_general(left, right, (((0,), (0,)), ((), ())), preferred_element_type=F32)


def rotate(omega, slow, real, imag, out):
    rows = slow.shape[0]
    sine, cosine = sincos(omega * slow)
    out[:rows] = (real * cosine - imag * sine).astype(BF16)
    out[rows:] = (imag * cosine + real * sine).astype(BF16)


def receiver_kernel(meta, scalars, mask, field, slowness, own, other):
    keep = mask[...].astype(F32)
    for k, out in ((1, other), (0, own)):
        f = meta[0] ^ k
        real = field[0, f, :, 0, :].astype(F32) * keep
        imag = -(field[0, f, :, 1, :].astype(F32) * keep)
        rotate(scalars[f], slowness[0], real, imag, out)


def other_kernel(meta, scalars, field, slowness, out, raw, slow):
    f = meta[0] ^ 1
    rotate(scalars[f], slowness[0], field[0, f, :, 0, :].astype(F32), field[0, f, :, 1, :].astype(F32), out)
    raw[...] = field[0, meta[0]]
    slow[...] = slowness[0]


def own_kernel(meta, scalars, raw, slow, inverse, out, blocks, sem):
    fetch = pltpu.make_async_copy(inverse.at[meta[0]], blocks, sem)
    fetch.start()
    rotate(scalars[meta[0]], slow[...], raw[:, 0, :].astype(F32), raw[:, 1, :].astype(F32), out)
    fetch.wait()


def edge_rows(meta, blocks, block, lanes):
    start = pl.multiple_of((1 - block) * (blocks.shape[2] - 16), 16)
    return jnp.concatenate([blocks[part, block, pl.ds(start, 16), lanes] for part in range(2)], axis=0)


def pick_edge(block, values):
    first = block == 0
    return jnp.where(first, values[15:16], values[0:1]), jnp.where(first, values[31:32], values[16:17])


def edge_product(block, real, imag):
    rr, ir = pick_edge(block, real)
    ri, ii = pick_edge(block, imag)
    return rr - ii, ri + ir


def slab_kernel(meta, scalars, own, core, blocks, same, cross, ends):
    rows = own.shape[0] // 2
    half = blocks.shape[2]
    f, zz = meta[0], meta[1]
    cr, ci = scalars[2 + 2 * f], scalars[3 + 2 * f]
    spot = lax.broadcasted_iota(jnp.int32, (16, half), 1)
    line = lax.broadcasted_iota(jnp.int32, (16, half), 0)
    solved, columns = [], []
    for k in range(2):
        cells = slice(k * half, (k + 1) * half)
        hot = jnp.where((spot == (half - 1 if k == 0 else 0)) & (line == 0), 1.0, 0.0).astype(BF16)
        left = jnp.concatenate(
            [own[:rows, cells], core[:rows, cells], own[rows:, cells], core[rows:, cells], hot], axis=0
        )
        by_real = dot_t(left, blocks[0, k])
        by_imag = dot_t(left, blocks[1, k])
        n = 2 * rows
        solved.append((by_real[:n] - by_imag[n : 2 * n], by_real[n : 2 * n] + by_imag[:n]))
        ar, ai = by_real[2 * n : 2 * n + 1], by_imag[2 * n : 2 * n + 1]
        columns.append((cr * ar - ci * ai, cr * ai + ci * ar))
        ends[2 * k : 2 * k + 1] = columns[k][0]
        ends[2 * k + 1 : 2 * k + 2] = columns[k][1]

    def couple(k, er, ei):
        qr, qi = columns[k]
        return solved[k][0] + er * qr - ei * qi, solved[k][1] + er * qi + ei * qr

    upper = couple(1, solved[0][0][:, half - 1 :], solved[0][1][:, half - 1 :])
    lower = couple(0, upper[0][:, 0:1], upper[1][:, 0:1])
    first = zz == 0
    for part in range(2):
        low, high = lower[part].astype(BF16), upper[part].astype(BF16)
        mine, away = jnp.where(first, low, high), jnp.where(first, high, low)
        for n in range(2):
            at = slice((2 * n + part) * rows, (2 * n + part + 1) * rows)
            same[at] = mine[n * rows : (n + 1) * rows]
            cross[at] = away[n * rows : (n + 1) * rows]


def edge_kernel(meta, blocks, same0, cross0, same1, cross1, edge_same, edge_cross):
    rows = same0.shape[0] // 4
    xb, local = meta[2], meta[3]
    for refs, out in (((same0, same1), edge_same), ((cross0, cross1), edge_cross)):
        for part in range(2):
            total = 0.0
            for n in range(2):
                lanes = pl.ds(pl.multiple_of((local ^ n) * rows, rows), rows)
                row = edge_rows(meta, blocks, xb, lanes)
                at = slice((2 * n + part) * rows, (2 * n + part + 1) * rows)
                total = total + dot(row, jnp.concatenate([ref[at] for ref in refs], axis=1))
            if part == 0:
                real = total
        er, ei = edge_product(xb, real, total)
        half = same0.shape[1]
        for k in range(2):
            out[2 * k : 2 * k + 1] = er[:, k * half : (k + 1) * half]
            out[2 * k + 1 : 2 * k + 2] = ei[:, k * half : (k + 1) * half]


def phase_kernel(meta, scalars, place, own, core, far, far_core, sine, cosine, weight):
    rows, half = own.shape
    omega = scalars[meta[0]]
    for k, piece in enumerate((own, core, far, far_core)):
        start = pl.multiple_of((meta[3] ^ k) * rows, rows)
        s, c = sincos(omega * (piece[...].astype(F32) + MIDDLE))
        sine[pl.ds(start, rows)] = s
        cosine[pl.ds(start, rows)] = c
    row = lax.broadcasted_iota(jnp.int32, (weight.shape[0], half), 0) + meta[2] * half - place[0, 0]
    col = lax.broadcasted_iota(jnp.int32, (weight.shape[0], half), 1) + meta[1] * half - place[0, 1]
    spread = (row * row + col * col).astype(F32)
    weight[...] = -omega / (1.0 + spread * (16.0 / (NX * NX)))


def turn_value(meta, scalars, blocks, block):
    cr, ci = scalars[2 + 2 * meta[0]], scalars[3 + 2 * meta[0]]
    ar = blocks[0, 1, 0:16, 0:128].astype(F32)[0:1, 0:1]
    ai = blocks[1, 1, 0:16, 0:128].astype(F32)[0:1, 0:1]
    first = block == 0
    return jnp.where(first, cr * ar - ci * ai, 0.0), jnp.where(first, cr * ai + ci * ar, 0.0)


def column_kernel(
    meta, scalars, near, far, blocks, edge_same, edge_cross, sine, cosine, solved, shifted, own_edge, real, imag
):
    rows = near.shape[0] // 4
    half = near.shape[1]
    xb = meta[2]
    for k, (piece, n) in enumerate(((near, 0), (near, 1), (far, 0), (far, 1))):
        start = pl.multiple_of((meta[3] ^ k) * rows, rows)
        real[pl.ds(start, rows)] = piece[2 * n * rows : (2 * n + 1) * rows]
        imag[pl.ds(start, rows)] = piece[(2 * n + 1) * rows : (2 * n + 2) * rows]
    cr, ci = scalars[2 + 2 * meta[0]], scalars[3 + 2 * meta[0]]
    ar, ai = turn_value(meta, scalars, blocks, xb)
    row = edge_rows(meta, blocks, xb, slice(0, half))
    own_real, own_imag = edge_product(xb, dot(row, real[...]), dot(row, imag[...]))
    hr = edge_same[0:1] + edge_cross[0:1] + ar * own_real - ai * own_imag
    hi = edge_same[1:2] + edge_cross[1:2] + ar * own_imag + ai * own_real
    add_real = cr * hr - ci * hi
    add_imag = cr * hi + ci * hr
    upper = xb == 1
    low = lax.broadcasted_iota(jnp.int32, (16, half), 0) == 0
    high = lax.broadcasted_iota(jnp.int32, (16, half), 0) == 15
    for ref, add in ((real, add_real), (imag, add_imag)):
        ref[0:16] = (ref[0:16].astype(F32) + jnp.where(low & upper, add, 0.0)).astype(BF16)
        ref[half - 16 :] = (
            ref[half - 16 :].astype(F32) + jnp.where(high & jnp.logical_not(upper), add, 0.0)
        ).astype(BF16)
    left = jnp.concatenate([blocks[0, xb], blocks[1, xb]], axis=0)
    for n in range(0, half, 256):
        cols = slice(n, n + 256)
        by_real = dot(left, real[:, cols])
        by_imag = dot(left, imag[:, cols])
        xr = (by_real[:half] - by_imag[half:]).astype(BF16)
        xi = (by_imag[:half] + by_real[half:]).astype(BF16)
        solved[:half, cols] = xr
        solved[half:, cols] = xi
        xr, xi = xr.astype(F32), xi.astype(F32)
        s, c = sine[:, cols], cosine[:, cols]
        shifted[:half, cols] = (xr * c - xi * s).astype(BF16)
        shifted[half:, cols] = (xi * c + xr * s).astype(BF16)
    own_real, own_imag = edge_product(xb, dot(row, shifted[:half]), dot(row, shifted[half:]))
    own_edge[0:1] = own_real
    own_edge[1:2] = own_imag


def both_kernel(meta, shifted, blocks, solved, edge):
    half = shifted.shape[1]
    xb, zz = meta[2], meta[1]
    left = jnp.concatenate([blocks[0, xb], blocks[1, xb]], axis=0)
    by_real = dot(left, shifted[:half])
    by_imag = dot(left, shifted[half:])
    u = jnp.concatenate(
        [(by_real[:half] - by_imag[half:]).astype(BF16), (by_imag[:half] + by_real[half:]).astype(BF16)], axis=0
    )
    row = dot_t(edge_rows(meta, blocks, zz, slice(0, half)), u)
    edge_real, edge_imag = edge_product(zz, row[:, :half], row[:, half:])
    edge[0:1] = edge_real
    edge[1:2] = edge_imag
    by_real = dot_t(u, blocks[0, zz])
    by_imag = dot_t(u, blocks[1, zz])
    solved[:half] = (by_real[:half] - by_imag[half:]).astype(BF16)
    solved[half:] = (by_real[half:] + by_imag[:half]).astype(BF16)


def image_pieces(meta, image, keep, send):
    rows, cols = keep.shape[1:]
    for kz in range(2):
        for kx in range(2):
            col = pl.multiple_of((meta[5] ^ kx) * cols, cols)
            for other, ref in ((0, keep), (1, send)):
                row = pl.multiple_of(((meta[4] ^ kz) * 2 + (meta[0] ^ other)) * rows, rows)
                ref[kz * 2 + kx] = image[pl.ds(row, rows), pl.ds(col, cols)].astype(BF16)


def pick_end(ends, block):
    first = block == 0
    return jnp.where(first, ends[0:1], ends[2:3]), jnp.where(first, ends[1:2], ends[3:4])


def turn_kernel(meta, scalars, edge_x, near_x, edge_y0, edge_y1, ends, blocks, whole, edge):
    ar, ai = turn_value(meta, scalars, blocks, meta[2])
    zz = meta[1]
    yr, yi = pick_edge(zz, edge_rows(meta, blocks, zz, slice(0, ends.shape[1])).astype(F32))
    pr, pi = pick_end(ends, meta[2])
    for n in range(2):
        r, i = slice(2 * n, 2 * n + 1), slice(2 * n + 1, 2 * n + 2)
        hr = near_x[r] + ar * edge_x[r] - ai * edge_x[i]
        hi = near_x[i] + ar * edge_x[i] + ai * edge_x[r]
        whole[r] = hr
        whole[i] = hi
        sr = jnp.sum(hr * yr - hi * yi, axis=1, keepdims=True)
        si = jnp.sum(hr * yi + hi * yr, axis=1, keepdims=True)
        edge_y = (edge_y0, edge_y1)[n]
        edge[r] = edge_y[0:1] + sr * pr - si * pi
        edge[i] = edge_y[1:2] + sr * pi + si * pr


def split(value):
    high = value.astype(BF16)
    return high.astype(F32), (value - high.astype(F32))


def between_kernel(meta, whole, blocks, source, receiver, weight, out, keep, send, image):
    high, low = split(whole[...])
    left = jnp.concatenate([high, low, high, low], axis=0).astype(BF16)
    by_real = dot_t(left, blocks[0, meta[1]])
    by_imag = dot_t(left, blocks[1, meta[1]])
    by_real = by_real[0:4] + by_real[4:8]
    by_imag = by_imag[0:4] + by_imag[4:8]
    for n in range(2):
        r, i = slice(2 * n, 2 * n + 1), slice(2 * n + 1, 2 * n + 2)
        out[r] = by_real[r] - by_imag[i]
        out[i] = by_real[i] + by_imag[r]
    half = source.shape[1]
    sr, si = source[:half].astype(F32), source[half:].astype(F32)
    rr, ri = receiver[:half].astype(F32), receiver[half:].astype(F32)
    image[...] = (sr * ri + si * rr) * weight[...]
    image_pieces(meta, image, keep, send)


def second_image_kernel(
    meta, scalars, source, receiver, weight, rows_y, edge, near, ends, blocks, keep, send, image
):
    half = source.shape[1]
    ar, ai = turn_value(meta, scalars, blocks, meta[1])
    pr, pi = pick_end(ends, meta[2])
    qr, qi = pick_end(ends, meta[1])

    def triple(value, order):
        high, low = split(value)
        return [high, high, low] if order == 0 else [high, low, high]

    fields = []
    for n, ref in enumerate((source, receiver)):
        r, i = slice(2 * n, 2 * n + 1), slice(2 * n + 1, 2 * n + 2)
        gr = near[r] + ar * edge[r] - ai * edge[i]
        gi = near[i] + ar * edge[i] + ai * edge[r]
        tr, ti = rows_y[r], rows_y[i]
        left, right_real, right_imag = [], [], []
        for a, b, c in ((pr, tr, ti), (pi, -ti, tr), (gr, qr, qi), (gi, -qi, qr)):
            left += triple(a, 0)
            right_real += triple(b, 1)
            right_imag += triple(c, 1)
        pad = [jnp.zeros((4, half), F32)]
        left = jnp.concatenate(left + pad, axis=0).astype(BF16)
        right_real = jnp.concatenate(right_real + pad, axis=0).astype(BF16)
        right_imag = jnp.concatenate(right_imag + pad, axis=0).astype(BF16)
        fields.append(
            (
                ref[:half].astype(F32) + dot_rows(left, right_real),
                ref[half:].astype(F32) + dot_rows(left, right_imag),
            )
        )
    (sr, si), (rr, ri) = fields
    image[...] = (sr * ri + si * rr) * weight[...]
    image_pieces(meta, image, keep, send)


def block_shards(
    source_field, residual_data, receiver_lines, shot_positions, slowness, frequency, line_inverse, coupling
):
    rows, length = slowness.shape[1:]
    half = line_inverse.shape[-1]
    slab = lax.axis_index("slab")
    shot = lax.axis_index("shot")
    meta = jnp.stack(
        [slab & 1, (slab >> 1) & 1, slab >> 2, slab & 3, shot >> 1, shot & 1]
    ).astype(jnp.int32)
    scalars = jnp.concatenate([frequency, coupling.reshape(-1)])
    smem = pl.BlockSpec(memory_space=SMEM)
    vmem = pl.BlockSpec(memory_space=VMEM)
    hbm = pl.BlockSpec(memory_space=pltpu.HBM)

    def shape(dtype, *sizes):
        return jax.ShapeDtypeStruct(sizes, dtype)

    def call(body, name, specs, outs, scratch, mib, *args):
        return pl.pallas_call(
            body,
            in_specs=specs,
            out_specs=[vmem] * len(outs),
            out_shape=outs,
            scratch_shapes=scratch,
            compiler_params=params(mib),
            name=name,
        )(*args)

    def move(array, k):
        return lax.ppermute(array, "slab", [(i, i ^ k) for i in range(8)])

    same, far, edges = [], [], []
    for n, field in enumerate((source_field, residual_data)):
        cut = shape(BF16, 2 * rows, length)
        if n == 0:
            core, raw, slow = call(
                other_kernel,
                "other",
                [smem, smem, vmem, vmem],
                [cut, shape(BF16, rows, 2, length), shape(F32, rows, length)],
                [],
                12,
                meta,
                scalars,
                field,
                slowness,
            )
            own, blocks = call(
                own_kernel,
                "own",
                [smem, smem, vmem, vmem, hbm],
                [cut, shape(BF16, *line_inverse.shape[1:])],
                [pltpu.SemaphoreType.DMA],
                48,
                meta,
                scalars,
                raw,
                slow,
                line_inverse,
            )
        else:
            mask, near_slow = lax.optimization_barrier((receiver_lines, near_slow))
            own, core = call(
                receiver_kernel,
                "receiver",
                [smem, smem, vmem, vmem, vmem],
                [cut] * 2,
                [],
                12,
                meta,
                scalars,
                mask,
                field,
                slowness,
            )
            far_slow = move(near_slow, 2)
        core = move(core, 1)
        mine, cross, ends = call(
            slab_kernel,
            "slab",
            [smem, smem, vmem, vmem, vmem],
            [shape(BF16, 4 * rows, half)] * 2 + [shape(F32, 4, half)],
            [],
            16,
            meta,
            scalars,
            own,
            core,
            blocks,
        )
        same.append(mine)
        edges.append(cross)
        if n == 0:
            far.append(move(cross, 2))
            layer, same[0] = lax.optimization_barrier((slowness[1], same[0]))
            layer = (layer - MIDDLE).astype(jnp.float16)
            low, high = layer[:, :half], layer[:, half:]
            first = meta[1] == 0
            own_slow = jnp.where(first, low, high)
            near_slow = jnp.where(first, high, low)
    edges = call(
        edge_kernel,
        "edge",
        [smem] + [vmem] * 5,
        [shape(F32, 4, half)] * 2,
        [],
        8,
        meta,
        blocks,
        same[0],
        edges[0],
        same[1],
        edges[1],
    )
    edge_same = move(edges[0], 4)
    edge_cross = move(edges[1], 6)
    cross, far[0] = lax.optimization_barrier((cross, far[0]))
    far.append(move(cross, 2))
    pair = shape(BF16, 2 * half, half)
    line = shape(F32, 2, half)
    four = shape(F32, 4, half)
    far_slow, edge_same, edge_cross = lax.optimization_barrier((far_slow, edge_same, edge_cross))
    core_slow = move(jnp.stack([own_slow, far_slow]), 1)
    block = shape(F32, half, half)
    sine, cosine, weight = call(
        phase_kernel,
        "phase",
        [smem] * 3 + [vmem] * 4,
        [block] * 3,
        [],
        8,
        meta,
        scalars,
        shot_positions,
        own_slow.astype(F32),
        core_slow[0].astype(F32),
        far_slow.astype(F32),
        core_slow[1].astype(F32),
    )
    solved, finals, edge_x, edge_y = [], [], [], []
    for n in range(2):
        if n == 1:
            same[1], finals[0] = lax.optimization_barrier((same[1], finals[0]))
        x0, turned, edge = call(
            column_kernel,
            "column",
            [smem, smem] + [vmem] * 7,
            [pair, pair, line],
            [VMEM((half, half), BF16)] * 2,
            16,
            meta,
            scalars,
            same[n],
            far[n],
            blocks,
            edge_same[2 * n : 2 * n + 2],
            edge_cross[2 * n : 2 * n + 2],
            sine,
            cosine,
        )
        v, across = call(both_kernel, "both", [smem] + [vmem] * 2, [pair, line], [], 20, meta, turned, blocks)
        solved.append(x0)
        finals.append(v)
        edge_x.append(edge)
        edge_y.append(across)
    edge_x = jnp.concatenate(edge_x)
    near_x = move(edge_x, 4)
    coupled, edge = call(
        turn_kernel,
        "turn",
        [smem, smem] + [vmem] * 6,
        [four, four],
        [],
        4,
        meta,
        scalars,
        edge_x,
        near_x,
        *edge_y,
        ends,
        blocks,
    )
    near_y = move(edge, 2)
    cut = shape(BF16, 4, rows, half // 2)
    scratch = [VMEM((half, half), F32)]
    rows_y, keep0, send0 = call(
        between_kernel,
        "between",
        [smem] + [vmem] * 5,
        [four, cut, cut],
        scratch,
        12,
        meta,
        coupled,
        blocks,
        solved[0],
        solved[1],
        weight,
    )
    near_y, rows_y, send0 = lax.optimization_barrier((near_y, rows_y, send0))
    keep1, send1 = call(
        second_image_kernel,
        "second_image",
        [smem] * 2 + [vmem] * 8,
        [cut] * 2,
        scratch,
        12,
        meta,
        scalars,
        finals[0],
        finals[1],
        weight,
        rows_y,
        edge,
        near_y,
        ends,
        blocks,
    )
    part0 = keep0.astype(F32) + move(send0, 1).astype(F32)
    part1 = keep1.astype(F32) + move(send1, 1).astype(F32)
    both = jnp.stack([part0, part1], axis=1).astype(BF16)
    total = 0.0
    for kz in (1, 0):
        for kx in (1, 0):
            route = []
            for s in range(4):
                for b in range(8):
                    sy, sx, bx, bc = s // 2, s % 2, b // 4, b % 2
                    by = (b // 2) % 2
                    target = (by * 2 + (sx ^ kx)) * 8 + bx * 4 + (sy ^ kz) * 2 + bc
                    route.append((s * 8 + b, target))
            total = total + lax.ppermute(both[kz * 2 + kx], ("shot", "slab"), route).astype(F32)
    return total


def solution(mesh):
    placed = (
        P("shot", None, "slab", None, None),
        P("shot", None, "slab", None, None),
        P("shot", None),
        P("shot", None),
        P(None, "slab", None),
        P(),
        P(),
        P(),
    )
    fits = mesh.shape["slab"] == 8 and mesh.shape["shot"] == 4

    def run(*args):
        line_inverse = args[6]
        blocks = fits and line_inverse.shape[0] == 2 and line_inverse.shape[2] == 2
        body = block_shards if blocks else general_shards
        return jax.shard_map(
            body, mesh=mesh, in_specs=placed, out_specs=P(None, "slab", "shot"), check_vma=False
        )(*args)

    return run
```

```python
from functools import partial

import jax
import jax.numpy as jnp
from jax import lax
from jax.experimental import pallas as pl
from jax.experimental.pallas import tpu as pltpu
from jax.sharding import PartitionSpec as P

NX = 1024
STEPS = 2


def pick_index(values, position, axis_number, keep=False):
    return lax.index_in_dim(values, position, axis_number, keepdims=keep)


def line_solve(wavefield, line_inverse, coupling, line_dim):
    in_shape = wavefield.shape
    freq_count = line_inverse.shape[0]
    blocks = line_inverse.shape[2]
    block_len = line_inverse.shape[3]
    real_blocks = line_inverse[:, 0]
    imag_blocks = line_inverse[:, 1]
    if line_dim == 5:
        pieces = wavefield.reshape(in_shape[:5] + (blocks, block_len))
        formula = "shfxcgj,fgij->shfxcgi"
    else:
        pieces = wavefield.reshape(in_shape[:3] + (blocks, block_len, in_shape[4] * in_shape[5]))
        formula = "shfgjz,fgij->shfgiz"
    with_real = jnp.einsum(formula, pieces, real_blocks, preferred_element_type=jnp.float32)
    with_imag = jnp.einsum(formula, pieces, imag_blocks, preferred_element_type=jnp.float32)
    if line_dim == 5:
        comp_axis, block_axis, cell_axis = (4, 4, 4)
        col_shape = (1, 1, freq_count, 1, block_len)
    else:
        with_real = with_real.reshape(in_shape[:3] + (blocks, block_len, in_shape[4], in_shape[5]))
        with_imag = with_imag.reshape(in_shape[:3] + (blocks, block_len, in_shape[4], in_shape[5]))
        comp_axis, block_axis, cell_axis = (5, 3, 3)
        col_shape = (1, 1, freq_count, block_len, 1)
    signs_six = jnp.array([1.0, -1.0], jnp.float32).reshape(1, 2, 1, 1, 1, 1)
    signs_five = jnp.array([1.0, -1.0], jnp.float32).reshape(1, 2, 1, 1, 1)
    u_real = pick_index(with_real, 0, comp_axis) - signs_six * pick_index(with_imag, 1, comp_axis)
    u_imag = pick_index(with_real, 1, comp_axis) + signs_six * pick_index(with_imag, 0, comp_axis)
    coup_real = coupling[:, 0].reshape(1, 1, freq_count, 1, 1)
    coup_imag = coupling[:, 1].reshape(1, 1, freq_count, 1, 1)

    def factor(block_index, column):
        col_real = line_inverse[:, 0, block_index, :, column].astype(jnp.float32).reshape(col_shape)
        col_imag = line_inverse[:, 1, block_index, :, column].astype(jnp.float32).reshape(col_shape)
        return (
            coup_real * col_real - coup_imag * col_imag,
            signs_five * (coup_imag * col_real + coup_real * col_imag),
        )

    fwd_real = [pick_index(u_real, 0, block_axis)]
    fwd_imag = [pick_index(u_imag, 0, block_axis)]
    block_index = 1
    mult_real, mult_imag = factor(block_index, 0)
    prev_real = pick_index(fwd_real[-1], block_len - 1, cell_axis, True)
    prev_imag = pick_index(fwd_imag[-1], block_len - 1, cell_axis, True)
    fwd_real.append(
        pick_index(u_real, block_index, block_axis) + mult_real * prev_real - mult_imag * prev_imag
    )
    fwd_imag.append(
        pick_index(u_imag, block_index, block_axis) + mult_real * prev_imag + mult_imag * prev_real
    )
    out_real = list(fwd_real)
    out_imag = list(fwd_imag)
    block_index = 0
    mult_real, mult_imag = factor(block_index, block_len - 1)
    next_real = pick_index(out_real[block_index + 1], 0, cell_axis, True)
    next_imag = pick_index(out_imag[block_index + 1], 0, cell_axis, True)
    out_real[block_index] = fwd_real[block_index] + mult_real * next_real - mult_imag * next_imag
    out_imag[block_index] = fwd_imag[block_index] + mult_real * next_imag + mult_imag * next_real
    real_line = jnp.stack(out_real, axis=block_axis).reshape(in_shape[:4] + (in_shape[5],))
    imag_line = jnp.stack(out_imag, axis=block_axis).reshape(in_shape[:4] + (in_shape[5],))
    return jnp.stack([real_line, imag_line], axis=4).astype(jnp.bfloat16)


def phase_shift(wavefield, slow_field, frequency):
    angles = frequency[:, None, None] * slow_field[None]
    cosine = jnp.cos(angles)[None, None]
    sine_part = jnp.sin(angles)[None, None]
    signs_five = jnp.array([1.0, -1.0], jnp.float32).reshape(1, 2, 1, 1, 1)
    real_part = wavefield[:, :, :, :, 0].astype(jnp.float32)
    imag_part = wavefield[:, :, :, :, 1].astype(jnp.float32)
    new_real = real_part * cosine - signs_five * imag_part * sine_part
    new_imag = imag_part * cosine + signs_five * real_part * sine_part
    return jnp.stack([new_real, new_imag], axis=4).astype(jnp.bfloat16)


def image_term(wavefield, row_cells, col_cells, shot_positions, frequency):
    source = wavefield[:, 0].astype(jnp.float32)
    receiver = wavefield[:, 1].astype(jnp.float32)
    cross = source[:, :, :, 0] * receiver[:, :, :, 1] - source[:, :, :, 1] * receiver[:, :, :, 0]
    weighted = jnp.sum(cross * frequency[None, :, None, None], axis=1)
    row_gap = row_cells[None, :, None] - shot_positions[:, 0][:, None, None]
    col_gap = col_cells[None, None, :] - shot_positions[:, 1][:, None, None]
    spread = (row_gap * row_gap + col_gap * col_gap).astype(jnp.float32)
    taper = 1.0 / (1.0 + spread * (16.0 / (NX * NX)))
    return jnp.sum(weighted * taper, axis=0)


def general_shards(
    source_field,
    residual_data,
    receiver_lines,
    shot_positions,
    slowness,
    frequency,
    line_inverse,
    coupling,
):
    row_count = source_field.shape[2]
    line_len = source_field.shape[4]
    receiver = residual_data * receiver_lines.astype(jnp.bfloat16)[:, None, None, None, :]
    wavefield = jnp.stack([source_field, receiver], axis=1)
    slab_start = lax.axis_index("slab") * row_count
    own_cells = slab_start + jnp.arange(row_count, dtype=jnp.int32)
    all_cells = jnp.arange(line_len, dtype=jnp.int32)
    solve_first = partial(line_solve, line_inverse=line_inverse, coupling=coupling, line_dim=3)
    solve_second = partial(line_solve, line_inverse=line_inverse, coupling=coupling, line_dim=5)

    def forward(fields):
        return solve_first(lax.all_to_all(fields, "slab", split_axis=5, concat_axis=3, tiled=True))

    def backward(fields):
        return lax.all_to_all(fields, "slab", split_axis=3, concat_axis=5, tiled=True)

    images = []
    for depth_index in range(STEPS):
        shifted = phase_shift(wavefield, slowness[depth_index], frequency)
        if depth_index % 2 == 0:
            wavefield = backward(forward(solve_second(shifted)))
        else:
            wavefield = solve_second(backward(forward(shifted)))
        local_image = image_term(wavefield, own_cells, all_cells, shot_positions, frequency)
        images.append(lax.psum_scatter(local_image, "shot", scatter_dimension=1, tiled=True))
    return jnp.stack(images)


F32 = jnp.float32
BF16 = jnp.bfloat16
SMEM = pltpu.SMEM
VMEM = pltpu.VMEM
OWN_MIB = 48
MIDDLE = 1.25


def params(mib):
    return pltpu.CompilerParams(vmem_limit_bytes=mib << 20)


def sincos(angle):
    turns = jnp.floor(angle * 0.15915494309189535 + 0.5)
    rest = (angle - turns * 6.28125) - turns * 1.9353071795864769e-3
    rest = rest * 0.25
    square = rest * rest
    sine = rest + rest * square * (
        -1.6666667e-1 + square * (8.3333333e-3 + square * (-1.9841270e-4 + square * 2.7557319e-6))
    )
    cosine = 1.0 + square * (
        -0.5 + square * (4.1666667e-2 + square * (-1.3888889e-3 + square * 2.4801587e-5))
    )
    sine, cosine = 2.0 * sine * cosine, 1.0 - 2.0 * sine * sine
    return 2.0 * sine * cosine, 1.0 - 2.0 * sine * sine


def dot_t(left, right):
    return lax.dot_general(left, right, (((1,), (1,)), ((), ())), preferred_element_type=F32)


def dot(left, right):
    return lax.dot_general(left, right, (((1,), (0,)), ((), ())), preferred_element_type=F32)


def dot_rows(left, right):
    return lax.dot_general(left, right, (((0,), (0,)), ((), ())), preferred_element_type=F32)


def rotate(omega, slow, real, imag, out):
    rows = slow.shape[0]
    sine, cosine = sincos(omega * slow)
    out[:rows] = (real * cosine - imag * sine).astype(BF16)
    out[rows:] = (imag * cosine + real * sine).astype(BF16)


def other_kernel(meta, freq, field, slowness, out, raw, slow, freq_out):
    f = meta[0] ^ 1
    raw[...] = field[0, meta[0]]
    slow[...] = slowness[0]
    for k in range(2):
        freq_out[k] = freq[k]
    rotate(freq[f], slowness[0], field[0, f, :, 0, :].astype(F32), field[0, f, :, 1, :].astype(F32), out)


def own_kernel(meta, freq, raw, slow, inverse, out, blocks, sem):
    fetch = pltpu.make_async_copy(inverse.at[meta[0]], blocks, sem)
    fetch.start()
    rotate(freq[meta[0]], slow[...], raw[:, 0, :].astype(F32), raw[:, 1, :].astype(F32), out)
    fetch.wait()


def source_kernel(meta, freq, coupling, own, core, blocks, same, cross, ends, scalars):
    for k in range(2):
        scalars[k] = freq[k]
        scalars[2 + 2 * k] = coupling[k, 0]
        scalars[3 + 2 * k] = coupling[k, 1]
    slab_kernel(meta, scalars, own, core, blocks, same, cross, ends)


def away_kernel(meta, residual, out):
    out[...] = residual[0, 1 - meta[0]]


def edge_rows(meta, blocks, block, lanes):
    start = pl.multiple_of((1 - block) * (blocks.shape[2] - 16), 16)
    return jnp.concatenate([blocks[part, block, pl.ds(start, 16), lanes] for part in range(2)], axis=0)


def pick_edge(block, values):
    first = block == 0
    return jnp.where(first, values[15:16], values[0:1]), jnp.where(first, values[31:32], values[16:17])


def edge_product(block, real, imag):
    rr, ir = pick_edge(block, real)
    ri, ii = pick_edge(block, imag)
    return rr - ii, ri + ir


def slab_kernel(meta, scalars, own, core, blocks, same, cross, ends):
    rows = own.shape[0] // 2
    half = blocks.shape[2]
    f, zz = meta[0], meta[1]
    cr, ci = scalars[2 + 2 * f], scalars[3 + 2 * f]
    spot = lax.broadcasted_iota(jnp.int32, (16, half), 1)
    line = lax.broadcasted_iota(jnp.int32, (16, half), 0)
    solved, columns = [], []
    for k in range(2):
        cells = slice(k * half, (k + 1) * half)
        hot = jnp.where((spot == (half - 1 if k == 0 else 0)) & (line == 0), 1.0, 0.0).astype(BF16)
        left = jnp.concatenate(
            [own[:rows, cells], core[:rows, cells], own[rows:, cells], core[rows:, cells], hot], axis=0
        )
        by_real = dot_t(left, blocks[0, k])
        by_imag = dot_t(left, blocks[1, k])
        n = 2 * rows
        solved.append((by_real[:n] - by_imag[n : 2 * n], by_real[n : 2 * n] + by_imag[:n]))
        ar, ai = by_real[2 * n : 2 * n + 1], by_imag[2 * n : 2 * n + 1]
        columns.append((cr * ar - ci * ai, cr * ai + ci * ar))
        ends[2 * k : 2 * k + 1] = columns[k][0]
        ends[2 * k + 1 : 2 * k + 2] = columns[k][1]

    def couple(k, er, ei):
        qr, qi = columns[k]
        return solved[k][0] + er * qr - ei * qi, solved[k][1] + er * qi + ei * qr

    upper = couple(1, solved[0][0][:, half - 1 :], solved[0][1][:, half - 1 :])
    lower = couple(0, upper[0][:, 0:1], upper[1][:, 0:1])
    first = zz == 0
    for part in range(2):
        low, high = lower[part].astype(BF16), upper[part].astype(BF16)
        mine, away = jnp.where(first, low, high), jnp.where(first, high, low)
        for n in range(2):
            at = slice((2 * n + part) * rows, (2 * n + part + 1) * rows)
            same[at] = mine[n * rows : (n + 1) * rows]
            cross[at] = away[n * rows : (n + 1) * rows]


def edge_kernel(meta, blocks, same0, cross0, same1, cross1, edge_same, edge_cross):
    rows = same0.shape[0] // 4
    xb, local = meta[2], meta[3]
    for refs, out in (((same0, same1), edge_same), ((cross0, cross1), edge_cross)):
        for part in range(2):
            total = 0.0
            for n in range(2):
                lanes = pl.ds(pl.multiple_of((local ^ n) * rows, rows), rows)
                row = edge_rows(meta, blocks, xb, lanes)
                at = slice((2 * n + part) * rows, (2 * n + part + 1) * rows)
                total = total + dot(row, jnp.concatenate([ref[at] for ref in refs], axis=1))
            if part == 0:
                real = total
        er, ei = edge_product(xb, real, total)
        half = same0.shape[1]
        for k in range(2):
            out[2 * k : 2 * k + 1] = er[:, k * half : (k + 1) * half]
            out[2 * k + 1 : 2 * k + 2] = ei[:, k * half : (k + 1) * half]


def receiver_kernel(
    meta, scalars, mask, field, core_raw, slow, core_slow, blocks, same0, cross0, same, cross, edge_same, edge_cross, own, core, ends
):
    keep = mask[...].astype(F32)
    f = meta[0]
    for raw, slowness, out in ((field.at[0, f], slow, own), (core_raw, core_slow, core)):
        rotate(
            scalars[f], slowness[...], raw[:, 0, :].astype(F32) * keep, -(raw[:, 1, :].astype(F32) * keep), out
        )
    slab_kernel(meta, scalars, own, core, blocks, same, cross, ends)
    edge_kernel(meta, blocks, same0, cross0, same, cross, edge_same, edge_cross)


def phase_kernel(meta, scalars, place, own, core, far, far_core, sine, cosine, weight):
    rows, half = own.shape
    omega = scalars[meta[0]]
    for k, piece in enumerate((own, core, far, far_core)):
        start = pl.multiple_of((meta[3] ^ k) * rows, rows)
        s, c = sincos(omega * (piece[...].astype(F32) + MIDDLE))
        sine[pl.ds(start, rows)] = s
        cosine[pl.ds(start, rows)] = c
    row = lax.broadcasted_iota(jnp.int32, (weight.shape[0], half), 0) + meta[2] * half - place[0, 0]
    col = lax.broadcasted_iota(jnp.int32, (weight.shape[0], half), 1) + meta[1] * half - place[0, 1]
    spread = (row * row + col * col).astype(F32)
    weight[...] = -omega / (1.0 + spread * (16.0 / (NX * NX)))


def turn_value(meta, scalars, blocks, block):
    cr, ci = scalars[2 + 2 * meta[0]], scalars[3 + 2 * meta[0]]
    ar = blocks[0, 1, 0:16, 0:128].astype(F32)[0:1, 0:1]
    ai = blocks[1, 1, 0:16, 0:128].astype(F32)[0:1, 0:1]
    first = block == 0
    return jnp.where(first, cr * ar - ci * ai, 0.0), jnp.where(first, cr * ai + ci * ar, 0.0)


def column_kernel(
    meta, scalars, near, far, blocks, edge_same, edge_cross, sine, cosine, solved, shifted, own_edge, real, imag
):
    rows = near.shape[0] // 4
    half = near.shape[1]
    xb = meta[2]
    for k, (piece, n) in enumerate(((near, 0), (near, 1), (far, 0), (far, 1))):
        start = pl.multiple_of((meta[3] ^ k) * rows, rows)
        real[pl.ds(start, rows)] = piece[2 * n * rows : (2 * n + 1) * rows]
        imag[pl.ds(start, rows)] = piece[(2 * n + 1) * rows : (2 * n + 2) * rows]
    cr, ci = scalars[2 + 2 * meta[0]], scalars[3 + 2 * meta[0]]
    ar, ai = turn_value(meta, scalars, blocks, xb)
    row = edge_rows(meta, blocks, xb, slice(0, half))
    own_real, own_imag = edge_product(xb, dot(row, real[...]), dot(row, imag[...]))
    hr = edge_same[0:1] + edge_cross[0:1] + ar * own_real - ai * own_imag
    hi = edge_same[1:2] + edge_cross[1:2] + ar * own_imag + ai * own_real
    add_real = cr * hr - ci * hi
    add_imag = cr * hi + ci * hr
    upper = xb == 1
    low = lax.broadcasted_iota(jnp.int32, (16, half), 0) == 0
    high = lax.broadcasted_iota(jnp.int32, (16, half), 0) == 15
    for ref, add in ((real, add_real), (imag, add_imag)):
        ref[0:16] = (ref[0:16].astype(F32) + jnp.where(low & upper, add, 0.0)).astype(BF16)
        ref[half - 16 :] = (
            ref[half - 16 :].astype(F32) + jnp.where(high & jnp.logical_not(upper), add, 0.0)
        ).astype(BF16)
    left = jnp.concatenate([blocks[0, xb], blocks[1, xb]], axis=0)
    for n in range(0, half, 256):
        cols = slice(n, n + 256)
        by_real = dot(left, real[:, cols])
        by_imag = dot(left, imag[:, cols])
        xr = (by_real[:half] - by_imag[half:]).astype(BF16)
        xi = (by_imag[:half] + by_real[half:]).astype(BF16)
        solved[:half, cols] = xr
        solved[half:, cols] = xi
        xr, xi = xr.astype(F32), xi.astype(F32)
        s, c = sine[:, cols], cosine[:, cols]
        shifted[:half, cols] = (xr * c - xi * s).astype(BF16)
        shifted[half:, cols] = (xi * c + xr * s).astype(BF16)
    own_real, own_imag = edge_product(xb, dot(row, shifted[:half]), dot(row, shifted[half:]))
    own_edge[0:1] = own_real
    own_edge[1:2] = own_imag


def both_kernel(meta, shifted, blocks, solved, edge):
    half = shifted.shape[1]
    xb, zz = meta[2], meta[1]
    left = jnp.concatenate([blocks[0, xb], blocks[1, xb]], axis=0)
    by_real = dot(left, shifted[:half])
    by_imag = dot(left, shifted[half:])
    u = jnp.concatenate(
        [(by_real[:half] - by_imag[half:]).astype(BF16), (by_imag[:half] + by_real[half:]).astype(BF16)], axis=0
    )
    row = dot_t(edge_rows(meta, blocks, zz, slice(0, half)), u)
    edge_real, edge_imag = edge_product(zz, row[:, :half], row[:, half:])
    edge[0:1] = edge_real
    edge[1:2] = edge_imag
    by_real = dot_t(u, blocks[0, zz])
    by_imag = dot_t(u, blocks[1, zz])
    solved[:half] = (by_real[:half] - by_imag[half:]).astype(BF16)
    solved[half:] = (by_real[half:] + by_imag[:half]).astype(BF16)


def image_pieces(meta, image, keep, send):
    rows, cols = keep.shape[1:]
    for kz in range(2):
        for kx in range(2):
            col = pl.multiple_of((meta[5] ^ kx) * cols, cols)
            for other, ref in ((0, keep), (1, send)):
                row = pl.multiple_of(((meta[4] ^ kz) * 2 + (meta[0] ^ other)) * rows, rows)
                ref[kz * 2 + kx] = image[pl.ds(row, rows), pl.ds(col, cols)].astype(BF16)


def pick_end(ends, block):
    first = block == 0
    return jnp.where(first, ends[0:1], ends[2:3]), jnp.where(first, ends[1:2], ends[3:4])


def turn_kernel(meta, scalars, edge_x, near_x, edge_y0, edge_y1, ends, blocks, whole, edge):
    ar, ai = turn_value(meta, scalars, blocks, meta[2])
    zz = meta[1]
    yr, yi = pick_edge(zz, edge_rows(meta, blocks, zz, slice(0, ends.shape[1])).astype(F32))
    pr, pi = pick_end(ends, meta[2])
    for n in range(2):
        r, i = slice(2 * n, 2 * n + 1), slice(2 * n + 1, 2 * n + 2)
        hr = near_x[r] + ar * edge_x[r] - ai * edge_x[i]
        hi = near_x[i] + ar * edge_x[i] + ai * edge_x[r]
        whole[r] = hr
        whole[i] = hi
        sr = jnp.sum(hr * yr - hi * yi, axis=1, keepdims=True)
        si = jnp.sum(hr * yi + hi * yr, axis=1, keepdims=True)
        edge_y = (edge_y0, edge_y1)[n]
        edge[r] = edge_y[0:1] + sr * pr - si * pi
        edge[i] = edge_y[1:2] + sr * pi + si * pr


def split(value):
    high = value.astype(BF16)
    return high.astype(F32), (value - high.astype(F32))


def between_kernel(meta, whole, blocks, source, receiver, weight, out, keep, send, image):
    high, low = split(whole[...])
    left = jnp.concatenate([high, low, high, low], axis=0).astype(BF16)
    by_real = dot_t(left, blocks[0, meta[1]])
    by_imag = dot_t(left, blocks[1, meta[1]])
    by_real = by_real[0:4] + by_real[4:8]
    by_imag = by_imag[0:4] + by_imag[4:8]
    for n in range(2):
        r, i = slice(2 * n, 2 * n + 1), slice(2 * n + 1, 2 * n + 2)
        out[r] = by_real[r] - by_imag[i]
        out[i] = by_real[i] + by_imag[r]
    half = source.shape[1]
    sr, si = source[:half].astype(F32), source[half:].astype(F32)
    rr, ri = receiver[:half].astype(F32), receiver[half:].astype(F32)
    image[...] = (sr * ri + si * rr) * weight[...]
    image_pieces(meta, image, keep, send)


def second_image_kernel(
    meta, scalars, source, receiver, weight, rows_y, edge, near, ends, blocks, keep, send, image
):
    half = source.shape[1]
    ar, ai = turn_value(meta, scalars, blocks, meta[1])
    pr, pi = pick_end(ends, meta[2])
    qr, qi = pick_end(ends, meta[1])

    def triple(value, order):
        high, low = split(value)
        return [high, high, low] if order == 0 else [high, low, high]

    fields = []
    for n, ref in enumerate((source, receiver)):
        r, i = slice(2 * n, 2 * n + 1), slice(2 * n + 1, 2 * n + 2)
        gr = near[r] + ar * edge[r] - ai * edge[i]
        gi = near[i] + ar * edge[i] + ai * edge[r]
        tr, ti = rows_y[r], rows_y[i]
        left, right_real, right_imag = [], [], []
        for a, b, c in ((pr, tr, ti), (pi, -ti, tr), (gr, qr, qi), (gi, -qi, qr)):
            left += triple(a, 0)
            right_real += triple(b, 1)
            right_imag += triple(c, 1)
        pad = [jnp.zeros((4, half), F32)]
        left = jnp.concatenate(left + pad, axis=0).astype(BF16)
        right_real = jnp.concatenate(right_real + pad, axis=0).astype(BF16)
        right_imag = jnp.concatenate(right_imag + pad, axis=0).astype(BF16)
        fields.append(
            (
                ref[:half].astype(F32) + dot_rows(left, right_real),
                ref[half:].astype(F32) + dot_rows(left, right_imag),
            )
        )
    (sr, si), (rr, ri) = fields
    image[...] = (sr * ri + si * rr) * weight[...]
    image_pieces(meta, image, keep, send)


def block_shards(
    source_field, residual_data, receiver_lines, shot_positions, slowness, frequency, line_inverse, coupling
):
    rows, length = slowness.shape[1:]
    half = line_inverse.shape[-1]
    slab = lax.axis_index("slab")
    shot = lax.axis_index("shot")
    meta = jnp.stack(
        [slab & 1, (slab >> 1) & 1, slab >> 2, slab & 3, shot >> 1, shot & 1]
    ).astype(jnp.int32)
    smem = pl.BlockSpec(memory_space=SMEM)
    vmem = pl.BlockSpec(memory_space=VMEM)
    hbm = pl.BlockSpec(memory_space=pltpu.HBM)

    def shape(dtype, *sizes):
        return jax.ShapeDtypeStruct(sizes, dtype)

    def call(body, name, specs, outs, scratch, mib, *args):
        return pl.pallas_call(
            body,
            in_specs=specs,
            out_specs=[vmem] * len(outs),
            out_shape=outs,
            scratch_shapes=scratch,
            compiler_params=params(mib),
            name=name,
        )(*args)

    def move(array, k):
        return lax.ppermute(array, "slab", [(i, i ^ k) for i in range(8)])

    cut = shape(BF16, 2 * rows, length)
    block_shape = shape(BF16, *line_inverse.shape[1:])
    core, raw, slow, freq = pl.pallas_call(
        other_kernel,
        in_specs=[smem, smem, vmem, vmem],
        out_specs=[vmem] * 3 + [smem],
        out_shape=[cut, shape(BF16, rows, 2, length), shape(F32, rows, length), shape(F32, 2)],
        compiler_params=params(12),
        name="other",
    )(meta, frequency, source_field, slowness)
    own, blocks = pl.pallas_call(
        own_kernel,
        in_specs=[smem, smem, vmem, vmem, hbm],
        out_specs=[vmem, vmem],
        out_shape=[cut, block_shape],
        scratch_shapes=[pltpu.SemaphoreType.DMA],
        compiler_params=params(OWN_MIB),
        name="own",
    )(meta, freq, raw, slow, line_inverse)
    core = move(core, 1)
    block_piece = shape(BF16, 4 * rows, half)
    same0, cross0, ends, scalars = pl.pallas_call(
        source_kernel,
        in_specs=[smem] * 3 + [vmem] * 3,
        out_specs=[vmem] * 3 + [smem],
        out_shape=[block_piece] * 2 + [shape(F32, 4, half), shape(F32, 6)],
        compiler_params=params(16),
        name="slab",
    )(meta, freq, coupling, own, core, blocks)
    far = [move(cross0, 2)]
    residual, same0, slow0 = lax.optimization_barrier((residual_data, same0, slow))
    (away,) = call(
        away_kernel, "away", [smem, vmem], [shape(BF16, rows, 2, length)], [], 12, meta, residual
    )
    core_raw = move(away, 1)
    core_slow0 = move(slow0, 1)
    layer, same0 = lax.optimization_barrier((slowness[1], same0))
    layer = (layer - MIDDLE).astype(jnp.float16)
    low, high = layer[:, :half], layer[:, half:]
    first = meta[1] == 0
    own_slow = jnp.where(first, low, high)
    far_slow = move(jnp.where(first, high, low), 2)
    same1, cross, *edges = call(
        receiver_kernel,
        "receiver",
        [smem, smem] + [vmem] * 8,
        [block_piece] * 2 + [shape(F32, 4, half)] * 2,
        [VMEM((2 * rows, length), BF16)] * 2 + [VMEM((4, half), F32)],
        20,
        meta,
        scalars,
        receiver_lines,
        residual_data,
        core_raw,
        slow,
        core_slow0,
        blocks,
        same0,
        cross0,
    )
    same = [same0, same1]
    edge_same = move(edges[0], 4)
    edge_cross = move(edges[1], 6)
    cross, far[0] = lax.optimization_barrier((cross, far[0]))
    far.append(move(cross, 2))
    pair = shape(BF16, 2 * half, half)
    line = shape(F32, 2, half)
    four = shape(F32, 4, half)
    far_slow, edge_same, edge_cross = lax.optimization_barrier((far_slow, edge_same, edge_cross))
    core_slow = move(jnp.stack([own_slow, far_slow]), 1)
    block = shape(F32, half, half)
    sine, cosine, weight = call(
        phase_kernel,
        "phase",
        [smem] * 3 + [vmem] * 4,
        [block] * 3,
        [],
        8,
        meta,
        scalars,
        shot_positions,
        own_slow.astype(F32),
        core_slow[0].astype(F32),
        far_slow.astype(F32),
        core_slow[1].astype(F32),
    )
    solved, finals, edge_x, edge_y = [], [], [], []
    for n in range(2):
        if n == 1:
            same[1], finals[0] = lax.optimization_barrier((same[1], finals[0]))
        x0, turned, edge = call(
            column_kernel,
            "column",
            [smem, smem] + [vmem] * 7,
            [pair, pair, line],
            [VMEM((half, half), BF16)] * 2,
            16,
            meta,
            scalars,
            same[n],
            far[n],
            blocks,
            edge_same[2 * n : 2 * n + 2],
            edge_cross[2 * n : 2 * n + 2],
            sine,
            cosine,
        )
        v, across = call(both_kernel, "both", [smem] + [vmem] * 2, [pair, line], [], 20, meta, turned, blocks)
        solved.append(x0)
        finals.append(v)
        edge_x.append(edge)
        edge_y.append(across)
    edge_x = jnp.concatenate(edge_x)
    near_x = move(edge_x, 4)
    coupled, edge = call(
        turn_kernel,
        "turn",
        [smem, smem] + [vmem] * 6,
        [four, four],
        [],
        4,
        meta,
        scalars,
        edge_x,
        near_x,
        *edge_y,
        ends,
        blocks,
    )
    near_y = move(edge, 2)
    cut = shape(BF16, 4, rows, half // 2)
    scratch = [VMEM((half, half), F32)]
    rows_y, keep0, send0 = call(
        between_kernel,
        "between",
        [smem] + [vmem] * 5,
        [four, cut, cut],
        scratch,
        12,
        meta,
        coupled,
        blocks,
        solved[0],
        solved[1],
        weight,
    )
    near_y, rows_y, send0 = lax.optimization_barrier((near_y, rows_y, send0))
    keep1, send1 = call(
        second_image_kernel,
        "second_image",
        [smem] * 2 + [vmem] * 8,
        [cut] * 2,
        scratch,
        12,
        meta,
        scalars,
        finals[0],
        finals[1],
        weight,
        rows_y,
        edge,
        near_y,
        ends,
        blocks,
    )
    part0 = keep0.astype(F32) + move(send0, 1).astype(F32)
    part1 = keep1.astype(F32) + move(send1, 1).astype(F32)
    both = jnp.stack([part0, part1], axis=1).astype(BF16)
    total = 0.0
    for kz in (1, 0):
        for kx in (1, 0):
            route = []
            for s in range(4):
                for b in range(8):
                    sy, sx, bx, bc = s // 2, s % 2, b // 4, b % 2
                    by = (b // 2) % 2
                    target = (by * 2 + (sx ^ kx)) * 8 + bx * 4 + (sy ^ kz) * 2 + bc
                    route.append((s * 8 + b, target))
            total = total + lax.ppermute(both[kz * 2 + kx], ("shot", "slab"), route).astype(F32)
    return total


def solution(mesh):
    placed = (
        P("shot", None, "slab", None, None),
        P("shot", None, "slab", None, None),
        P("shot", None),
        P("shot", None),
        P(None, "slab", None),
        P(),
        P(),
        P(),
    )
    fits = mesh.shape["slab"] == 8 and mesh.shape["shot"] == 4

    def run(*args):
        line_inverse = args[6]
        blocks = fits and line_inverse.shape[0] == 2 and line_inverse.shape[2] == 2
        body = block_shards if blocks else general_shards
        return jax.shard_map(
            body, mesh=mesh, in_specs=placed, out_specs=P(None, "slab", "shot"), check_vma=False
        )(*args)

    return run
```

```python
from functools import partial

import jax
import jax.numpy as jnp
from jax import lax
from jax.experimental import pallas as pl
from jax.experimental.pallas import tpu as pltpu
from jax.sharding import PartitionSpec as P

NX = 1024
STEPS = 2


def pick_index(values, position, axis_number, keep=False):
    return lax.index_in_dim(values, position, axis_number, keepdims=keep)


def line_solve(wavefield, line_inverse, coupling, line_dim):
    in_shape = wavefield.shape
    freq_count = line_inverse.shape[0]
    blocks = line_inverse.shape[2]
    block_len = line_inverse.shape[3]
    real_blocks = line_inverse[:, 0]
    imag_blocks = line_inverse[:, 1]
    if line_dim == 5:
        pieces = wavefield.reshape(in_shape[:5] + (blocks, block_len))
        formula = "shfxcgj,fgij->shfxcgi"
    else:
        pieces = wavefield.reshape(in_shape[:3] + (blocks, block_len, in_shape[4] * in_shape[5]))
        formula = "shfgjz,fgij->shfgiz"
    with_real = jnp.einsum(formula, pieces, real_blocks, preferred_element_type=jnp.float32)
    with_imag = jnp.einsum(formula, pieces, imag_blocks, preferred_element_type=jnp.float32)
    if line_dim == 5:
        comp_axis, block_axis, cell_axis = (4, 4, 4)
        col_shape = (1, 1, freq_count, 1, block_len)
    else:
        with_real = with_real.reshape(in_shape[:3] + (blocks, block_len, in_shape[4], in_shape[5]))
        with_imag = with_imag.reshape(in_shape[:3] + (blocks, block_len, in_shape[4], in_shape[5]))
        comp_axis, block_axis, cell_axis = (5, 3, 3)
        col_shape = (1, 1, freq_count, block_len, 1)
    signs_six = jnp.array([1.0, -1.0], jnp.float32).reshape(1, 2, 1, 1, 1, 1)
    signs_five = jnp.array([1.0, -1.0], jnp.float32).reshape(1, 2, 1, 1, 1)
    u_real = pick_index(with_real, 0, comp_axis) - signs_six * pick_index(with_imag, 1, comp_axis)
    u_imag = pick_index(with_real, 1, comp_axis) + signs_six * pick_index(with_imag, 0, comp_axis)
    coup_real = coupling[:, 0].reshape(1, 1, freq_count, 1, 1)
    coup_imag = coupling[:, 1].reshape(1, 1, freq_count, 1, 1)

    def factor(block_index, column):
        col_real = line_inverse[:, 0, block_index, :, column].astype(jnp.float32).reshape(col_shape)
        col_imag = line_inverse[:, 1, block_index, :, column].astype(jnp.float32).reshape(col_shape)
        return (
            coup_real * col_real - coup_imag * col_imag,
            signs_five * (coup_imag * col_real + coup_real * col_imag),
        )

    fwd_real = [pick_index(u_real, 0, block_axis)]
    fwd_imag = [pick_index(u_imag, 0, block_axis)]
    block_index = 1
    mult_real, mult_imag = factor(block_index, 0)
    prev_real = pick_index(fwd_real[-1], block_len - 1, cell_axis, True)
    prev_imag = pick_index(fwd_imag[-1], block_len - 1, cell_axis, True)
    fwd_real.append(
        pick_index(u_real, block_index, block_axis) + mult_real * prev_real - mult_imag * prev_imag
    )
    fwd_imag.append(
        pick_index(u_imag, block_index, block_axis) + mult_real * prev_imag + mult_imag * prev_real
    )
    out_real = list(fwd_real)
    out_imag = list(fwd_imag)
    block_index = 0
    mult_real, mult_imag = factor(block_index, block_len - 1)
    next_real = pick_index(out_real[block_index + 1], 0, cell_axis, True)
    next_imag = pick_index(out_imag[block_index + 1], 0, cell_axis, True)
    out_real[block_index] = fwd_real[block_index] + mult_real * next_real - mult_imag * next_imag
    out_imag[block_index] = fwd_imag[block_index] + mult_real * next_imag + mult_imag * next_real
    real_line = jnp.stack(out_real, axis=block_axis).reshape(in_shape[:4] + (in_shape[5],))
    imag_line = jnp.stack(out_imag, axis=block_axis).reshape(in_shape[:4] + (in_shape[5],))
    return jnp.stack([real_line, imag_line], axis=4).astype(jnp.bfloat16)


def phase_shift(wavefield, slow_field, frequency):
    angles = frequency[:, None, None] * slow_field[None]
    cosine = jnp.cos(angles)[None, None]
    sine_part = jnp.sin(angles)[None, None]
    signs_five = jnp.array([1.0, -1.0], jnp.float32).reshape(1, 2, 1, 1, 1)
    real_part = wavefield[:, :, :, :, 0].astype(jnp.float32)
    imag_part = wavefield[:, :, :, :, 1].astype(jnp.float32)
    new_real = real_part * cosine - signs_five * imag_part * sine_part
    new_imag = imag_part * cosine + signs_five * real_part * sine_part
    return jnp.stack([new_real, new_imag], axis=4).astype(jnp.bfloat16)


def image_term(wavefield, row_cells, col_cells, shot_positions, frequency):
    source = wavefield[:, 0].astype(jnp.float32)
    receiver = wavefield[:, 1].astype(jnp.float32)
    cross = source[:, :, :, 0] * receiver[:, :, :, 1] - source[:, :, :, 1] * receiver[:, :, :, 0]
    weighted = jnp.sum(cross * frequency[None, :, None, None], axis=1)
    row_gap = row_cells[None, :, None] - shot_positions[:, 0][:, None, None]
    col_gap = col_cells[None, None, :] - shot_positions[:, 1][:, None, None]
    spread = (row_gap * row_gap + col_gap * col_gap).astype(jnp.float32)
    taper = 1.0 / (1.0 + spread * (16.0 / (NX * NX)))
    return jnp.sum(weighted * taper, axis=0)


def general_shards(
    source_field,
    residual_data,
    receiver_lines,
    shot_positions,
    slowness,
    frequency,
    line_inverse,
    coupling,
):
    row_count = source_field.shape[2]
    line_len = source_field.shape[4]
    receiver = residual_data * receiver_lines.astype(jnp.bfloat16)[:, None, None, None, :]
    wavefield = jnp.stack([source_field, receiver], axis=1)
    slab_start = lax.axis_index("slab") * row_count
    own_cells = slab_start + jnp.arange(row_count, dtype=jnp.int32)
    all_cells = jnp.arange(line_len, dtype=jnp.int32)
    solve_first = partial(line_solve, line_inverse=line_inverse, coupling=coupling, line_dim=3)
    solve_second = partial(line_solve, line_inverse=line_inverse, coupling=coupling, line_dim=5)

    def forward(fields):
        return solve_first(lax.all_to_all(fields, "slab", split_axis=5, concat_axis=3, tiled=True))

    def backward(fields):
        return lax.all_to_all(fields, "slab", split_axis=3, concat_axis=5, tiled=True)

    images = []
    for depth_index in range(STEPS):
        shifted = phase_shift(wavefield, slowness[depth_index], frequency)
        if depth_index % 2 == 0:
            wavefield = backward(forward(solve_second(shifted)))
        else:
            wavefield = solve_second(backward(forward(shifted)))
        local_image = image_term(wavefield, own_cells, all_cells, shot_positions, frequency)
        images.append(lax.psum_scatter(local_image, "shot", scatter_dimension=1, tiled=True))
    return jnp.stack(images)


F32 = jnp.float32
BF16 = jnp.bfloat16
SMEM = pltpu.SMEM
VMEM = pltpu.VMEM
OWN_MIB = 48
MIDDLE = 1.25


def params(mib):
    return pltpu.CompilerParams(vmem_limit_bytes=mib << 20)


def sincos(angle):
    turns = jnp.floor(angle * 0.15915494309189535 + 0.5)
    rest = (angle - turns * 6.28125) - turns * 1.9353071795864769e-3
    rest = rest * 0.25
    square = rest * rest
    sine = rest + rest * square * (
        -1.6666667e-1 + square * (8.3333333e-3 + square * (-1.9841270e-4 + square * 2.7557319e-6))
    )
    cosine = 1.0 + square * (
        -0.5 + square * (4.1666667e-2 + square * (-1.3888889e-3 + square * 2.4801587e-5))
    )
    sine, cosine = 2.0 * sine * cosine, 1.0 - 2.0 * sine * sine
    return 2.0 * sine * cosine, 1.0 - 2.0 * sine * sine


def dot_t(left, right):
    return lax.dot_general(left, right, (((1,), (1,)), ((), ())), preferred_element_type=F32)


def dot(left, right):
    return lax.dot_general(left, right, (((1,), (0,)), ((), ())), preferred_element_type=F32)


def dot_rows(left, right):
    return lax.dot_general(left, right, (((0,), (0,)), ((), ())), preferred_element_type=F32)


def rotate(omega, slow, real, imag, out):
    rows = slow.shape[0]
    sine, cosine = sincos(omega * slow)
    out[:rows] = (real * cosine - imag * sine).astype(BF16)
    out[rows:] = (imag * cosine + real * sine).astype(BF16)


def other_kernel(meta, freq, field, slowness, out, raw, slow, freq_out):
    f = meta[0] ^ 1
    raw[...] = field[0, meta[0]]
    slow[...] = slowness[0]
    for k in range(2):
        freq_out[k] = freq[k]
    rotate(freq[f], slowness[0], field[0, f, :, 0, :].astype(F32), field[0, f, :, 1, :].astype(F32), out)


def own_kernel(meta, freq, raw, slow, inverse, out, blocks, sem):
    fetch = pltpu.make_async_copy(inverse.at[meta[0]], blocks, sem)
    fetch.start()
    rotate(freq[meta[0]], slow[...], raw[:, 0, :].astype(F32), raw[:, 1, :].astype(F32), out)
    fetch.wait()


def source_kernel(meta, freq, coupling, own, core, blocks, same, cross, ends, scalars):
    for k in range(2):
        scalars[k] = freq[k]
        scalars[2 + 2 * k] = coupling[k, 0]
        scalars[3 + 2 * k] = coupling[k, 1]
    slab_kernel(meta, scalars, own, core, blocks, same, cross, ends)


def away_kernel(meta, residual, out):
    out[...] = residual[0, 1 - meta[0]]


def edge_rows(meta, blocks, block, lanes):
    start = pl.multiple_of((1 - block) * (blocks.shape[2] - 16), 16)
    return jnp.concatenate([blocks[part, block, pl.ds(start, 16), lanes] for part in range(2)], axis=0)


def pick_edge(block, values):
    first = block == 0
    return jnp.where(first, values[15:16], values[0:1]), jnp.where(first, values[31:32], values[16:17])


def edge_product(block, real, imag):
    rr, ir = pick_edge(block, real)
    ri, ii = pick_edge(block, imag)
    return rr - ii, ri + ir


def slab_kernel(meta, scalars, own, core, blocks, same, cross, ends):
    rows = own.shape[0] // 2
    half = blocks.shape[2]
    f, zz = meta[0], meta[1]
    cr, ci = scalars[2 + 2 * f], scalars[3 + 2 * f]
    spot = lax.broadcasted_iota(jnp.int32, (16, half), 1)
    line = lax.broadcasted_iota(jnp.int32, (16, half), 0)
    solved, columns = [], []
    for k in range(2):
        cells = slice(k * half, (k + 1) * half)
        hot = jnp.where((spot == (half - 1 if k == 0 else 0)) & (line == 0), 1.0, 0.0).astype(BF16)
        left = jnp.concatenate(
            [own[:rows, cells], core[:rows, cells], own[rows:, cells], core[rows:, cells], hot], axis=0
        )
        by_real = dot_t(left, blocks[0, k])
        by_imag = dot_t(left, blocks[1, k])
        n = 2 * rows
        solved.append((by_real[:n] - by_imag[n : 2 * n], by_real[n : 2 * n] + by_imag[:n]))
        ar, ai = by_real[2 * n : 2 * n + 1], by_imag[2 * n : 2 * n + 1]
        columns.append((cr * ar - ci * ai, cr * ai + ci * ar))
        ends[2 * k : 2 * k + 1] = columns[k][0]
        ends[2 * k + 1 : 2 * k + 2] = columns[k][1]

    def couple(k, er, ei):
        qr, qi = columns[k]
        return solved[k][0] + er * qr - ei * qi, solved[k][1] + er * qi + ei * qr

    upper = couple(1, solved[0][0][:, half - 1 :], solved[0][1][:, half - 1 :])
    lower = couple(0, upper[0][:, 0:1], upper[1][:, 0:1])
    first = zz == 0
    for part in range(2):
        low, high = lower[part].astype(BF16), upper[part].astype(BF16)
        mine, away = jnp.where(first, low, high), jnp.where(first, high, low)
        for n in range(2):
            at = slice((2 * n + part) * rows, (2 * n + part + 1) * rows)
            same[at] = mine[n * rows : (n + 1) * rows]
            cross[at] = away[n * rows : (n + 1) * rows]


def edge_kernel(meta, blocks, same0, cross0, same1, cross1, edge_same, edge_cross):
    rows = same0.shape[0] // 4
    xb, local = meta[2], meta[3]
    for refs, out in (((same0, same1), edge_same), ((cross0, cross1), edge_cross)):
        for part in range(2):
            total = 0.0
            for n in range(2):
                lanes = pl.ds(pl.multiple_of((local ^ n) * rows, rows), rows)
                row = edge_rows(meta, blocks, xb, lanes)
                at = slice((2 * n + part) * rows, (2 * n + part + 1) * rows)
                total = total + dot(row, jnp.concatenate([ref[at] for ref in refs], axis=1))
            if part == 0:
                real = total
        er, ei = edge_product(xb, real, total)
        half = same0.shape[1]
        for k in range(2):
            out[2 * k : 2 * k + 1] = er[:, k * half : (k + 1) * half]
            out[2 * k + 1 : 2 * k + 2] = ei[:, k * half : (k + 1) * half]


def receiver_kernel(
    meta, scalars, mask, field, core_raw, slow, core_slow, blocks, same0, cross0, same, cross, edge_same, edge_cross, own, core, ends
):
    keep = mask[...].astype(F32)
    f = meta[0]
    for raw, slowness, out in ((field.at[0, f], slow, own), (core_raw, core_slow, core)):
        rotate(
            scalars[f], slowness[...], raw[:, 0, :].astype(F32) * keep, -(raw[:, 1, :].astype(F32) * keep), out
        )
    slab_kernel(meta, scalars, own, core, blocks, same, cross, ends)
    edge_kernel(meta, blocks, same0, cross0, same, cross, edge_same, edge_cross)


def phase_kernel(meta, scalars, place, own, core, far, far_core, sine, cosine, weight):
    rows, half = own.shape
    omega = scalars[meta[0]]
    for k, piece in enumerate((own, core, far, far_core)):
        start = pl.multiple_of((meta[3] ^ k) * rows, rows)
        s, c = sincos(omega * (piece[...].astype(F32) + MIDDLE))
        sine[pl.ds(start, rows)] = s
        cosine[pl.ds(start, rows)] = c
    row = lax.broadcasted_iota(jnp.int32, (weight.shape[0], half), 0) + meta[2] * half - place[0, 0]
    col = lax.broadcasted_iota(jnp.int32, (weight.shape[0], half), 1) + meta[1] * half - place[0, 1]
    spread = (row * row + col * col).astype(F32)
    weight[...] = -omega / (1.0 + spread * (16.0 / (NX * NX)))


def turn_value(meta, scalars, blocks, block):
    cr, ci = scalars[2 + 2 * meta[0]], scalars[3 + 2 * meta[0]]
    ar = blocks[0, 1, 0:16, 0:128].astype(F32)[0:1, 0:1]
    ai = blocks[1, 1, 0:16, 0:128].astype(F32)[0:1, 0:1]
    first = block == 0
    return jnp.where(first, cr * ar - ci * ai, 0.0), jnp.where(first, cr * ai + ci * ar, 0.0)


def column_kernel(
    meta, scalars, near, far, blocks, edge_same, edge_cross, sine, cosine, solved, shifted, own_edge, real, imag
):
    rows = near.shape[0] // 4
    half = near.shape[1]
    xb = meta[2]
    for k, (piece, n) in enumerate(((near, 0), (near, 1), (far, 0), (far, 1))):
        start = pl.multiple_of((meta[3] ^ k) * rows, rows)
        real[pl.ds(start, rows)] = piece[2 * n * rows : (2 * n + 1) * rows]
        imag[pl.ds(start, rows)] = piece[(2 * n + 1) * rows : (2 * n + 2) * rows]
    cr, ci = scalars[2 + 2 * meta[0]], scalars[3 + 2 * meta[0]]
    ar, ai = turn_value(meta, scalars, blocks, xb)
    row = edge_rows(meta, blocks, xb, slice(0, half))
    own_real, own_imag = edge_product(xb, dot(row, real[...]), dot(row, imag[...]))
    hr = edge_same[0:1] + edge_cross[0:1] + ar * own_real - ai * own_imag
    hi = edge_same[1:2] + edge_cross[1:2] + ar * own_imag + ai * own_real
    add_real = cr * hr - ci * hi
    add_imag = cr * hi + ci * hr
    upper = xb == 1
    low = lax.broadcasted_iota(jnp.int32, (16, half), 0) == 0
    high = lax.broadcasted_iota(jnp.int32, (16, half), 0) == 15
    for ref, add in ((real, add_real), (imag, add_imag)):
        ref[0:16] = (ref[0:16].astype(F32) + jnp.where(low & upper, add, 0.0)).astype(BF16)
        ref[half - 16 :] = (
            ref[half - 16 :].astype(F32) + jnp.where(high & jnp.logical_not(upper), add, 0.0)
        ).astype(BF16)
    left = jnp.concatenate([blocks[0, xb], blocks[1, xb]], axis=0)
    for n in range(0, half, 256):
        cols = slice(n, n + 256)
        by_real = dot(left, real[:, cols])
        by_imag = dot(left, imag[:, cols])
        xr = (by_real[:half] - by_imag[half:]).astype(BF16)
        xi = (by_imag[:half] + by_real[half:]).astype(BF16)
        solved[:half, cols] = xr
        solved[half:, cols] = xi
        xr, xi = xr.astype(F32), xi.astype(F32)
        s, c = sine[:, cols], cosine[:, cols]
        shifted[:half, cols] = (xr * c - xi * s).astype(BF16)
        shifted[half:, cols] = (xi * c + xr * s).astype(BF16)
    own_real, own_imag = edge_product(xb, dot(row, shifted[:half]), dot(row, shifted[half:]))
    own_edge[0:1] = own_real
    own_edge[1:2] = own_imag


def both_kernel(meta, shifted, blocks, solved, edge):
    half = shifted.shape[1]
    xb, zz = meta[2], meta[1]
    left = jnp.concatenate([blocks[0, xb], blocks[1, xb]], axis=0)
    by_real = dot(left, shifted[:half])
    by_imag = dot(left, shifted[half:])
    u = jnp.concatenate(
        [(by_real[:half] - by_imag[half:]).astype(BF16), (by_imag[:half] + by_real[half:]).astype(BF16)], axis=0
    )
    row = dot_t(edge_rows(meta, blocks, zz, slice(0, half)), u)
    edge_real, edge_imag = edge_product(zz, row[:, :half], row[:, half:])
    edge[0:1] = edge_real
    edge[1:2] = edge_imag
    by_real = dot_t(u, blocks[0, zz])
    by_imag = dot_t(u, blocks[1, zz])
    solved[:half] = (by_real[:half] - by_imag[half:]).astype(BF16)
    solved[half:] = (by_real[half:] + by_imag[:half]).astype(BF16)


def image_pieces(meta, image, keep, send):
    rows, cols = keep.shape[1:]
    for kz in range(2):
        for kx in range(2):
            col = pl.multiple_of((meta[5] ^ kx) * cols, cols)
            for other, ref in ((0, keep), (1, send)):
                row = pl.multiple_of(((meta[4] ^ kz) * 2 + (meta[0] ^ other)) * rows, rows)
                ref[kz * 2 + kx] = image[pl.ds(row, rows), pl.ds(col, cols)].astype(BF16)


def pick_end(ends, block):
    first = block == 0
    return jnp.where(first, ends[0:1], ends[2:3]), jnp.where(first, ends[1:2], ends[3:4])


def turn_kernel(meta, scalars, edge_x, near_x, edge_y0, edge_y1, ends, blocks, whole, edge):
    ar, ai = turn_value(meta, scalars, blocks, meta[2])
    zz = meta[1]
    yr, yi = pick_edge(zz, edge_rows(meta, blocks, zz, slice(0, ends.shape[1])).astype(F32))
    pr, pi = pick_end(ends, meta[2])
    for n in range(2):
        r, i = slice(2 * n, 2 * n + 1), slice(2 * n + 1, 2 * n + 2)
        hr = near_x[r] + ar * edge_x[r] - ai * edge_x[i]
        hi = near_x[i] + ar * edge_x[i] + ai * edge_x[r]
        whole[r] = hr
        whole[i] = hi
        sr = jnp.sum(hr * yr - hi * yi, axis=1, keepdims=True)
        si = jnp.sum(hr * yi + hi * yr, axis=1, keepdims=True)
        edge_y = (edge_y0, edge_y1)[n]
        edge[r] = edge_y[0:1] + sr * pr - si * pi
        edge[i] = edge_y[1:2] + sr * pi + si * pr


def split(value):
    high = value.astype(BF16)
    return high.astype(F32), (value - high.astype(F32))


def between_kernel(meta, whole, blocks, source, receiver, weight, out, keep, send, image):
    high, low = split(whole[...])
    left = jnp.concatenate([high, low, high, low], axis=0).astype(BF16)
    by_real = dot_t(left, blocks[0, meta[1]])
    by_imag = dot_t(left, blocks[1, meta[1]])
    by_real = by_real[0:4] + by_real[4:8]
    by_imag = by_imag[0:4] + by_imag[4:8]
    for n in range(2):
        r, i = slice(2 * n, 2 * n + 1), slice(2 * n + 1, 2 * n + 2)
        out[r] = by_real[r] - by_imag[i]
        out[i] = by_real[i] + by_imag[r]
    half = source.shape[1]
    sr, si = source[:half].astype(F32), source[half:].astype(F32)
    rr, ri = receiver[:half].astype(F32), receiver[half:].astype(F32)
    image[...] = (sr * ri + si * rr) * weight[...]
    image_pieces(meta, image, keep, send)


def second_image_kernel(
    meta, scalars, source, receiver, weight, rows_y, edge, near, ends, blocks, keep, send, image
):
    half = source.shape[1]
    ar, ai = turn_value(meta, scalars, blocks, meta[1])
    pr, pi = pick_end(ends, meta[2])
    qr, qi = pick_end(ends, meta[1])

    def triple(value, order):
        high, low = split(value)
        return [high, high, low] if order == 0 else [high, low, high]

    fields = []
    for n, ref in enumerate((source, receiver)):
        r, i = slice(2 * n, 2 * n + 1), slice(2 * n + 1, 2 * n + 2)
        gr = near[r] + ar * edge[r] - ai * edge[i]
        gi = near[i] + ar * edge[i] + ai * edge[r]
        tr, ti = rows_y[r], rows_y[i]
        left, right_real, right_imag = [], [], []
        for a, b, c in ((pr, tr, ti), (pi, -ti, tr), (gr, qr, qi), (gi, -qi, qr)):
            left += triple(a, 0)
            right_real += triple(b, 1)
            right_imag += triple(c, 1)
        pad = [jnp.zeros((4, half), F32)]
        left = jnp.concatenate(left + pad, axis=0).astype(BF16)
        right_real = jnp.concatenate(right_real + pad, axis=0).astype(BF16)
        right_imag = jnp.concatenate(right_imag + pad, axis=0).astype(BF16)
        fields.append(
            (
                ref[:half].astype(F32) + dot_rows(left, right_real),
                ref[half:].astype(F32) + dot_rows(left, right_imag),
            )
        )
    (sr, si), (rr, ri) = fields
    image[...] = (sr * ri + si * rr) * weight[...]
    image_pieces(meta, image, keep, send)


def block_shards(
    source_field, residual_data, receiver_lines, shot_positions, slowness, frequency, line_inverse, coupling
):
    rows, length = slowness.shape[1:]
    half = line_inverse.shape[-1]
    slab = lax.axis_index("slab")
    shot = lax.axis_index("shot")
    meta = jnp.stack(
        [slab & 1, (slab >> 1) & 1, slab >> 2, slab & 3, shot >> 1, shot & 1]
    ).astype(jnp.int32)
    smem = pl.BlockSpec(memory_space=SMEM)
    vmem = pl.BlockSpec(memory_space=VMEM)
    hbm = pl.BlockSpec(memory_space=pltpu.HBM)

    def shape(dtype, *sizes):
        return jax.ShapeDtypeStruct(sizes, dtype)

    def call(body, name, specs, outs, scratch, mib, *args):
        return pl.pallas_call(
            body,
            in_specs=specs,
            out_specs=[vmem] * len(outs),
            out_shape=outs,
            scratch_shapes=scratch,
            compiler_params=params(mib),
            name=name,
        )(*args)

    def move(array, k):
        return lax.ppermute(array, "slab", [(i, i ^ k) for i in range(8)])

    cut = shape(BF16, 2 * rows, length)
    block_shape = shape(BF16, *line_inverse.shape[1:])
    core, raw, slow, freq = pl.pallas_call(
        other_kernel,
        in_specs=[smem, smem, vmem, vmem],
        out_specs=[vmem] * 3 + [smem],
        out_shape=[cut, shape(BF16, rows, 2, length), shape(F32, rows, length), shape(F32, 2)],
        compiler_params=params(12),
        name="other",
    )(meta, frequency, source_field, slowness)
    own, blocks = pl.pallas_call(
        own_kernel,
        in_specs=[smem, smem, vmem, vmem, hbm],
        out_specs=[vmem, vmem],
        out_shape=[cut, block_shape],
        scratch_shapes=[pltpu.SemaphoreType.DMA],
        compiler_params=params(OWN_MIB),
        name="own",
    )(meta, freq, raw, slow, line_inverse)
    core = move(core, 1)
    block_piece = shape(BF16, 4 * rows, half)
    same0, cross0, ends, scalars = pl.pallas_call(
        source_kernel,
        in_specs=[smem] * 3 + [vmem] * 3,
        out_specs=[vmem] * 3 + [smem],
        out_shape=[block_piece] * 2 + [shape(F32, 4, half), shape(F32, 6)],
        compiler_params=params(16),
        name="slab",
    )(meta, freq, coupling, own, core, blocks)
    far = [move(cross0, 2)]
    residual, same0, slow0 = lax.optimization_barrier((residual_data, same0, slow))
    (away,) = call(
        away_kernel, "away", [smem, vmem], [shape(BF16, rows, 2, length)], [], 12, meta, residual
    )
    core_raw = move(away, 1)
    core_slow0 = move(slow0, 1)
    layer, same0 = lax.optimization_barrier((slowness[1], same0))
    layer = (layer - MIDDLE).astype(jnp.float16)
    low, high = layer[:, :half], layer[:, half:]
    first = meta[1] == 0
    own_slow = jnp.where(first, low, high)
    far_slow = move(jnp.where(first, high, low), 2)
    same1, cross, *edges = call(
        receiver_kernel,
        "receiver",
        [smem, smem] + [vmem] * 8,
        [block_piece] * 2 + [shape(F32, 4, half)] * 2,
        [VMEM((2 * rows, length), BF16)] * 2 + [VMEM((4, half), F32)],
        20,
        meta,
        scalars,
        receiver_lines,
        residual_data,
        core_raw,
        slow,
        core_slow0,
        blocks,
        same0,
        cross0,
    )
    same = [same0, same1]
    edge_same = move(edges[0], 4)
    edge_cross = move(edges[1], 6)
    cross, far[0] = lax.optimization_barrier((cross, far[0]))
    far.append(move(cross, 2))
    pair = shape(BF16, 2 * half, half)
    line = shape(F32, 2, half)
    four = shape(F32, 4, half)
    far_slow, edge_same, edge_cross = lax.optimization_barrier((far_slow, edge_same, edge_cross))
    core_slow = move(jnp.stack([own_slow, far_slow]), 1)
    block = shape(F32, half, half)
    sine, cosine, weight = call(
        phase_kernel,
        "phase",
        [smem] * 3 + [vmem] * 4,
        [block] * 3,
        [],
        8,
        meta,
        scalars,
        shot_positions,
        own_slow.astype(F32),
        core_slow[0].astype(F32),
        far_slow.astype(F32),
        core_slow[1].astype(F32),
    )
    solved, finals, edge_x, edge_y = [], [], [], []
    for n in range(2):
        if n == 1:
            same[1], finals[0] = lax.optimization_barrier((same[1], finals[0]))
        x0, turned, edge = call(
            column_kernel,
            "column",
            [smem, smem] + [vmem] * 7,
            [pair, pair, line],
            [VMEM((half, half), BF16)] * 2,
            16,
            meta,
            scalars,
            same[n],
            far[n],
            blocks,
            edge_same[2 * n : 2 * n + 2],
            edge_cross[2 * n : 2 * n + 2],
            sine,
            cosine,
        )
        v, across = call(both_kernel, "both", [smem] + [vmem] * 2, [pair, line], [], 20, meta, turned, blocks)
        solved.append(x0)
        finals.append(v)
        edge_x.append(edge)
        edge_y.append(across)
    edge_x = jnp.concatenate(edge_x)
    near_x = move(edge_x, 4)
    coupled, edge = call(
        turn_kernel,
        "turn",
        [smem, smem] + [vmem] * 6,
        [four, four],
        [],
        4,
        meta,
        scalars,
        edge_x,
        near_x,
        *edge_y,
        ends,
        blocks,
    )
    near_y = move(edge, 2)
    cut = shape(BF16, 4, rows, half // 2)
    scratch = [VMEM((half, half), F32)]
    rows_y, keep0, send0 = call(
        between_kernel,
        "between",
        [smem] + [vmem] * 5,
        [four, cut, cut],
        scratch,
        12,
        meta,
        coupled,
        blocks,
        solved[0],
        solved[1],
        weight,
    )
    near_y, rows_y, send0 = lax.optimization_barrier((near_y, rows_y, send0))
    keep1, send1 = call(
        second_image_kernel,
        "second_image",
        [smem] * 2 + [vmem] * 8,
        [cut] * 2,
        scratch,
        12,
        meta,
        scalars,
        finals[0],
        finals[1],
        weight,
        rows_y,
        edge,
        near_y,
        ends,
        blocks,
    )
    part0 = keep0.astype(F32) + move(send0, 1).astype(F32)
    part1 = keep1.astype(F32) + move(send1, 1).astype(F32)
    both = jnp.stack([part0, part1], axis=1).astype(BF16)
    total = 0.0
    for kz, kx in ((0, 1), (1, 1), (0, 0), (1, 0)):
        route = []
        for s in range(4):
            for b in range(8):
                sy, sx, bx, bc = s // 2, s % 2, b // 4, b % 2
                by = (b // 2) % 2
                target = (by * 2 + (sx ^ kx)) * 8 + bx * 4 + (sy ^ kz) * 2 + bc
                route.append((s * 8 + b, target))
        total = total + lax.ppermute(both[kz * 2 + kx], ("shot", "slab"), route).astype(F32)
    return total


def solution(mesh):
    placed = (
        P("shot", None, "slab", None, None),
        P("shot", None, "slab", None, None),
        P("shot", None),
        P("shot", None),
        P(None, "slab", None),
        P(),
        P(),
        P(),
    )
    fits = mesh.shape["slab"] == 8 and mesh.shape["shot"] == 4

    def run(*args):
        line_inverse = args[6]
        blocks = fits and line_inverse.shape[0] == 2 and line_inverse.shape[2] == 2
        body = block_shards if blocks else general_shards
        return jax.shard_map(
            body, mesh=mesh, in_specs=placed, out_specs=P(None, "slab", "shot"), check_vma=False
        )(*args)

    return run
```

```python
from functools import partial

import jax
import jax.numpy as jnp
from jax import lax
from jax.experimental import pallas as pl
from jax.experimental.pallas import tpu as pltpu
from jax.sharding import PartitionSpec as P

NX = 1024
STEPS = 2


def pick_index(values, position, axis_number, keep=False):
    return lax.index_in_dim(values, position, axis_number, keepdims=keep)


def line_solve(wavefield, line_inverse, coupling, line_dim):
    in_shape = wavefield.shape
    freq_count = line_inverse.shape[0]
    blocks = line_inverse.shape[2]
    block_len = line_inverse.shape[3]
    real_blocks = line_inverse[:, 0]
    imag_blocks = line_inverse[:, 1]
    if line_dim == 5:
        pieces = wavefield.reshape(in_shape[:5] + (blocks, block_len))
        formula = "shfxcgj,fgij->shfxcgi"
    else:
        pieces = wavefield.reshape(in_shape[:3] + (blocks, block_len, in_shape[4] * in_shape[5]))
        formula = "shfgjz,fgij->shfgiz"
    with_real = jnp.einsum(formula, pieces, real_blocks, preferred_element_type=jnp.float32)
    with_imag = jnp.einsum(formula, pieces, imag_blocks, preferred_element_type=jnp.float32)
    if line_dim == 5:
        comp_axis, block_axis, cell_axis = (4, 4, 4)
        col_shape = (1, 1, freq_count, 1, block_len)
    else:
        with_real = with_real.reshape(in_shape[:3] + (blocks, block_len, in_shape[4], in_shape[5]))
        with_imag = with_imag.reshape(in_shape[:3] + (blocks, block_len, in_shape[4], in_shape[5]))
        comp_axis, block_axis, cell_axis = (5, 3, 3)
        col_shape = (1, 1, freq_count, block_len, 1)
    signs_six = jnp.array([1.0, -1.0], jnp.float32).reshape(1, 2, 1, 1, 1, 1)
    signs_five = jnp.array([1.0, -1.0], jnp.float32).reshape(1, 2, 1, 1, 1)
    u_real = pick_index(with_real, 0, comp_axis) - signs_six * pick_index(with_imag, 1, comp_axis)
    u_imag = pick_index(with_real, 1, comp_axis) + signs_six * pick_index(with_imag, 0, comp_axis)
    coup_real = coupling[:, 0].reshape(1, 1, freq_count, 1, 1)
    coup_imag = coupling[:, 1].reshape(1, 1, freq_count, 1, 1)

    def factor(block_index, column):
        col_real = line_inverse[:, 0, block_index, :, column].astype(jnp.float32).reshape(col_shape)
        col_imag = line_inverse[:, 1, block_index, :, column].astype(jnp.float32).reshape(col_shape)
        return (
            coup_real * col_real - coup_imag * col_imag,
            signs_five * (coup_imag * col_real + coup_real * col_imag),
        )

    fwd_real = [pick_index(u_real, 0, block_axis)]
    fwd_imag = [pick_index(u_imag, 0, block_axis)]
    block_index = 1
    mult_real, mult_imag = factor(block_index, 0)
    prev_real = pick_index(fwd_real[-1], block_len - 1, cell_axis, True)
    prev_imag = pick_index(fwd_imag[-1], block_len - 1, cell_axis, True)
    fwd_real.append(
        pick_index(u_real, block_index, block_axis) + mult_real * prev_real - mult_imag * prev_imag
    )
    fwd_imag.append(
        pick_index(u_imag, block_index, block_axis) + mult_real * prev_imag + mult_imag * prev_real
    )
    out_real = list(fwd_real)
    out_imag = list(fwd_imag)
    block_index = 0
    mult_real, mult_imag = factor(block_index, block_len - 1)
    next_real = pick_index(out_real[block_index + 1], 0, cell_axis, True)
    next_imag = pick_index(out_imag[block_index + 1], 0, cell_axis, True)
    out_real[block_index] = fwd_real[block_index] + mult_real * next_real - mult_imag * next_imag
    out_imag[block_index] = fwd_imag[block_index] + mult_real * next_imag + mult_imag * next_real
    real_line = jnp.stack(out_real, axis=block_axis).reshape(in_shape[:4] + (in_shape[5],))
    imag_line = jnp.stack(out_imag, axis=block_axis).reshape(in_shape[:4] + (in_shape[5],))
    return jnp.stack([real_line, imag_line], axis=4).astype(jnp.bfloat16)


def phase_shift(wavefield, slow_field, frequency):
    angles = frequency[:, None, None] * slow_field[None]
    cosine = jnp.cos(angles)[None, None]
    sine_part = jnp.sin(angles)[None, None]
    signs_five = jnp.array([1.0, -1.0], jnp.float32).reshape(1, 2, 1, 1, 1)
    real_part = wavefield[:, :, :, :, 0].astype(jnp.float32)
    imag_part = wavefield[:, :, :, :, 1].astype(jnp.float32)
    new_real = real_part * cosine - signs_five * imag_part * sine_part
    new_imag = imag_part * cosine + signs_five * real_part * sine_part
    return jnp.stack([new_real, new_imag], axis=4).astype(jnp.bfloat16)


def image_term(wavefield, row_cells, col_cells, shot_positions, frequency):
    source = wavefield[:, 0].astype(jnp.float32)
    receiver = wavefield[:, 1].astype(jnp.float32)
    cross = source[:, :, :, 0] * receiver[:, :, :, 1] - source[:, :, :, 1] * receiver[:, :, :, 0]
    weighted = jnp.sum(cross * frequency[None, :, None, None], axis=1)
    row_gap = row_cells[None, :, None] - shot_positions[:, 0][:, None, None]
    col_gap = col_cells[None, None, :] - shot_positions[:, 1][:, None, None]
    spread = (row_gap * row_gap + col_gap * col_gap).astype(jnp.float32)
    taper = 1.0 / (1.0 + spread * (16.0 / (NX * NX)))
    return jnp.sum(weighted * taper, axis=0)


def general_shards(
    source_field,
    residual_data,
    receiver_lines,
    shot_positions,
    slowness,
    frequency,
    line_inverse,
    coupling,
):
    row_count = source_field.shape[2]
    line_len = source_field.shape[4]
    receiver = residual_data * receiver_lines.astype(jnp.bfloat16)[:, None, None, None, :]
    wavefield = jnp.stack([source_field, receiver], axis=1)
    slab_start = lax.axis_index("slab") * row_count
    own_cells = slab_start + jnp.arange(row_count, dtype=jnp.int32)
    all_cells = jnp.arange(line_len, dtype=jnp.int32)
    solve_first = partial(line_solve, line_inverse=line_inverse, coupling=coupling, line_dim=3)
    solve_second = partial(line_solve, line_inverse=line_inverse, coupling=coupling, line_dim=5)

    def forward(fields):
        return solve_first(lax.all_to_all(fields, "slab", split_axis=5, concat_axis=3, tiled=True))

    def backward(fields):
        return lax.all_to_all(fields, "slab", split_axis=3, concat_axis=5, tiled=True)

    images = []
    for depth_index in range(STEPS):
        shifted = phase_shift(wavefield, slowness[depth_index], frequency)
        if depth_index % 2 == 0:
            wavefield = backward(forward(solve_second(shifted)))
        else:
            wavefield = solve_second(backward(forward(shifted)))
        local_image = image_term(wavefield, own_cells, all_cells, shot_positions, frequency)
        images.append(lax.psum_scatter(local_image, "shot", scatter_dimension=1, tiled=True))
    return jnp.stack(images)


F32 = jnp.float32
BF16 = jnp.bfloat16
SMEM = pltpu.SMEM
VMEM = pltpu.VMEM
OWN_MIB = 48
MIDDLE = 1.25


def params(mib):
    return pltpu.CompilerParams(vmem_limit_bytes=mib << 20)


def sincos(angle):
    turns = jnp.floor(angle * 0.15915494309189535 + 0.5)
    rest = (angle - turns * 6.28125) - turns * 1.9353071795864769e-3
    rest = rest * 0.25
    square = rest * rest
    sine = rest + rest * square * (
        -1.6666667e-1 + square * (8.3333333e-3 + square * (-1.9841270e-4 + square * 2.7557319e-6))
    )
    cosine = 1.0 + square * (
        -0.5 + square * (4.1666667e-2 + square * (-1.3888889e-3 + square * 2.4801587e-5))
    )
    sine, cosine = 2.0 * sine * cosine, 1.0 - 2.0 * sine * sine
    return 2.0 * sine * cosine, 1.0 - 2.0 * sine * sine


def dot_t(left, right):
    return lax.dot_general(left, right, (((1,), (1,)), ((), ())), preferred_element_type=F32)


def dot(left, right):
    return lax.dot_general(left, right, (((1,), (0,)), ((), ())), preferred_element_type=F32)


def dot_rows(left, right):
    return lax.dot_general(left, right, (((0,), (0,)), ((), ())), preferred_element_type=F32)


def rotate(omega, slow, real, imag, out):
    rows = slow.shape[0]
    sine, cosine = sincos(omega * slow)
    out[:rows] = (real * cosine - imag * sine).astype(BF16)
    out[rows:] = (imag * cosine + real * sine).astype(BF16)


def other_kernel(meta, freq, field, slowness, out, raw, slow, freq_out):
    f = meta[0] ^ 1
    raw[...] = field[0, meta[0]]
    slow[...] = slowness[0]
    for k in range(2):
        freq_out[k] = freq[k]
    rotate(freq[f], slowness[0], field[0, f, :, 0, :].astype(F32), field[0, f, :, 1, :].astype(F32), out)


def own_kernel(meta, freq, raw, slow, inverse, out, blocks, sem):
    fetch = pltpu.make_async_copy(inverse.at[meta[0]], blocks, sem)
    fetch.start()
    rotate(freq[meta[0]], slow[...], raw[:, 0, :].astype(F32), raw[:, 1, :].astype(F32), out)
    fetch.wait()


def source_kernel(meta, freq, coupling, own, core, blocks, same, cross, ends, scalars):
    for k in range(2):
        scalars[k] = freq[k]
        scalars[2 + 2 * k] = coupling[k, 0]
        scalars[3 + 2 * k] = coupling[k, 1]
    slab_kernel(meta, scalars, own, core, blocks, same, cross, ends)


def away_kernel(meta, residual, out):
    out[...] = residual[0, 1 - meta[0]]


def edge_rows(meta, blocks, block, lanes):
    start = pl.multiple_of((1 - block) * (blocks.shape[2] - 16), 16)
    return jnp.concatenate([blocks[part, block, pl.ds(start, 16), lanes] for part in range(2)], axis=0)


def pick_edge(block, values):
    first = block == 0
    return jnp.where(first, values[15:16], values[0:1]), jnp.where(first, values[31:32], values[16:17])


def edge_product(block, real, imag):
    rr, ir = pick_edge(block, real)
    ri, ii = pick_edge(block, imag)
    return rr - ii, ri + ir


def slab_kernel(meta, scalars, own, core, blocks, same, cross, ends):
    rows = own.shape[0] // 2
    half = blocks.shape[2]
    f, zz = meta[0], meta[1]
    cr, ci = scalars[2 + 2 * f], scalars[3 + 2 * f]
    spot = lax.broadcasted_iota(jnp.int32, (16, half), 1)
    line = lax.broadcasted_iota(jnp.int32, (16, half), 0)
    solved, columns = [], []
    for k in range(2):
        cells = slice(k * half, (k + 1) * half)
        hot = jnp.where((spot == (half - 1 if k == 0 else 0)) & (line == 0), 1.0, 0.0).astype(BF16)
        left = jnp.concatenate(
            [own[:rows, cells], core[:rows, cells], own[rows:, cells], core[rows:, cells], hot], axis=0
        )
        by_real = dot_t(left, blocks[0, k])
        by_imag = dot_t(left, blocks[1, k])
        n = 2 * rows
        solved.append((by_real[:n] - by_imag[n : 2 * n], by_real[n : 2 * n] + by_imag[:n]))
        ar, ai = by_real[2 * n : 2 * n + 1], by_imag[2 * n : 2 * n + 1]
        columns.append((cr * ar - ci * ai, cr * ai + ci * ar))
        ends[2 * k : 2 * k + 1] = columns[k][0]
        ends[2 * k + 1 : 2 * k + 2] = columns[k][1]

    def couple(k, er, ei):
        qr, qi = columns[k]
        return solved[k][0] + er * qr - ei * qi, solved[k][1] + er * qi + ei * qr

    upper = couple(1, solved[0][0][:, half - 1 :], solved[0][1][:, half - 1 :])
    lower = couple(0, upper[0][:, 0:1], upper[1][:, 0:1])
    first = zz == 0
    for part in range(2):
        low, high = lower[part].astype(BF16), upper[part].astype(BF16)
        mine, away = jnp.where(first, low, high), jnp.where(first, high, low)
        for n in range(2):
            at = slice((2 * n + part) * rows, (2 * n + part + 1) * rows)
            same[at] = mine[n * rows : (n + 1) * rows]
            cross[at] = away[n * rows : (n + 1) * rows]


def edge_kernel(meta, blocks, same0, cross0, same1, cross1, edge_same, edge_cross):
    rows = same0.shape[0] // 4
    xb, local = meta[2], meta[3]
    for refs, out in (((same0, same1), edge_same), ((cross0, cross1), edge_cross)):
        for part in range(2):
            total = 0.0
            for n in range(2):
                lanes = pl.ds(pl.multiple_of((local ^ n) * rows, rows), rows)
                row = edge_rows(meta, blocks, xb, lanes)
                at = slice((2 * n + part) * rows, (2 * n + part + 1) * rows)
                total = total + dot(row, jnp.concatenate([ref[at] for ref in refs], axis=1))
            if part == 0:
                real = total
        er, ei = edge_product(xb, real, total)
        half = same0.shape[1]
        for k in range(2):
            out[2 * k : 2 * k + 1] = er[:, k * half : (k + 1) * half]
            out[2 * k + 1 : 2 * k + 2] = ei[:, k * half : (k + 1) * half]


def receiver_kernel(
    meta, scalars, mask, field, core_raw, slow, core_slow, blocks, same0, cross0, same, cross, edge_same, edge_cross, own, core, ends
):
    keep = mask[...].astype(F32)
    f = meta[0]
    for raw, slowness, out in ((field.at[0, f], slow, own), (core_raw, core_slow, core)):
        rotate(
            scalars[f], slowness[...], raw[:, 0, :].astype(F32) * keep, -(raw[:, 1, :].astype(F32) * keep), out
        )
    slab_kernel(meta, scalars, own, core, blocks, same, cross, ends)
    edge_kernel(meta, blocks, same0, cross0, same, cross, edge_same, edge_cross)


def phase_kernel(meta, scalars, place, own, core, far, far_core, sine, cosine, weight):
    rows, half = own.shape
    omega = scalars[meta[0]]
    for k, piece in enumerate((own, core, far, far_core)):
        start = pl.multiple_of((meta[3] ^ k) * rows, rows)
        s, c = sincos(omega * (piece[...].astype(F32) + MIDDLE))
        sine[pl.ds(start, rows)] = s
        cosine[pl.ds(start, rows)] = c
    row = lax.broadcasted_iota(jnp.int32, (weight.shape[0], half), 0) + meta[2] * half - place[0, 0]
    col = lax.broadcasted_iota(jnp.int32, (weight.shape[0], half), 1) + meta[1] * half - place[0, 1]
    spread = (row * row + col * col).astype(F32)
    weight[...] = -omega / (1.0 + spread * (16.0 / (NX * NX)))


def turn_value(meta, scalars, blocks, block):
    cr, ci = scalars[2 + 2 * meta[0]], scalars[3 + 2 * meta[0]]
    ar = blocks[0, 1, 0:16, 0:128].astype(F32)[0:1, 0:1]
    ai = blocks[1, 1, 0:16, 0:128].astype(F32)[0:1, 0:1]
    first = block == 0
    return jnp.where(first, cr * ar - ci * ai, 0.0), jnp.where(first, cr * ai + ci * ar, 0.0)


def column_kernel(
    meta, scalars, near, far, blocks, edge_same, edge_cross, sine, cosine, solved, shifted, own_edge, lines
):
    rows = near.shape[0] // 4
    half = near.shape[1]
    xb = meta[2]
    real, imag = lines.at[pl.ds(0, half)], lines.at[pl.ds(half, half)]
    for k, (piece, n) in enumerate(((near, 0), (near, 1), (far, 0), (far, 1))):
        start = pl.multiple_of((meta[3] ^ k) * rows, rows)
        real[pl.ds(start, rows)] = piece[2 * n * rows : (2 * n + 1) * rows]
        imag[pl.ds(start, rows)] = piece[(2 * n + 1) * rows : (2 * n + 2) * rows]
    cr, ci = scalars[2 + 2 * meta[0]], scalars[3 + 2 * meta[0]]
    ar, ai = turn_value(meta, scalars, blocks, xb)
    row = edge_rows(meta, blocks, xb, slice(0, half))
    own_real, own_imag = edge_product(xb, dot(row, real[...]), dot(row, imag[...]))
    hr = edge_same[0:1] + edge_cross[0:1] + ar * own_real - ai * own_imag
    hi = edge_same[1:2] + edge_cross[1:2] + ar * own_imag + ai * own_real
    add_real = cr * hr - ci * hi
    add_imag = cr * hi + ci * hr
    upper = xb == 1
    low = lax.broadcasted_iota(jnp.int32, (16, half), 0) == 0
    high = lax.broadcasted_iota(jnp.int32, (16, half), 0) == 15
    for ref, add in ((real, add_real), (imag, add_imag)):
        ref[0:16] = (ref[0:16].astype(F32) + jnp.where(low & upper, add, 0.0)).astype(BF16)
        ref[half - 16 :] = (
            ref[half - 16 :].astype(F32) + jnp.where(high & jnp.logical_not(upper), add, 0.0)
        ).astype(BF16)
    left = complex_block(blocks, xb)
    for n in range(0, half, 256):
        cols = slice(n, n + 256)
        x = dot(left, lines[:, cols]).astype(BF16)
        xr, xi = x[:half], x[half:]
        solved[:half, cols] = xr
        solved[half:, cols] = xi
        xr, xi = xr.astype(F32), xi.astype(F32)
        s, c = sine[:, cols], cosine[:, cols]
        shifted[:half, cols] = (xr * c - xi * s).astype(BF16)
        shifted[half:, cols] = (xi * c + xr * s).astype(BF16)
    own_real, own_imag = edge_product(xb, dot(row, shifted[:half]), dot(row, shifted[half:]))
    own_edge[0:1] = own_real
    own_edge[1:2] = own_imag


def complex_block(blocks, block):
    real, imag = blocks[0, block], blocks[1, block]
    return jnp.concatenate(
        [jnp.concatenate([real, -imag], axis=1), jnp.concatenate([imag, real], axis=1)], axis=0
    )


def both_kernel(meta, shifted, blocks, solved, edge):
    half = shifted.shape[1]
    xb, zz = meta[2], meta[1]
    u = dot(complex_block(blocks, xb), shifted[...]).astype(BF16)
    row = dot_t(edge_rows(meta, blocks, zz, slice(0, half)), u)
    edge_real, edge_imag = edge_product(zz, row[:, :half], row[:, half:])
    edge[0:1] = edge_real
    edge[1:2] = edge_imag
    wide = jnp.concatenate([u[:half], u[half:]], axis=1)
    real, imag = blocks[0, zz], blocks[1, zz]
    solved[:half] = dot_t(wide, jnp.concatenate([real, -imag], axis=1)).astype(BF16)
    solved[half:] = dot_t(wide, jnp.concatenate([imag, real], axis=1)).astype(BF16)


def image_pieces(meta, image, keep, send):
    rows, cols = keep.shape[1:]
    for kz in range(2):
        for kx in range(2):
            col = pl.multiple_of((meta[5] ^ kx) * cols, cols)
            for other, ref in ((0, keep), (1, send)):
                row = pl.multiple_of(((meta[4] ^ kz) * 2 + (meta[0] ^ other)) * rows, rows)
                ref[kz * 2 + kx] = image[pl.ds(row, rows), pl.ds(col, cols)].astype(BF16)


def pick_end(ends, block):
    first = block == 0
    return jnp.where(first, ends[0:1], ends[2:3]), jnp.where(first, ends[1:2], ends[3:4])


def turn_kernel(meta, scalars, edge_x, near_x, edge_y0, edge_y1, ends, blocks, whole, edge):
    ar, ai = turn_value(meta, scalars, blocks, meta[2])
    zz = meta[1]
    yr, yi = pick_edge(zz, edge_rows(meta, blocks, zz, slice(0, ends.shape[1])).astype(F32))
    pr, pi = pick_end(ends, meta[2])
    for n in range(2):
        r, i = slice(2 * n, 2 * n + 1), slice(2 * n + 1, 2 * n + 2)
        hr = near_x[r] + ar * edge_x[r] - ai * edge_x[i]
        hi = near_x[i] + ar * edge_x[i] + ai * edge_x[r]
        whole[r] = hr
        whole[i] = hi
        sr = jnp.sum(hr * yr - hi * yi, axis=1, keepdims=True)
        si = jnp.sum(hr * yi + hi * yr, axis=1, keepdims=True)
        edge_y = (edge_y0, edge_y1)[n]
        edge[r] = edge_y[0:1] + sr * pr - si * pi
        edge[i] = edge_y[1:2] + sr * pi + si * pr


def split(value):
    high = value.astype(BF16)
    return high.astype(F32), (value - high.astype(F32))


def between_kernel(meta, whole, blocks, source, receiver, weight, out, keep, send, image):
    high, low = split(whole[...])
    left = jnp.concatenate([high, low, high, low], axis=0).astype(BF16)
    by_real = dot_t(left, blocks[0, meta[1]])
    by_imag = dot_t(left, blocks[1, meta[1]])
    by_real = by_real[0:4] + by_real[4:8]
    by_imag = by_imag[0:4] + by_imag[4:8]
    for n in range(2):
        r, i = slice(2 * n, 2 * n + 1), slice(2 * n + 1, 2 * n + 2)
        out[r] = by_real[r] - by_imag[i]
        out[i] = by_real[i] + by_imag[r]
    half = source.shape[1]
    sr, si = source[:half].astype(F32), source[half:].astype(F32)
    rr, ri = receiver[:half].astype(F32), receiver[half:].astype(F32)
    image[...] = (sr * ri + si * rr) * weight[...]
    image_pieces(meta, image, keep, send)


def second_image_kernel(
    meta, scalars, source, receiver, weight, rows_y, edge, near, ends, blocks, keep, send, image
):
    half = source.shape[1]
    ar, ai = turn_value(meta, scalars, blocks, meta[1])
    pr, pi = pick_end(ends, meta[2])
    qr, qi = pick_end(ends, meta[1])

    def triple(value, order):
        high, low = split(value)
        return [high, high, low] if order == 0 else [high, low, high]

    fields = []
    for n, ref in enumerate((source, receiver)):
        r, i = slice(2 * n, 2 * n + 1), slice(2 * n + 1, 2 * n + 2)
        gr = near[r] + ar * edge[r] - ai * edge[i]
        gi = near[i] + ar * edge[i] + ai * edge[r]
        tr, ti = rows_y[r], rows_y[i]
        left, right_real, right_imag = [], [], []
        for a, b, c in ((pr, tr, ti), (pi, -ti, tr), (gr, qr, qi), (gi, -qi, qr)):
            left += triple(a, 0)
            right_real += triple(b, 1)
            right_imag += triple(c, 1)
        pad = [jnp.zeros((4, half), F32)]
        left = jnp.concatenate(left + pad, axis=0).astype(BF16)
        right_real = jnp.concatenate(right_real + pad, axis=0).astype(BF16)
        right_imag = jnp.concatenate(right_imag + pad, axis=0).astype(BF16)
        fields.append(
            (
                ref[:half].astype(F32) + dot_rows(left, right_real),
                ref[half:].astype(F32) + dot_rows(left, right_imag),
            )
        )
    (sr, si), (rr, ri) = fields
    image[...] = (sr * ri + si * rr) * weight[...]
    image_pieces(meta, image, keep, send)


def block_shards(
    source_field, residual_data, receiver_lines, shot_positions, slowness, frequency, line_inverse, coupling
):
    rows, length = slowness.shape[1:]
    half = line_inverse.shape[-1]
    slab = lax.axis_index("slab")
    shot = lax.axis_index("shot")
    meta = jnp.stack(
        [slab & 1, (slab >> 1) & 1, slab >> 2, slab & 3, shot >> 1, shot & 1]
    ).astype(jnp.int32)
    smem = pl.BlockSpec(memory_space=SMEM)
    vmem = pl.BlockSpec(memory_space=VMEM)
    hbm = pl.BlockSpec(memory_space=pltpu.HBM)

    def shape(dtype, *sizes):
        return jax.ShapeDtypeStruct(sizes, dtype)

    def call(body, name, specs, outs, scratch, mib, *args):
        return pl.pallas_call(
            body,
            in_specs=specs,
            out_specs=[vmem] * len(outs),
            out_shape=outs,
            scratch_shapes=scratch,
            compiler_params=params(mib),
            name=name,
        )(*args)

    def move(array, k):
        return lax.ppermute(array, "slab", [(i, i ^ k) for i in range(8)])

    cut = shape(BF16, 2 * rows, length)
    block_shape = shape(BF16, *line_inverse.shape[1:])
    core, raw, slow, freq = pl.pallas_call(
        other_kernel,
        in_specs=[smem, smem, vmem, vmem],
        out_specs=[vmem] * 3 + [smem],
        out_shape=[cut, shape(BF16, rows, 2, length), shape(F32, rows, length), shape(F32, 2)],
        compiler_params=params(12),
        name="other",
    )(meta, frequency, source_field, slowness)
    own, blocks = pl.pallas_call(
        own_kernel,
        in_specs=[smem, smem, vmem, vmem, hbm],
        out_specs=[vmem, vmem],
        out_shape=[cut, block_shape],
        scratch_shapes=[pltpu.SemaphoreType.DMA],
        compiler_params=params(OWN_MIB),
        name="own",
    )(meta, freq, raw, slow, line_inverse)
    core = move(core, 1)
    block_piece = shape(BF16, 4 * rows, half)
    same0, cross0, ends, scalars = pl.pallas_call(
        source_kernel,
        in_specs=[smem] * 3 + [vmem] * 3,
        out_specs=[vmem] * 3 + [smem],
        out_shape=[block_piece] * 2 + [shape(F32, 4, half), shape(F32, 6)],
        compiler_params=params(16),
        name="slab",
    )(meta, freq, coupling, own, core, blocks)
    far = [move(cross0, 2)]
    residual, same0, slow0 = lax.optimization_barrier((residual_data, same0, slow))
    (away,) = call(
        away_kernel, "away", [smem, vmem], [shape(BF16, rows, 2, length)], [], 12, meta, residual
    )
    core_raw = move(away, 1)
    core_slow0 = move(slow0, 1)
    layer, same0 = lax.optimization_barrier((slowness[1], same0))
    layer = (layer - MIDDLE).astype(jnp.float16)
    low, high = layer[:, :half], layer[:, half:]
    first = meta[1] == 0
    own_slow = jnp.where(first, low, high)
    far_slow = move(jnp.where(first, high, low), 2)
    same1, cross, *edges = call(
        receiver_kernel,
        "receiver",
        [smem, smem] + [vmem] * 8,
        [block_piece] * 2 + [shape(F32, 4, half)] * 2,
        [VMEM((2 * rows, length), BF16)] * 2 + [VMEM((4, half), F32)],
        20,
        meta,
        scalars,
        receiver_lines,
        residual_data,
        core_raw,
        slow,
        core_slow0,
        blocks,
        same0,
        cross0,
    )
    same = [same0, same1]
    edge_same = move(edges[0], 4)
    edge_cross = move(edges[1], 6)
    cross, far[0] = lax.optimization_barrier((cross, far[0]))
    far.append(move(cross, 2))
    pair = shape(BF16, 2 * half, half)
    line = shape(F32, 2, half)
    four = shape(F32, 4, half)
    far_slow, edge_same, edge_cross = lax.optimization_barrier((far_slow, edge_same, edge_cross))
    core_slow = move(jnp.stack([own_slow, far_slow]), 1)
    block = shape(F32, half, half)
    sine, cosine, weight = call(
        phase_kernel,
        "phase",
        [smem] * 3 + [vmem] * 4,
        [block] * 3,
        [],
        8,
        meta,
        scalars,
        shot_positions,
        own_slow.astype(F32),
        core_slow[0].astype(F32),
        far_slow.astype(F32),
        core_slow[1].astype(F32),
    )
    solved, finals, edge_x, edge_y = [], [], [], []
    for n in range(2):
        if n == 1:
            same[1], finals[0] = lax.optimization_barrier((same[1], finals[0]))
        x0, turned, edge = call(
            column_kernel,
            "column",
            [smem, smem] + [vmem] * 7,
            [pair, pair, line],
            [VMEM((2 * half, half), BF16)],
            16,
            meta,
            scalars,
            same[n],
            far[n],
            blocks,
            edge_same[2 * n : 2 * n + 2],
            edge_cross[2 * n : 2 * n + 2],
            sine,
            cosine,
        )
        v, across = call(both_kernel, "both", [smem] + [vmem] * 2, [pair, line], [], 20, meta, turned, blocks)
        solved.append(x0)
        finals.append(v)
        edge_x.append(edge)
        edge_y.append(across)
    edge_x = jnp.concatenate(edge_x)
    near_x = move(edge_x, 4)
    coupled, edge = call(
        turn_kernel,
        "turn",
        [smem, smem] + [vmem] * 6,
        [four, four],
        [],
        4,
        meta,
        scalars,
        edge_x,
        near_x,
        *edge_y,
        ends,
        blocks,
    )
    near_y = move(edge, 2)
    cut = shape(BF16, 4, rows, half // 2)
    scratch = [VMEM((half, half), F32)]
    rows_y, keep0, send0 = call(
        between_kernel,
        "between",
        [smem] + [vmem] * 5,
        [four, cut, cut],
        scratch,
        12,
        meta,
        coupled,
        blocks,
        solved[0],
        solved[1],
        weight,
    )
    near_y, rows_y, send0 = lax.optimization_barrier((near_y, rows_y, send0))
    keep1, send1 = call(
        second_image_kernel,
        "second_image",
        [smem] * 2 + [vmem] * 8,
        [cut] * 2,
        scratch,
        12,
        meta,
        scalars,
        finals[0],
        finals[1],
        weight,
        rows_y,
        edge,
        near_y,
        ends,
        blocks,
    )
    part0 = keep0.astype(F32) + move(send0, 1).astype(F32)
    part1 = keep1.astype(F32) + move(send1, 1).astype(F32)
    both = jnp.stack([part0, part1], axis=1).astype(BF16)
    total = 0.0
    for kz, kx in ((0, 1), (1, 1), (0, 0), (1, 0)):
        route = []
        for s in range(4):
            for b in range(8):
                sy, sx, bx, bc = s // 2, s % 2, b // 4, b % 2
                by = (b // 2) % 2
                target = (by * 2 + (sx ^ kx)) * 8 + bx * 4 + (sy ^ kz) * 2 + bc
                route.append((s * 8 + b, target))
        total = total + lax.ppermute(both[kz * 2 + kx], ("shot", "slab"), route).astype(F32)
    return total


def solution(mesh):
    placed = (
        P("shot", None, "slab", None, None),
        P("shot", None, "slab", None, None),
        P("shot", None),
        P("shot", None),
        P(None, "slab", None),
        P(),
        P(),
        P(),
    )
    fits = mesh.shape["slab"] == 8 and mesh.shape["shot"] == 4

    def run(*args):
        line_inverse = args[6]
        blocks = fits and line_inverse.shape[0] == 2 and line_inverse.shape[2] == 2
        body = block_shards if blocks else general_shards
        return jax.shard_map(
            body, mesh=mesh, in_specs=placed, out_specs=P(None, "slab", "shot"), check_vma=False
        )(*args)

    return run
```

```python
from functools import partial

import jax
import jax.numpy as jnp
from jax import lax
from jax.experimental import pallas as pl
from jax.experimental.pallas import tpu as pltpu
from jax.sharding import PartitionSpec as P

NX = 1024
STEPS = 2


def pick_index(values, position, axis_number, keep=False):
    return lax.index_in_dim(values, position, axis_number, keepdims=keep)


def line_solve(wavefield, line_inverse, coupling, line_dim):
    in_shape = wavefield.shape
    freq_count = line_inverse.shape[0]
    blocks = line_inverse.shape[2]
    block_len = line_inverse.shape[3]
    real_blocks = line_inverse[:, 0]
    imag_blocks = line_inverse[:, 1]
    if line_dim == 5:
        pieces = wavefield.reshape(in_shape[:5] + (blocks, block_len))
        formula = "shfxcgj,fgij->shfxcgi"
    else:
        pieces = wavefield.reshape(in_shape[:3] + (blocks, block_len, in_shape[4] * in_shape[5]))
        formula = "shfgjz,fgij->shfgiz"
    with_real = jnp.einsum(formula, pieces, real_blocks, preferred_element_type=jnp.float32)
    with_imag = jnp.einsum(formula, pieces, imag_blocks, preferred_element_type=jnp.float32)
    if line_dim == 5:
        comp_axis, block_axis, cell_axis = (4, 4, 4)
        col_shape = (1, 1, freq_count, 1, block_len)
    else:
        with_real = with_real.reshape(in_shape[:3] + (blocks, block_len, in_shape[4], in_shape[5]))
        with_imag = with_imag.reshape(in_shape[:3] + (blocks, block_len, in_shape[4], in_shape[5]))
        comp_axis, block_axis, cell_axis = (5, 3, 3)
        col_shape = (1, 1, freq_count, block_len, 1)
    signs_six = jnp.array([1.0, -1.0], jnp.float32).reshape(1, 2, 1, 1, 1, 1)
    signs_five = jnp.array([1.0, -1.0], jnp.float32).reshape(1, 2, 1, 1, 1)
    u_real = pick_index(with_real, 0, comp_axis) - signs_six * pick_index(with_imag, 1, comp_axis)
    u_imag = pick_index(with_real, 1, comp_axis) + signs_six * pick_index(with_imag, 0, comp_axis)
    coup_real = coupling[:, 0].reshape(1, 1, freq_count, 1, 1)
    coup_imag = coupling[:, 1].reshape(1, 1, freq_count, 1, 1)

    def factor(block_index, column):
        col_real = line_inverse[:, 0, block_index, :, column].astype(jnp.float32).reshape(col_shape)
        col_imag = line_inverse[:, 1, block_index, :, column].astype(jnp.float32).reshape(col_shape)
        return (
            coup_real * col_real - coup_imag * col_imag,
            signs_five * (coup_imag * col_real + coup_real * col_imag),
        )

    fwd_real = [pick_index(u_real, 0, block_axis)]
    fwd_imag = [pick_index(u_imag, 0, block_axis)]
    block_index = 1
    mult_real, mult_imag = factor(block_index, 0)
    prev_real = pick_index(fwd_real[-1], block_len - 1, cell_axis, True)
    prev_imag = pick_index(fwd_imag[-1], block_len - 1, cell_axis, True)
    fwd_real.append(
        pick_index(u_real, block_index, block_axis) + mult_real * prev_real - mult_imag * prev_imag
    )
    fwd_imag.append(
        pick_index(u_imag, block_index, block_axis) + mult_real * prev_imag + mult_imag * prev_real
    )
    out_real = list(fwd_real)
    out_imag = list(fwd_imag)
    block_index = 0
    mult_real, mult_imag = factor(block_index, block_len - 1)
    next_real = pick_index(out_real[block_index + 1], 0, cell_axis, True)
    next_imag = pick_index(out_imag[block_index + 1], 0, cell_axis, True)
    out_real[block_index] = fwd_real[block_index] + mult_real * next_real - mult_imag * next_imag
    out_imag[block_index] = fwd_imag[block_index] + mult_real * next_imag + mult_imag * next_real
    real_line = jnp.stack(out_real, axis=block_axis).reshape(in_shape[:4] + (in_shape[5],))
    imag_line = jnp.stack(out_imag, axis=block_axis).reshape(in_shape[:4] + (in_shape[5],))
    return jnp.stack([real_line, imag_line], axis=4).astype(jnp.bfloat16)


def phase_shift(wavefield, slow_field, frequency):
    angles = frequency[:, None, None] * slow_field[None]
    cosine = jnp.cos(angles)[None, None]
    sine_part = jnp.sin(angles)[None, None]
    signs_five = jnp.array([1.0, -1.0], jnp.float32).reshape(1, 2, 1, 1, 1)
    real_part = wavefield[:, :, :, :, 0].astype(jnp.float32)
    imag_part = wavefield[:, :, :, :, 1].astype(jnp.float32)
    new_real = real_part * cosine - signs_five * imag_part * sine_part
    new_imag = imag_part * cosine + signs_five * real_part * sine_part
    return jnp.stack([new_real, new_imag], axis=4).astype(jnp.bfloat16)


def image_term(wavefield, row_cells, col_cells, shot_positions, frequency):
    source = wavefield[:, 0].astype(jnp.float32)
    receiver = wavefield[:, 1].astype(jnp.float32)
    cross = source[:, :, :, 0] * receiver[:, :, :, 1] - source[:, :, :, 1] * receiver[:, :, :, 0]
    weighted = jnp.sum(cross * frequency[None, :, None, None], axis=1)
    row_gap = row_cells[None, :, None] - shot_positions[:, 0][:, None, None]
    col_gap = col_cells[None, None, :] - shot_positions[:, 1][:, None, None]
    spread = (row_gap * row_gap + col_gap * col_gap).astype(jnp.float32)
    taper = 1.0 / (1.0 + spread * (16.0 / (NX * NX)))
    return jnp.sum(weighted * taper, axis=0)


def general_shards(
    source_field,
    residual_data,
    receiver_lines,
    shot_positions,
    slowness,
    frequency,
    line_inverse,
    coupling,
):
    row_count = source_field.shape[2]
    line_len = source_field.shape[4]
    receiver = residual_data * receiver_lines.astype(jnp.bfloat16)[:, None, None, None, :]
    wavefield = jnp.stack([source_field, receiver], axis=1)
    slab_start = lax.axis_index("slab") * row_count
    own_cells = slab_start + jnp.arange(row_count, dtype=jnp.int32)
    all_cells = jnp.arange(line_len, dtype=jnp.int32)
    solve_first = partial(line_solve, line_inverse=line_inverse, coupling=coupling, line_dim=3)
    solve_second = partial(line_solve, line_inverse=line_inverse, coupling=coupling, line_dim=5)

    def forward(fields):
        return solve_first(lax.all_to_all(fields, "slab", split_axis=5, concat_axis=3, tiled=True))

    def backward(fields):
        return lax.all_to_all(fields, "slab", split_axis=3, concat_axis=5, tiled=True)

    images = []
    for depth_index in range(STEPS):
        shifted = phase_shift(wavefield, slowness[depth_index], frequency)
        if depth_index % 2 == 0:
            wavefield = backward(forward(solve_second(shifted)))
        else:
            wavefield = solve_second(backward(forward(shifted)))
        local_image = image_term(wavefield, own_cells, all_cells, shot_positions, frequency)
        images.append(lax.psum_scatter(local_image, "shot", scatter_dimension=1, tiled=True))
    return jnp.stack(images)


F32 = jnp.float32
BF16 = jnp.bfloat16
SMEM = pltpu.SMEM
VMEM = pltpu.VMEM
OWN_MIB = 48
MIDDLE = 1.25


def params(mib):
    return pltpu.CompilerParams(vmem_limit_bytes=mib << 20)


def sincos(angle):
    turns = jnp.floor(angle * 0.15915494309189535 + 0.5)
    rest = (angle - turns * 6.28125) - turns * 1.9353071795864769e-3
    rest = rest * 0.25
    square = rest * rest
    sine = rest + rest * square * (
        -1.6666667e-1 + square * (8.3333333e-3 + square * (-1.9841270e-4 + square * 2.7557319e-6))
    )
    cosine = 1.0 + square * (
        -0.5 + square * (4.1666667e-2 + square * (-1.3888889e-3 + square * 2.4801587e-5))
    )
    sine, cosine = 2.0 * sine * cosine, 1.0 - 2.0 * sine * sine
    return 2.0 * sine * cosine, 1.0 - 2.0 * sine * sine


def dot_t(left, right):
    return lax.dot_general(left, right, (((1,), (1,)), ((), ())), preferred_element_type=F32)


def dot(left, right):
    return lax.dot_general(left, right, (((1,), (0,)), ((), ())), preferred_element_type=F32)


def dot_rows(left, right):
    return lax.dot_general(left, right, (((0,), (0,)), ((), ())), preferred_element_type=F32)


def rotate(omega, slow, real, imag, out):
    rows = slow.shape[0]
    sine, cosine = sincos(omega * slow)
    out[:rows] = (real * cosine - imag * sine).astype(BF16)
    out[rows:] = (imag * cosine + real * sine).astype(BF16)


def other_kernel(meta, freq, field, slowness, out, raw, slow, freq_out):
    f = meta[0] ^ 1
    raw[...] = field[0, meta[0]]
    slow[...] = slowness[0]
    for k in range(2):
        freq_out[k] = freq[k]
    rotate(freq[f], slowness[0], field[0, f, :, 0, :].astype(F32), field[0, f, :, 1, :].astype(F32), out)


def own_kernel(meta, freq, raw, slow, inverse, out, blocks, sem):
    fetch = pltpu.make_async_copy(inverse.at[meta[0]], blocks, sem)
    fetch.start()
    rotate(freq[meta[0]], slow[...], raw[:, 0, :].astype(F32), raw[:, 1, :].astype(F32), out)
    fetch.wait()


def source_kernel(meta, freq, coupling, own, core, blocks, same, cross, ends, scalars):
    for k in range(2):
        scalars[k] = freq[k]
        scalars[2 + 2 * k] = coupling[k, 0]
        scalars[3 + 2 * k] = coupling[k, 1]
    slab_kernel(meta, scalars, own, core, blocks, same, cross, ends)


def away_kernel(meta, residual, out):
    out[...] = residual[0, 1 - meta[0]]


def edge_rows(meta, blocks, block, lanes):
    start = pl.multiple_of((1 - block) * (blocks.shape[2] - 16), 16)
    return jnp.concatenate([blocks[part, block, pl.ds(start, 16), lanes] for part in range(2)], axis=0)


def pick_edge(block, values):
    first = block == 0
    return jnp.where(first, values[15:16], values[0:1]), jnp.where(first, values[31:32], values[16:17])


def edge_product(block, real, imag):
    rr, ir = pick_edge(block, real)
    ri, ii = pick_edge(block, imag)
    return rr - ii, ri + ir


def slab_kernel(meta, scalars, own, core, blocks, same, cross, ends):
    rows = own.shape[0] // 2
    half = blocks.shape[2]
    f, zz = meta[0], meta[1]
    cr, ci = scalars[2 + 2 * f], scalars[3 + 2 * f]
    spot = lax.broadcasted_iota(jnp.int32, (16, half), 1)
    line = lax.broadcasted_iota(jnp.int32, (16, half), 0)
    solved, columns = [], []
    for k in range(2):
        cells = slice(k * half, (k + 1) * half)
        hot = jnp.where((spot == (half - 1 if k == 0 else 0)) & (line == 0), 1.0, 0.0).astype(BF16)
        left = jnp.concatenate(
            [own[:rows, cells], core[:rows, cells], own[rows:, cells], core[rows:, cells], hot], axis=0
        )
        by_real = dot_t(left, blocks[0, k])
        by_imag = dot_t(left, blocks[1, k])
        n = 2 * rows
        solved.append((by_real[:n] - by_imag[n : 2 * n], by_real[n : 2 * n] + by_imag[:n]))
        ar, ai = by_real[2 * n : 2 * n + 1], by_imag[2 * n : 2 * n + 1]
        columns.append((cr * ar - ci * ai, cr * ai + ci * ar))
        ends[2 * k : 2 * k + 1] = columns[k][0]
        ends[2 * k + 1 : 2 * k + 2] = columns[k][1]

    def couple(k, er, ei):
        qr, qi = columns[k]
        return solved[k][0] + er * qr - ei * qi, solved[k][1] + er * qi + ei * qr

    upper = couple(1, solved[0][0][:, half - 1 :], solved[0][1][:, half - 1 :])
    lower = couple(0, upper[0][:, 0:1], upper[1][:, 0:1])
    first = zz == 0
    for part in range(2):
        low, high = lower[part].astype(BF16), upper[part].astype(BF16)
        mine, away = jnp.where(first, low, high), jnp.where(first, high, low)
        for n in range(2):
            at = slice((2 * n + part) * rows, (2 * n + part + 1) * rows)
            same[at] = mine[n * rows : (n + 1) * rows]
            cross[at] = away[n * rows : (n + 1) * rows]


def edge_kernel(meta, blocks, same0, cross0, same1, cross1, edge_same, edge_cross):
    rows = same0.shape[0] // 4
    xb, local = meta[2], meta[3]
    for refs, out in (((same0, same1), edge_same), ((cross0, cross1), edge_cross)):
        for part in range(2):
            total = 0.0
            for n in range(2):
                lanes = pl.ds(pl.multiple_of((local ^ n) * rows, rows), rows)
                row = edge_rows(meta, blocks, xb, lanes)
                at = slice((2 * n + part) * rows, (2 * n + part + 1) * rows)
                total = total + dot(row, jnp.concatenate([ref[at] for ref in refs], axis=1))
            if part == 0:
                real = total
        er, ei = edge_product(xb, real, total)
        half = same0.shape[1]
        for k in range(2):
            out[2 * k : 2 * k + 1] = er[:, k * half : (k + 1) * half]
            out[2 * k + 1 : 2 * k + 2] = ei[:, k * half : (k + 1) * half]


def receiver_kernel(
    meta, scalars, mask, field, core_raw, slow, core_slow, blocks, same0, cross0, same, cross, edge_same, edge_cross, own, core, ends
):
    keep = mask[...].astype(F32)
    f = meta[0]
    for raw, slowness, out in ((field.at[0, f], slow, own), (core_raw, core_slow, core)):
        rotate(
            scalars[f], slowness[...], raw[:, 0, :].astype(F32) * keep, -(raw[:, 1, :].astype(F32) * keep), out
        )
    slab_kernel(meta, scalars, own, core, blocks, same, cross, ends)
    edge_kernel(meta, blocks, same0, cross0, same, cross, edge_same, edge_cross)


def phase_kernel(meta, scalars, place, own, core, far, far_core, sine, cosine, weight):
    rows, half = own.shape
    omega = scalars[meta[0]]
    for k, piece in enumerate((own, core, far, far_core)):
        start = pl.multiple_of((meta[3] ^ k) * rows, rows)
        s, c = sincos(omega * (piece[...].astype(F32) + MIDDLE))
        sine[pl.ds(start, rows)] = s
        cosine[pl.ds(start, rows)] = c
    row = lax.broadcasted_iota(jnp.int32, (weight.shape[0], half), 0) + meta[2] * half - place[0, 0]
    col = lax.broadcasted_iota(jnp.int32, (weight.shape[0], half), 1) + meta[1] * half - place[0, 1]
    spread = (row * row + col * col).astype(F32)
    weight[...] = -omega / (1.0 + spread * (16.0 / (NX * NX)))


def turn_value(meta, scalars, blocks, block):
    cr, ci = scalars[2 + 2 * meta[0]], scalars[3 + 2 * meta[0]]
    ar = blocks[0, 1, 0:16, 0:128].astype(F32)[0:1, 0:1]
    ai = blocks[1, 1, 0:16, 0:128].astype(F32)[0:1, 0:1]
    first = block == 0
    return jnp.where(first, cr * ar - ci * ai, 0.0), jnp.where(first, cr * ai + ci * ar, 0.0)


def column_kernel(
    meta, scalars, near, far, blocks, edge_same, edge_cross, sine, cosine, solved, shifted, own_edge, lines
):
    rows = near.shape[0] // 4
    half = near.shape[1]
    xb = meta[2]
    real, imag = lines.at[pl.ds(0, half)], lines.at[pl.ds(half, half)]
    for k, (piece, n) in enumerate(((near, 0), (near, 1), (far, 0), (far, 1))):
        start = pl.multiple_of((meta[3] ^ k) * rows, rows)
        real[pl.ds(start, rows)] = piece[2 * n * rows : (2 * n + 1) * rows]
        imag[pl.ds(start, rows)] = piece[(2 * n + 1) * rows : (2 * n + 2) * rows]
    cr, ci = scalars[2 + 2 * meta[0]], scalars[3 + 2 * meta[0]]
    ar, ai = turn_value(meta, scalars, blocks, xb)
    row = edge_rows(meta, blocks, xb, slice(0, half))
    own_real, own_imag = edge_product(xb, dot(row, real[...]), dot(row, imag[...]))
    hr = edge_same[0:1] + edge_cross[0:1] + ar * own_real - ai * own_imag
    hi = edge_same[1:2] + edge_cross[1:2] + ar * own_imag + ai * own_real
    add_real = cr * hr - ci * hi
    add_imag = cr * hi + ci * hr
    upper = xb == 1
    low = lax.broadcasted_iota(jnp.int32, (16, half), 0) == 0
    high = lax.broadcasted_iota(jnp.int32, (16, half), 0) == 15
    for ref, add in ((real, add_real), (imag, add_imag)):
        ref[0:16] = (ref[0:16].astype(F32) + jnp.where(low & upper, add, 0.0)).astype(BF16)
        ref[half - 16 :] = (
            ref[half - 16 :].astype(F32) + jnp.where(high & jnp.logical_not(upper), add, 0.0)
        ).astype(BF16)
    left = complex_block(blocks, xb)
    for n in range(0, half, 256):
        cols = slice(n, n + 256)
        x = dot(left, lines[:, cols]).astype(BF16)
        xr, xi = x[:half], x[half:]
        solved[:half, cols] = xr
        solved[half:, cols] = xi
        xr, xi = xr.astype(F32), xi.astype(F32)
        s, c = sine[:, cols], cosine[:, cols]
        shifted[:half, cols] = (xr * c - xi * s).astype(BF16)
        shifted[half:, cols] = (xi * c + xr * s).astype(BF16)
    own_real, own_imag = edge_product(xb, dot(row, shifted[:half]), dot(row, shifted[half:]))
    own_edge[0:1] = own_real
    own_edge[1:2] = own_imag


def complex_block(blocks, block):
    real, imag = blocks[0, block], blocks[1, block]
    return jnp.concatenate(
        [jnp.concatenate([real, -imag], axis=1), jnp.concatenate([imag, real], axis=1)], axis=0
    )


def both_kernel(meta, shifted, blocks, solved, edge):
    half = shifted.shape[1]
    xb, zz = meta[2], meta[1]
    u = dot(complex_block(blocks, xb), shifted[...]).astype(BF16)
    row = dot_t(edge_rows(meta, blocks, zz, slice(0, half)), u)
    edge_real, edge_imag = edge_product(zz, row[:, :half], row[:, half:])
    edge[0:1] = edge_real
    edge[1:2] = edge_imag
    wide = jnp.concatenate([u[:half], u[half:]], axis=1)
    real, imag = blocks[0, zz], blocks[1, zz]
    solved[:half] = dot_t(wide, jnp.concatenate([real, -imag], axis=1)).astype(BF16)
    solved[half:] = dot_t(wide, jnp.concatenate([imag, real], axis=1)).astype(BF16)


def image_pieces(meta, image, keep, send):
    rows, cols = keep.shape[1:]
    for kz in range(2):
        for kx in range(2):
            col = pl.multiple_of((meta[5] ^ kx) * cols, cols)
            for other, ref in ((0, keep), (1, send)):
                row = pl.multiple_of(((meta[4] ^ kz) * 2 + (meta[0] ^ other)) * rows, rows)
                ref[kz * 2 + kx] = image[pl.ds(row, rows), pl.ds(col, cols)].astype(BF16)


def pick_end(ends, block):
    first = block == 0
    return jnp.where(first, ends[0:1], ends[2:3]), jnp.where(first, ends[1:2], ends[3:4])


def turn_kernel(meta, scalars, edge_x, near_x, edge_y0, edge_y1, ends, blocks, whole, edge):
    ar, ai = turn_value(meta, scalars, blocks, meta[2])
    zz = meta[1]
    yr, yi = pick_edge(zz, edge_rows(meta, blocks, zz, slice(0, ends.shape[1])).astype(F32))
    pr, pi = pick_end(ends, meta[2])
    for n in range(2):
        r, i = slice(2 * n, 2 * n + 1), slice(2 * n + 1, 2 * n + 2)
        hr = near_x[r] + ar * edge_x[r] - ai * edge_x[i]
        hi = near_x[i] + ar * edge_x[i] + ai * edge_x[r]
        whole[r] = hr
        whole[i] = hi
        sr = jnp.sum(hr * yr - hi * yi, axis=1, keepdims=True)
        si = jnp.sum(hr * yi + hi * yr, axis=1, keepdims=True)
        edge_y = (edge_y0, edge_y1)[n]
        edge[r] = edge_y[0:1] + sr * pr - si * pi
        edge[i] = edge_y[1:2] + sr * pi + si * pr


def split(value):
    high = value.astype(BF16)
    return high.astype(F32), (value - high.astype(F32))


def between_kernel(meta, whole, blocks, source, receiver, weight, out, keep, send, image):
    high, low = split(whole[...])
    left = jnp.concatenate([high, low, high, low], axis=0).astype(BF16)
    by_real = dot_t(left, blocks[0, meta[1]])
    by_imag = dot_t(left, blocks[1, meta[1]])
    by_real = by_real[0:4] + by_real[4:8]
    by_imag = by_imag[0:4] + by_imag[4:8]
    for n in range(2):
        r, i = slice(2 * n, 2 * n + 1), slice(2 * n + 1, 2 * n + 2)
        out[r] = by_real[r] - by_imag[i]
        out[i] = by_real[i] + by_imag[r]
    half = source.shape[1]
    sr, si = source[:half].astype(F32), source[half:].astype(F32)
    rr, ri = receiver[:half].astype(F32), receiver[half:].astype(F32)
    image[...] = (sr * ri + si * rr) * weight[...]
    image_pieces(meta, image, keep, send)


def second_image_kernel(
    meta, scalars, source, receiver, weight, rows_y, edge, near, ends, blocks, keep, send, image
):
    half = source.shape[1]
    ar, ai = turn_value(meta, scalars, blocks, meta[1])
    pr, pi = pick_end(ends, meta[2])
    qr, qi = pick_end(ends, meta[1])

    def triple(value, order):
        high, low = split(value)
        return [high, high, low] if order == 0 else [high, low, high]

    fields = []
    for n, ref in enumerate((source, receiver)):
        r, i = slice(2 * n, 2 * n + 1), slice(2 * n + 1, 2 * n + 2)
        gr = near[r] + ar * edge[r] - ai * edge[i]
        gi = near[i] + ar * edge[i] + ai * edge[r]
        tr, ti = rows_y[r], rows_y[i]
        left, right_real, right_imag = [], [], []
        for a, b, c in ((pr, tr, ti), (pi, -ti, tr), (gr, qr, qi), (gi, -qi, qr)):
            left += triple(a, 0)
            right_real += triple(b, 1)
            right_imag += triple(c, 1)
        pad = [jnp.zeros((4, half), F32)]
        left = jnp.concatenate(left + pad, axis=0).astype(BF16)
        right_real = jnp.concatenate(right_real + pad, axis=0).astype(BF16)
        right_imag = jnp.concatenate(right_imag + pad, axis=0).astype(BF16)
        fields.append(
            (
                ref[:half].astype(F32) + dot_rows(left, right_real),
                ref[half:].astype(F32) + dot_rows(left, right_imag),
            )
        )
    (sr, si), (rr, ri) = fields
    image[...] = (sr * ri + si * rr) * weight[...]
    image_pieces(meta, image, keep, send)


def block_shards(
    source_field, residual_data, receiver_lines, shot_positions, slowness, frequency, line_inverse, coupling
):
    rows, length = slowness.shape[1:]
    half = line_inverse.shape[-1]
    slab = lax.axis_index("slab")
    shot = lax.axis_index("shot")
    meta = jnp.stack(
        [slab & 1, (slab >> 1) & 1, slab >> 2, slab & 3, shot >> 1, shot & 1]
    ).astype(jnp.int32)
    smem = pl.BlockSpec(memory_space=SMEM)
    vmem = pl.BlockSpec(memory_space=VMEM)
    hbm = pl.BlockSpec(memory_space=pltpu.HBM)

    def shape(dtype, *sizes):
        return jax.ShapeDtypeStruct(sizes, dtype)

    def call(body, name, specs, outs, scratch, mib, *args):
        return pl.pallas_call(
            body,
            in_specs=specs,
            out_specs=[vmem] * len(outs),
            out_shape=outs,
            scratch_shapes=scratch,
            compiler_params=params(mib),
            name=name,
        )(*args)

    def move(array, k):
        return lax.ppermute(array, "slab", [(i, i ^ k) for i in range(8)])

    cut = shape(BF16, 2 * rows, length)
    block_shape = shape(BF16, *line_inverse.shape[1:])
    core, raw, slow, freq = pl.pallas_call(
        other_kernel,
        in_specs=[smem, smem, vmem, vmem],
        out_specs=[vmem] * 3 + [smem],
        out_shape=[cut, shape(BF16, rows, 2, length), shape(F32, rows, length), shape(F32, 2)],
        compiler_params=params(12),
        name="other",
    )(meta, frequency, source_field, slowness)
    own, blocks = pl.pallas_call(
        own_kernel,
        in_specs=[smem, smem, vmem, vmem, hbm],
        out_specs=[vmem, vmem],
        out_shape=[cut, block_shape],
        scratch_shapes=[pltpu.SemaphoreType.DMA],
        compiler_params=params(OWN_MIB),
        name="own",
    )(meta, freq, raw, slow, line_inverse)
    core = move(core, 1)
    block_piece = shape(BF16, 4 * rows, half)
    same0, cross0, ends, scalars = pl.pallas_call(
        source_kernel,
        in_specs=[smem] * 3 + [vmem] * 3,
        out_specs=[vmem] * 3 + [smem],
        out_shape=[block_piece] * 2 + [shape(F32, 4, half), shape(F32, 6)],
        compiler_params=params(16),
        name="slab",
    )(meta, freq, coupling, own, core, blocks)
    far = [move(cross0, 2)]
    residual, same0, slow0 = lax.optimization_barrier((residual_data, same0, slow))
    (away,) = call(
        away_kernel, "away", [smem, vmem], [shape(BF16, rows, 2, length)], [], 12, meta, residual
    )
    core_raw = move(away, 1)
    core_slow0 = move(slow0, 1)
    layer, same0 = lax.optimization_barrier((slowness[1], same0))
    layer = (layer - MIDDLE).astype(jnp.float16)
    low, high = layer[:, :half], layer[:, half:]
    first = meta[1] == 0
    own_slow = jnp.where(first, low, high)
    far_slow = move(jnp.where(first, high, low), 2)
    same1, cross, *edges = call(
        receiver_kernel,
        "receiver",
        [smem, smem] + [vmem] * 8,
        [block_piece] * 2 + [shape(F32, 4, half)] * 2,
        [VMEM((2 * rows, length), BF16)] * 2 + [VMEM((4, half), F32)],
        20,
        meta,
        scalars,
        receiver_lines,
        residual_data,
        core_raw,
        slow,
        core_slow0,
        blocks,
        same0,
        cross0,
    )
    same = [same0, same1]
    edge_same = move(edges[0], 4)
    edge_cross = move(edges[1], 6)
    cross, far[0] = lax.optimization_barrier((cross, far[0]))
    far.append(move(cross, 2))
    pair = shape(BF16, 2 * half, half)
    line = shape(F32, 2, half)
    four = shape(F32, 4, half)
    far_slow, edge_same = lax.optimization_barrier((far_slow, edge_same))
    core_slow = move(jnp.stack([own_slow, far_slow]), 1)
    block = shape(F32, half, half)
    sine, cosine, weight = call(
        phase_kernel,
        "phase",
        [smem] * 3 + [vmem] * 4,
        [block] * 3,
        [],
        8,
        meta,
        scalars,
        shot_positions,
        own_slow.astype(F32),
        core_slow[0].astype(F32),
        far_slow.astype(F32),
        core_slow[1].astype(F32),
    )
    solved, finals, edge_x, edge_y = [], [], [], []
    for n in range(2):
        if n == 1:
            same[1], finals[0] = lax.optimization_barrier((same[1], finals[0]))
        x0, turned, edge = call(
            column_kernel,
            "column",
            [smem, smem] + [vmem] * 7,
            [pair, pair, line],
            [VMEM((2 * half, half), BF16)],
            16,
            meta,
            scalars,
            same[n],
            far[n],
            blocks,
            edge_same[2 * n : 2 * n + 2],
            edge_cross[2 * n : 2 * n + 2],
            sine,
            cosine,
        )
        v, across = call(both_kernel, "both", [smem] + [vmem] * 2, [pair, line], [], 20, meta, turned, blocks)
        solved.append(x0)
        finals.append(v)
        edge_x.append(edge)
        edge_y.append(across)
    edge_x = jnp.concatenate(edge_x)
    near_x = move(edge_x, 4)
    coupled, edge = call(
        turn_kernel,
        "turn",
        [smem, smem] + [vmem] * 6,
        [four, four],
        [],
        4,
        meta,
        scalars,
        edge_x,
        near_x,
        *edge_y,
        ends,
        blocks,
    )
    near_y = move(edge, 2)
    cut = shape(BF16, 4, rows, half // 2)
    scratch = [VMEM((half, half), F32)]
    rows_y, keep0, send0 = call(
        between_kernel,
        "between",
        [smem] + [vmem] * 5,
        [four, cut, cut],
        scratch,
        12,
        meta,
        coupled,
        blocks,
        solved[0],
        solved[1],
        weight,
    )
    near_y, rows_y, send0 = lax.optimization_barrier((near_y, rows_y, send0))
    keep1, send1 = call(
        second_image_kernel,
        "second_image",
        [smem] * 2 + [vmem] * 8,
        [cut] * 2,
        scratch,
        12,
        meta,
        scalars,
        finals[0],
        finals[1],
        weight,
        rows_y,
        edge,
        near_y,
        ends,
        blocks,
    )
    part0 = keep0.astype(F32) + move(send0, 1).astype(F32)
    part1 = keep1.astype(F32) + move(send1, 1).astype(F32)
    both = jnp.stack([part0, part1], axis=1).astype(BF16)
    total = 0.0
    for kz, kx in ((0, 1), (1, 1), (0, 0), (1, 0)):
        route = []
        for s in range(4):
            for b in range(8):
                sy, sx, bx, bc = s // 2, s % 2, b // 4, b % 2
                by = (b // 2) % 2
                target = (by * 2 + (sx ^ kx)) * 8 + bx * 4 + (sy ^ kz) * 2 + bc
                route.append((s * 8 + b, target))
        total = total + lax.ppermute(both[kz * 2 + kx], ("shot", "slab"), route).astype(F32)
    return total


def solution(mesh):
    placed = (
        P("shot", None, "slab", None, None),
        P("shot", None, "slab", None, None),
        P("shot", None),
        P("shot", None),
        P(None, "slab", None),
        P(),
        P(),
        P(),
    )
    fits = mesh.shape["slab"] == 8 and mesh.shape["shot"] == 4

    def run(*args):
        line_inverse = args[6]
        blocks = fits and line_inverse.shape[0] == 2 and line_inverse.shape[2] == 2
        body = block_shards if blocks else general_shards
        return jax.shard_map(
            body, mesh=mesh, in_specs=placed, out_specs=P(None, "slab", "shot"), check_vma=False
        )(*args)

    return run
```

```python
from functools import partial

import jax
import jax.numpy as jnp
from jax import lax
from jax.experimental import pallas as pl
from jax.experimental.pallas import tpu as pltpu
from jax.sharding import PartitionSpec as P

NX = 1024
STEPS = 2


def pick_index(values, position, axis_number, keep=False):
    return lax.index_in_dim(values, position, axis_number, keepdims=keep)


def line_solve(wavefield, line_inverse, coupling, line_dim):
    in_shape = wavefield.shape
    freq_count = line_inverse.shape[0]
    blocks = line_inverse.shape[2]
    block_len = line_inverse.shape[3]
    real_blocks = line_inverse[:, 0]
    imag_blocks = line_inverse[:, 1]
    if line_dim == 5:
        pieces = wavefield.reshape(in_shape[:5] + (blocks, block_len))
        formula = "shfxcgj,fgij->shfxcgi"
    else:
        pieces = wavefield.reshape(in_shape[:3] + (blocks, block_len, in_shape[4] * in_shape[5]))
        formula = "shfgjz,fgij->shfgiz"
    with_real = jnp.einsum(formula, pieces, real_blocks, preferred_element_type=jnp.float32)
    with_imag = jnp.einsum(formula, pieces, imag_blocks, preferred_element_type=jnp.float32)
    if line_dim == 5:
        comp_axis, block_axis, cell_axis = (4, 4, 4)
        col_shape = (1, 1, freq_count, 1, block_len)
    else:
        with_real = with_real.reshape(in_shape[:3] + (blocks, block_len, in_shape[4], in_shape[5]))
        with_imag = with_imag.reshape(in_shape[:3] + (blocks, block_len, in_shape[4], in_shape[5]))
        comp_axis, block_axis, cell_axis = (5, 3, 3)
        col_shape = (1, 1, freq_count, block_len, 1)
    signs_six = jnp.array([1.0, -1.0], jnp.float32).reshape(1, 2, 1, 1, 1, 1)
    signs_five = jnp.array([1.0, -1.0], jnp.float32).reshape(1, 2, 1, 1, 1)
    u_real = pick_index(with_real, 0, comp_axis) - signs_six * pick_index(with_imag, 1, comp_axis)
    u_imag = pick_index(with_real, 1, comp_axis) + signs_six * pick_index(with_imag, 0, comp_axis)
    coup_real = coupling[:, 0].reshape(1, 1, freq_count, 1, 1)
    coup_imag = coupling[:, 1].reshape(1, 1, freq_count, 1, 1)

    def factor(block_index, column):
        col_real = line_inverse[:, 0, block_index, :, column].astype(jnp.float32).reshape(col_shape)
        col_imag = line_inverse[:, 1, block_index, :, column].astype(jnp.float32).reshape(col_shape)
        return (
            coup_real * col_real - coup_imag * col_imag,
            signs_five * (coup_imag * col_real + coup_real * col_imag),
        )

    fwd_real = [pick_index(u_real, 0, block_axis)]
    fwd_imag = [pick_index(u_imag, 0, block_axis)]
    block_index = 1
    mult_real, mult_imag = factor(block_index, 0)
    prev_real = pick_index(fwd_real[-1], block_len - 1, cell_axis, True)
    prev_imag = pick_index(fwd_imag[-1], block_len - 1, cell_axis, True)
    fwd_real.append(
        pick_index(u_real, block_index, block_axis) + mult_real * prev_real - mult_imag * prev_imag
    )
    fwd_imag.append(
        pick_index(u_imag, block_index, block_axis) + mult_real * prev_imag + mult_imag * prev_real
    )
    out_real = list(fwd_real)
    out_imag = list(fwd_imag)
    block_index = 0
    mult_real, mult_imag = factor(block_index, block_len - 1)
    next_real = pick_index(out_real[block_index + 1], 0, cell_axis, True)
    next_imag = pick_index(out_imag[block_index + 1], 0, cell_axis, True)
    out_real[block_index] = fwd_real[block_index] + mult_real * next_real - mult_imag * next_imag
    out_imag[block_index] = fwd_imag[block_index] + mult_real * next_imag + mult_imag * next_real
    real_line = jnp.stack(out_real, axis=block_axis).reshape(in_shape[:4] + (in_shape[5],))
    imag_line = jnp.stack(out_imag, axis=block_axis).reshape(in_shape[:4] + (in_shape[5],))
    return jnp.stack([real_line, imag_line], axis=4).astype(jnp.bfloat16)


def phase_shift(wavefield, slow_field, frequency):
    angles = frequency[:, None, None] * slow_field[None]
    cosine = jnp.cos(angles)[None, None]
    sine_part = jnp.sin(angles)[None, None]
    signs_five = jnp.array([1.0, -1.0], jnp.float32).reshape(1, 2, 1, 1, 1)
    real_part = wavefield[:, :, :, :, 0].astype(jnp.float32)
    imag_part = wavefield[:, :, :, :, 1].astype(jnp.float32)
    new_real = real_part * cosine - signs_five * imag_part * sine_part
    new_imag = imag_part * cosine + signs_five * real_part * sine_part
    return jnp.stack([new_real, new_imag], axis=4).astype(jnp.bfloat16)


def image_term(wavefield, row_cells, col_cells, shot_positions, frequency):
    source = wavefield[:, 0].astype(jnp.float32)
    receiver = wavefield[:, 1].astype(jnp.float32)
    cross = source[:, :, :, 0] * receiver[:, :, :, 1] - source[:, :, :, 1] * receiver[:, :, :, 0]
    weighted = jnp.sum(cross * frequency[None, :, None, None], axis=1)
    row_gap = row_cells[None, :, None] - shot_positions[:, 0][:, None, None]
    col_gap = col_cells[None, None, :] - shot_positions[:, 1][:, None, None]
    spread = (row_gap * row_gap + col_gap * col_gap).astype(jnp.float32)
    taper = 1.0 / (1.0 + spread * (16.0 / (NX * NX)))
    return jnp.sum(weighted * taper, axis=0)


def general_shards(
    source_field,
    residual_data,
    receiver_lines,
    shot_positions,
    slowness,
    frequency,
    line_inverse,
    coupling,
):
    row_count = source_field.shape[2]
    line_len = source_field.shape[4]
    receiver = residual_data * receiver_lines.astype(jnp.bfloat16)[:, None, None, None, :]
    wavefield = jnp.stack([source_field, receiver], axis=1)
    slab_start = lax.axis_index("slab") * row_count
    own_cells = slab_start + jnp.arange(row_count, dtype=jnp.int32)
    all_cells = jnp.arange(line_len, dtype=jnp.int32)
    solve_first = partial(line_solve, line_inverse=line_inverse, coupling=coupling, line_dim=3)
    solve_second = partial(line_solve, line_inverse=line_inverse, coupling=coupling, line_dim=5)

    def forward(fields):
        return solve_first(lax.all_to_all(fields, "slab", split_axis=5, concat_axis=3, tiled=True))

    def backward(fields):
        return lax.all_to_all(fields, "slab", split_axis=3, concat_axis=5, tiled=True)

    images = []
    for depth_index in range(STEPS):
        shifted = phase_shift(wavefield, slowness[depth_index], frequency)
        if depth_index % 2 == 0:
            wavefield = backward(forward(solve_second(shifted)))
        else:
            wavefield = solve_second(backward(forward(shifted)))
        local_image = image_term(wavefield, own_cells, all_cells, shot_positions, frequency)
        images.append(lax.psum_scatter(local_image, "shot", scatter_dimension=1, tiled=True))
    return jnp.stack(images)


F32 = jnp.float32
BF16 = jnp.bfloat16
SMEM = pltpu.SMEM
VMEM = pltpu.VMEM
OWN_MIB = 48
MIDDLE = 1.25


def params(mib):
    return pltpu.CompilerParams(vmem_limit_bytes=mib << 20)


def sincos(angle):
    turns = jnp.floor(angle * 0.15915494309189535 + 0.5)
    rest = (angle - turns * 6.28125) - turns * 1.9353071795864769e-3
    rest = rest * 0.25
    square = rest * rest
    sine = rest + rest * square * (
        -1.6666667e-1 + square * (8.3333333e-3 + square * (-1.9841270e-4 + square * 2.7557319e-6))
    )
    cosine = 1.0 + square * (
        -0.5 + square * (4.1666667e-2 + square * (-1.3888889e-3 + square * 2.4801587e-5))
    )
    sine, cosine = 2.0 * sine * cosine, 1.0 - 2.0 * sine * sine
    return 2.0 * sine * cosine, 1.0 - 2.0 * sine * sine


def dot_t(left, right):
    return lax.dot_general(left, right, (((1,), (1,)), ((), ())), preferred_element_type=F32)


def dot(left, right):
    return lax.dot_general(left, right, (((1,), (0,)), ((), ())), preferred_element_type=F32)


def dot_rows(left, right):
    return lax.dot_general(left, right, (((0,), (0,)), ((), ())), preferred_element_type=F32)


def rotate(omega, slow, real, imag, out):
    rows = slow.shape[0]
    sine, cosine = sincos(omega * slow)
    out[:rows] = (real * cosine - imag * sine).astype(BF16)
    out[rows:] = (imag * cosine + real * sine).astype(BF16)


def other_kernel(meta, freq, field, slowness, out, raw, slow, freq_out):
    f = meta[0] ^ 1
    raw[...] = field[0, meta[0]]
    slow[...] = slowness[0]
    for k in range(2):
        freq_out[k] = freq[k]
    rotate(freq[f], slowness[0], field[0, f, :, 0, :].astype(F32), field[0, f, :, 1, :].astype(F32), out)


def own_kernel(meta, freq, raw, slow, inverse, out, blocks, sem):
    fetch = pltpu.make_async_copy(inverse.at[meta[0]], blocks, sem)
    fetch.start()
    rotate(freq[meta[0]], slow[...], raw[:, 0, :].astype(F32), raw[:, 1, :].astype(F32), out)
    fetch.wait()


def source_kernel(meta, freq, coupling, own, core, blocks, same, cross, ends, scalars):
    for k in range(2):
        scalars[k] = freq[k]
        scalars[2 + 2 * k] = coupling[k, 0]
        scalars[3 + 2 * k] = coupling[k, 1]
    slab_kernel(meta, scalars, own, core, blocks, same, cross, ends)


def away_kernel(meta, residual, out):
    out[...] = residual[0, 1 - meta[0]]


def edge_rows(meta, blocks, block, lanes):
    start = pl.multiple_of((1 - block) * (blocks.shape[2] - 16), 16)
    return jnp.concatenate([blocks[part, block, pl.ds(start, 16), lanes] for part in range(2)], axis=0)


def pick_edge(block, values):
    first = block == 0
    return jnp.where(first, values[15:16], values[0:1]), jnp.where(first, values[31:32], values[16:17])


def edge_product(block, real, imag):
    rr, ir = pick_edge(block, real)
    ri, ii = pick_edge(block, imag)
    return rr - ii, ri + ir


def slab_kernel(meta, scalars, own, core, blocks, same, cross, ends):
    rows = own.shape[0] // 2
    half = blocks.shape[2]
    f, zz = meta[0], meta[1]
    cr, ci = scalars[2 + 2 * f], scalars[3 + 2 * f]
    spot = lax.broadcasted_iota(jnp.int32, (16, half), 1)
    line = lax.broadcasted_iota(jnp.int32, (16, half), 0)
    solved, columns = [], []
    for k in range(2):
        cells = slice(k * half, (k + 1) * half)
        hot = jnp.where((spot == (half - 1 if k == 0 else 0)) & (line == 0), 1.0, 0.0).astype(BF16)
        left = jnp.concatenate(
            [own[:rows, cells], core[:rows, cells], own[rows:, cells], core[rows:, cells], hot], axis=0
        )
        by_real = dot_t(left, blocks[0, k])
        by_imag = dot_t(left, blocks[1, k])
        n = 2 * rows
        solved.append((by_real[:n] - by_imag[n : 2 * n], by_real[n : 2 * n] + by_imag[:n]))
        ar, ai = by_real[2 * n : 2 * n + 1], by_imag[2 * n : 2 * n + 1]
        columns.append((cr * ar - ci * ai, cr * ai + ci * ar))
        ends[2 * k : 2 * k + 1] = columns[k][0]
        ends[2 * k + 1 : 2 * k + 2] = columns[k][1]

    def couple(k, er, ei):
        qr, qi = columns[k]
        return solved[k][0] + er * qr - ei * qi, solved[k][1] + er * qi + ei * qr

    upper = couple(1, solved[0][0][:, half - 1 :], solved[0][1][:, half - 1 :])
    lower = couple(0, upper[0][:, 0:1], upper[1][:, 0:1])
    first = zz == 0
    for part in range(2):
        low, high = lower[part].astype(BF16), upper[part].astype(BF16)
        mine, away = jnp.where(first, low, high), jnp.where(first, high, low)
        for n in range(2):
            at = slice((2 * n + part) * rows, (2 * n + part + 1) * rows)
            same[at] = mine[n * rows : (n + 1) * rows]
            cross[at] = away[n * rows : (n + 1) * rows]


def edge_kernel(meta, blocks, same0, cross0, same1, cross1, edge_same, edge_cross):
    rows = same0.shape[0] // 4
    xb, local = meta[2], meta[3]
    for refs, out in (((same0, same1), edge_same), ((cross0, cross1), edge_cross)):
        for part in range(2):
            total = 0.0
            for n in range(2):
                lanes = pl.ds(pl.multiple_of((local ^ n) * rows, rows), rows)
                row = edge_rows(meta, blocks, xb, lanes)
                at = slice((2 * n + part) * rows, (2 * n + part + 1) * rows)
                total = total + dot(row, jnp.concatenate([ref[at] for ref in refs], axis=1))
            if part == 0:
                real = total
        er, ei = edge_product(xb, real, total)
        half = same0.shape[1]
        for k in range(2):
            out[2 * k : 2 * k + 1] = er[:, k * half : (k + 1) * half]
            out[2 * k + 1 : 2 * k + 2] = ei[:, k * half : (k + 1) * half]


def receiver_kernel(
    meta, scalars, mask, field, core_raw, slow, core_slow, blocks, same0, cross0, same, cross, edge_same, edge_cross, own, core, ends
):
    keep = mask[...].astype(F32)
    f = meta[0]
    for raw, slowness, out in ((field.at[0, f], slow, own), (core_raw, core_slow, core)):
        rotate(
            scalars[f], slowness[...], raw[:, 0, :].astype(F32) * keep, -(raw[:, 1, :].astype(F32) * keep), out
        )
    slab_kernel(meta, scalars, own, core, blocks, same, cross, ends)
    edge_kernel(meta, blocks, same0, cross0, same, cross, edge_same, edge_cross)


def phase_kernel(meta, scalars, place, own, core, far, far_core, sine, cosine, weight):
    rows, half = own.shape
    omega = scalars[meta[0]]
    for k, piece in enumerate((own, core, far, far_core)):
        start = pl.multiple_of((meta[3] ^ k) * rows, rows)
        s, c = sincos(omega * (piece[...].astype(F32) + MIDDLE))
        sine[pl.ds(start, rows)] = s
        cosine[pl.ds(start, rows)] = c
    row = lax.broadcasted_iota(jnp.int32, (weight.shape[0], half), 0) + meta[2] * half - place[0, 0]
    col = lax.broadcasted_iota(jnp.int32, (weight.shape[0], half), 1) + meta[1] * half - place[0, 1]
    spread = (row * row + col * col).astype(F32)
    weight[...] = -omega / (1.0 + spread * (16.0 / (NX * NX)))


def turn_value(meta, scalars, blocks, block):
    cr, ci = scalars[2 + 2 * meta[0]], scalars[3 + 2 * meta[0]]
    ar = blocks[0, 1, 0:16, 0:128].astype(F32)[0:1, 0:1]
    ai = blocks[1, 1, 0:16, 0:128].astype(F32)[0:1, 0:1]
    first = block == 0
    return jnp.where(first, cr * ar - ci * ai, 0.0), jnp.where(first, cr * ai + ci * ar, 0.0)


def column_kernel(
    meta, scalars, near, far, blocks, edge_same, edge_cross, sine, cosine, solved, shifted, own_edge, lines
):
    rows = near.shape[0] // 4
    half = near.shape[1]
    xb = meta[2]
    real, imag = lines.at[pl.ds(0, half)], lines.at[pl.ds(half, half)]
    for k, (piece, n) in enumerate(((near, 0), (near, 1), (far, 0), (far, 1))):
        start = pl.multiple_of((meta[3] ^ k) * rows, rows)
        real[pl.ds(start, rows)] = piece[2 * n * rows : (2 * n + 1) * rows]
        imag[pl.ds(start, rows)] = piece[(2 * n + 1) * rows : (2 * n + 2) * rows]
    cr, ci = scalars[2 + 2 * meta[0]], scalars[3 + 2 * meta[0]]
    ar, ai = turn_value(meta, scalars, blocks, xb)
    row = edge_rows(meta, blocks, xb, slice(0, half))
    own_real, own_imag = edge_product(xb, dot(row, real[...]), dot(row, imag[...]))
    hr = edge_same[0:1] + edge_cross[0:1] + ar * own_real - ai * own_imag
    hi = edge_same[1:2] + edge_cross[1:2] + ar * own_imag + ai * own_real
    add_real = cr * hr - ci * hi
    add_imag = cr * hi + ci * hr
    upper = xb == 1
    low = lax.broadcasted_iota(jnp.int32, (16, half), 0) == 0
    high = lax.broadcasted_iota(jnp.int32, (16, half), 0) == 15
    for ref, add in ((real, add_real), (imag, add_imag)):
        ref[0:16] = (ref[0:16].astype(F32) + jnp.where(low & upper, add, 0.0)).astype(BF16)
        ref[half - 16 :] = (
            ref[half - 16 :].astype(F32) + jnp.where(high & jnp.logical_not(upper), add, 0.0)
        ).astype(BF16)
    left = complex_block(blocks, xb)
    for n in range(0, half, 256):
        cols = slice(n, n + 256)
        x = dot(left, lines[:, cols]).astype(BF16)
        xr, xi = x[:half], x[half:]
        solved[:half, cols] = xr
        solved[half:, cols] = xi
        xr, xi = xr.astype(F32), xi.astype(F32)
        s, c = sine[:, cols], cosine[:, cols]
        shifted[:half, cols] = (xr * c - xi * s).astype(BF16)
        shifted[half:, cols] = (xi * c + xr * s).astype(BF16)
    own_real, own_imag = edge_product(xb, dot(row, shifted[:half]), dot(row, shifted[half:]))
    own_edge[0:1] = own_real
    own_edge[1:2] = own_imag


def complex_block(blocks, block):
    real, imag = blocks[0, block], blocks[1, block]
    return jnp.concatenate(
        [jnp.concatenate([real, -imag], axis=1), jnp.concatenate([imag, real], axis=1)], axis=0
    )


def both_kernel(meta, shifted, blocks, solved, edge):
    half = shifted.shape[1]
    xb, zz = meta[2], meta[1]
    u = dot(complex_block(blocks, xb), shifted[...]).astype(BF16)
    row = dot_t(edge_rows(meta, blocks, zz, slice(0, half)), u)
    edge_real, edge_imag = edge_product(zz, row[:, :half], row[:, half:])
    edge[0:1] = edge_real
    edge[1:2] = edge_imag
    wide = jnp.concatenate([u[:half], u[half:]], axis=1)
    real, imag = blocks[0, zz], blocks[1, zz]
    solved[:half] = dot_t(wide, jnp.concatenate([real, -imag], axis=1)).astype(BF16)
    solved[half:] = dot_t(wide, jnp.concatenate([imag, real], axis=1)).astype(BF16)


def image_pieces(meta, image, keep, send):
    rows, cols = keep.shape[1:]
    for kz in range(2):
        for kx in range(2):
            col = pl.multiple_of((meta[5] ^ kx) * cols, cols)
            for other, ref in ((0, keep), (1, send)):
                row = pl.multiple_of(((meta[4] ^ kz) * 2 + (meta[0] ^ other)) * rows, rows)
                ref[kz * 2 + kx] = image[pl.ds(row, rows), pl.ds(col, cols)]


def pick_end(ends, block):
    first = block == 0
    return jnp.where(first, ends[0:1], ends[2:3]), jnp.where(first, ends[1:2], ends[3:4])


def turn_kernel(meta, scalars, edge_x, near_x, edge_y0, edge_y1, ends, blocks, whole, edge):
    ar, ai = turn_value(meta, scalars, blocks, meta[2])
    zz = meta[1]
    yr, yi = pick_edge(zz, edge_rows(meta, blocks, zz, slice(0, ends.shape[1])).astype(F32))
    pr, pi = pick_end(ends, meta[2])
    for n in range(2):
        r, i = slice(2 * n, 2 * n + 1), slice(2 * n + 1, 2 * n + 2)
        hr = near_x[r] + ar * edge_x[r] - ai * edge_x[i]
        hi = near_x[i] + ar * edge_x[i] + ai * edge_x[r]
        whole[r] = hr
        whole[i] = hi
        sr = jnp.sum(hr * yr - hi * yi, axis=1, keepdims=True)
        si = jnp.sum(hr * yi + hi * yr, axis=1, keepdims=True)
        edge_y = (edge_y0, edge_y1)[n]
        edge[r] = edge_y[0:1] + sr * pr - si * pi
        edge[i] = edge_y[1:2] + sr * pi + si * pr


def split(value):
    high = value.astype(BF16)
    return high.astype(F32), (value - high.astype(F32))


def between_kernel(meta, whole, blocks, source, receiver, weight, out, keep, send, image):
    high, low = split(whole[...])
    left = jnp.concatenate([high, low, high, low], axis=0).astype(BF16)
    by_real = dot_t(left, blocks[0, meta[1]])
    by_imag = dot_t(left, blocks[1, meta[1]])
    by_real = by_real[0:4] + by_real[4:8]
    by_imag = by_imag[0:4] + by_imag[4:8]
    for n in range(2):
        r, i = slice(2 * n, 2 * n + 1), slice(2 * n + 1, 2 * n + 2)
        out[r] = by_real[r] - by_imag[i]
        out[i] = by_real[i] + by_imag[r]
    half = source.shape[1]
    sr, si = source[:half].astype(F32), source[half:].astype(F32)
    rr, ri = receiver[:half].astype(F32), receiver[half:].astype(F32)
    image[...] = ((sr * ri + si * rr) * weight[...]).astype(BF16)
    image_pieces(meta, image, keep, send)


def second_image_kernel(
    meta, scalars, source, receiver, weight, rows_y, edge, near, ends, blocks, keep, send, image
):
    half = source.shape[1]
    ar, ai = turn_value(meta, scalars, blocks, meta[1])
    pr, pi = pick_end(ends, meta[2])
    qr, qi = pick_end(ends, meta[1])

    def triple(value, order):
        high, low = split(value)
        return [high, high, low] if order == 0 else [high, low, high]

    fields = []
    for n, ref in enumerate((source, receiver)):
        r, i = slice(2 * n, 2 * n + 1), slice(2 * n + 1, 2 * n + 2)
        gr = near[r] + ar * edge[r] - ai * edge[i]
        gi = near[i] + ar * edge[i] + ai * edge[r]
        tr, ti = rows_y[r], rows_y[i]
        left, right_real, right_imag = [], [], []
        for a, b, c in ((pr, tr, ti), (pi, -ti, tr), (gr, qr, qi), (gi, -qi, qr)):
            left += triple(a, 0)
            right_real += triple(b, 1)
            right_imag += triple(c, 1)
        pad = [jnp.zeros((4, half), F32)]
        left = jnp.concatenate(left + pad, axis=0).astype(BF16)
        right_real = jnp.concatenate(right_real + pad, axis=0).astype(BF16)
        right_imag = jnp.concatenate(right_imag + pad, axis=0).astype(BF16)
        fields.append(
            (
                ref[:half].astype(F32) + dot_rows(left, right_real),
                ref[half:].astype(F32) + dot_rows(left, right_imag),
            )
        )
    (sr, si), (rr, ri) = fields
    image[...] = ((sr * ri + si * rr) * weight[...]).astype(BF16)
    image_pieces(meta, image, keep, send)


def block_shards(
    source_field, residual_data, receiver_lines, shot_positions, slowness, frequency, line_inverse, coupling
):
    rows, length = slowness.shape[1:]
    half = line_inverse.shape[-1]
    slab = lax.axis_index("slab")
    shot = lax.axis_index("shot")
    meta = jnp.stack(
        [slab & 1, (slab >> 1) & 1, slab >> 2, slab & 3, shot >> 1, shot & 1]
    ).astype(jnp.int32)
    smem = pl.BlockSpec(memory_space=SMEM)
    vmem = pl.BlockSpec(memory_space=VMEM)
    hbm = pl.BlockSpec(memory_space=pltpu.HBM)

    def shape(dtype, *sizes):
        return jax.ShapeDtypeStruct(sizes, dtype)

    def call(body, name, specs, outs, scratch, mib, *args):
        return pl.pallas_call(
            body,
            in_specs=specs,
            out_specs=[vmem] * len(outs),
            out_shape=outs,
            scratch_shapes=scratch,
            compiler_params=params(mib),
            name=name,
        )(*args)

    def move(array, k):
        return lax.ppermute(array, "slab", [(i, i ^ k) for i in range(8)])

    cut = shape(BF16, 2 * rows, length)
    block_shape = shape(BF16, *line_inverse.shape[1:])
    core, raw, slow, freq = pl.pallas_call(
        other_kernel,
        in_specs=[smem, smem, vmem, vmem],
        out_specs=[vmem] * 3 + [smem],
        out_shape=[cut, shape(BF16, rows, 2, length), shape(F32, rows, length), shape(F32, 2)],
        compiler_params=params(12),
        name="other",
    )(meta, frequency, source_field, slowness)
    own, blocks = pl.pallas_call(
        own_kernel,
        in_specs=[smem, smem, vmem, vmem, hbm],
        out_specs=[vmem, vmem],
        out_shape=[cut, block_shape],
        scratch_shapes=[pltpu.SemaphoreType.DMA],
        compiler_params=params(OWN_MIB),
        name="own",
    )(meta, freq, raw, slow, line_inverse)
    core = move(core, 1)
    block_piece = shape(BF16, 4 * rows, half)
    same0, cross0, ends, scalars = pl.pallas_call(
        source_kernel,
        in_specs=[smem] * 3 + [vmem] * 3,
        out_specs=[vmem] * 3 + [smem],
        out_shape=[block_piece] * 2 + [shape(F32, 4, half), shape(F32, 6)],
        compiler_params=params(16),
        name="slab",
    )(meta, freq, coupling, own, core, blocks)
    far = [move(cross0, 2)]
    residual, same0, slow0 = lax.optimization_barrier((residual_data, same0, slow))
    (away,) = call(
        away_kernel, "away", [smem, vmem], [shape(BF16, rows, 2, length)], [], 12, meta, residual
    )
    core_raw = move(away, 1)
    core_slow0 = move(slow0, 1)
    layer, same0 = lax.optimization_barrier((slowness[1], same0))
    layer = (layer - MIDDLE).astype(jnp.float16)
    low, high = layer[:, :half], layer[:, half:]
    first = meta[1] == 0
    own_slow = jnp.where(first, low, high)
    far_slow = move(jnp.where(first, high, low), 2)
    same1, cross, *edges = call(
        receiver_kernel,
        "receiver",
        [smem, smem] + [vmem] * 8,
        [block_piece] * 2 + [shape(F32, 4, half)] * 2,
        [VMEM((2 * rows, length), BF16)] * 2 + [VMEM((4, half), F32)],
        20,
        meta,
        scalars,
        receiver_lines,
        residual_data,
        core_raw,
        slow,
        core_slow0,
        blocks,
        same0,
        cross0,
    )
    same = [same0, same1]
    edge_same = move(edges[0], 4)
    edge_cross = move(edges[1], 6)
    cross, far[0] = lax.optimization_barrier((cross, far[0]))
    far.append(move(cross, 2))
    pair = shape(BF16, 2 * half, half)
    line = shape(F32, 2, half)
    four = shape(F32, 4, half)
    far_slow, edge_same, edge_cross = lax.optimization_barrier((far_slow, edge_same, edge_cross))
    core_slow = move(jnp.stack([own_slow, far_slow]), 1)
    block = shape(F32, half, half)
    sine, cosine, weight = call(
        phase_kernel,
        "phase",
        [smem] * 3 + [vmem] * 4,
        [block] * 3,
        [],
        8,
        meta,
        scalars,
        shot_positions,
        own_slow.astype(F32),
        core_slow[0].astype(F32),
        far_slow.astype(F32),
        core_slow[1].astype(F32),
    )
    solved, finals, edge_x, edge_y = [], [], [], []
    for n in range(2):
        if n == 1:
            same[1], finals[0] = lax.optimization_barrier((same[1], finals[0]))
        x0, turned, edge = call(
            column_kernel,
            "column",
            [smem, smem] + [vmem] * 7,
            [pair, pair, line],
            [VMEM((2 * half, half), BF16)],
            16,
            meta,
            scalars,
            same[n],
            far[n],
            blocks,
            edge_same[2 * n : 2 * n + 2],
            edge_cross[2 * n : 2 * n + 2],
            sine,
            cosine,
        )
        v, across = call(both_kernel, "both", [smem] + [vmem] * 2, [pair, line], [], 20, meta, turned, blocks)
        solved.append(x0)
        finals.append(v)
        edge_x.append(edge)
        edge_y.append(across)
    edge_x = jnp.concatenate(edge_x)
    near_x = move(edge_x, 4)
    coupled, edge = call(
        turn_kernel,
        "turn",
        [smem, smem] + [vmem] * 6,
        [four, four],
        [],
        4,
        meta,
        scalars,
        edge_x,
        near_x,
        *edge_y,
        ends,
        blocks,
    )
    near_y = move(edge, 2)
    cut = shape(BF16, 4, rows, half // 2)
    scratch = [VMEM((half, half), BF16)]
    rows_y, keep0, send0 = call(
        between_kernel,
        "between",
        [smem] + [vmem] * 5,
        [four, cut, cut],
        scratch,
        12,
        meta,
        coupled,
        blocks,
        solved[0],
        solved[1],
        weight,
    )
    near_y, rows_y, send0 = lax.optimization_barrier((near_y, rows_y, send0))
    keep1, send1 = call(
        second_image_kernel,
        "second_image",
        [smem] * 2 + [vmem] * 8,
        [cut] * 2,
        scratch,
        12,
        meta,
        scalars,
        finals[0],
        finals[1],
        weight,
        rows_y,
        edge,
        near_y,
        ends,
        blocks,
    )
    part0 = keep0.astype(F32) + move(send0, 1).astype(F32)
    part1 = keep1.astype(F32) + move(send1, 1).astype(F32)
    both = jnp.stack([part0, part1], axis=1).astype(BF16)
    total = 0.0
    for kz, kx in ((0, 1), (1, 1), (0, 0), (1, 0)):
        route = []
        for s in range(4):
            for b in range(8):
                sy, sx, bx, bc = s // 2, s % 2, b // 4, b % 2
                by = (b // 2) % 2
                target = (by * 2 + (sx ^ kx)) * 8 + bx * 4 + (sy ^ kz) * 2 + bc
                route.append((s * 8 + b, target))
        total = total + lax.ppermute(both[kz * 2 + kx], ("shot", "slab"), route).astype(F32)
    return total


def solution(mesh):
    placed = (
        P("shot", None, "slab", None, None),
        P("shot", None, "slab", None, None),
        P("shot", None),
        P("shot", None),
        P(None, "slab", None),
        P(),
        P(),
        P(),
    )
    fits = mesh.shape["slab"] == 8 and mesh.shape["shot"] == 4

    def run(*args):
        line_inverse = args[6]
        blocks = fits and line_inverse.shape[0] == 2 and line_inverse.shape[2] == 2
        body = block_shards if blocks else general_shards
        return jax.shard_map(
            body, mesh=mesh, in_specs=placed, out_specs=P(None, "slab", "shot"), check_vma=False
        )(*args)

    return run
```
